32 devices in a mesh: tm: 8 (over y, x, core), rows: 4 (over z).
Axes of the slice: x: 2, y: 2, z: 4, core: 2. Of those that a mesh axis runs over, the one named last changes fastest.
Arguments:
- latents: bfloat16 [16, 16, 64, 512], P('tm', 'rows'), may hold values from -128 to 128
- conv_weight: bfloat16 [27, 512, 512], P(None, 'tm'), may hold values from -0.0546875 to 0.0546875
- query_weight: bfloat16 [512, 512], replicated, may hold values from -1 to 4
- key_weight: bfloat16 [512, 512], replicated, may hold values from -1 to 4
- value_weight: bfloat16 [512, 512], replicated, may hold values from -0.25 to 0.25
- out_weight: bfloat16 [512, 512], replicated, may hold values from -1.5 to 1.5
Outputs:
- output: bfloat16 [16, 16, 64, 512], P('tm', 'rows')
The draws below stay inside these ranges and needn't reach their ends.
All inputs are finite; a program needn't handle non-finite values.
Results may differ from the reference program's by a relative error of at most 0.028.
Values may be sent and summed in bfloat16 or wider, within the bound.
No kernel may reach another device: no remote copies, remote signals or barrier semaphores. Data moves between devices by JAX's collectives and lax.ppermute only.
A program may use at most 128 MiB of HBM per device.

```python
import math
import jax
import jax.numpy as jnp
from jax import lax

C = 512
G = 32
W = 64
FRAMES = 16
H = 16


def draw_latents(key, part):
    first = jax.random.fold_in(key, 21)
    second = jax.random.fold_in(key, 22)
    third = jax.random.fold_in(key, 23)
    position = jnp.arange(H, dtype=jnp.float32) / max(H - 1, 1)
    roughness = jnp.exp(jax.random.uniform(first, (FRAMES, H, 1, 1), jnp.float32) * math.log(2.0))
    channel_scale = jnp.exp(jax.random.uniform(third, (1, 1, 1, C), jnp.float32) * math.log(3.0))
    rising = (3.0 ** position)[None, :, None, None]
    entries = jax.random.truncated_normal(second, -4.0, 4.0, (FRAMES, H, W, C), jnp.float32)
    return ((entries + 0.5) * rising * roughness * channel_scale).astype(jnp.bfloat16)


def drawn_weight(key, constant):
    random_part = jax.random.truncated_normal(jax.random.fold_in(key, constant), -6.0, 6.0, (C, C), jnp.float32) / math.sqrt(C)
    return random_part.astype(jnp.bfloat16)


def draw_query_weight(key, part):
    return drawn_weight(key, 31)


def draw_key_weight(key, part):
    return drawn_weight(key, 32)


def steps_of(stream_key, dims, shards, least, largest):
    def one(dim, blocks):
        heights = jax.random.uniform(jax.random.fold_in(jax.random.fold_in(stream_key, 6), dim), (blocks,), jnp.float32, least / len(shards), largest / len(shards))
        return jnp.repeat(jnp.exp(heights), dims[dim] // blocks).reshape((-1,) + (1,) * (len(dims) - dim - 1))

    loudness = one(*shards[0])
    for cut in shards[1:]:
        loudness = loudness * one(*cut)
    return loudness


def noise(key, shape, scale, most, pieces=(), held_as=jnp.bfloat16):
    array = scale * jax.random.normal(key, shape, jnp.float32)
    if pieces:
        array = array * steps_of(key, shape, pieces, -0.22, 0.18)
    return jnp.clip(array, -most, most).astype(held_as)


def setup_inputs(seed: int = 0) -> dict:
    key_list = jax.random.split(jax.random.key(seed), 7)
    return {
        "latents": draw_latents(jax.random.fold_in(key_list[6], 71), 0),
        "conv_weight": noise(key_list[1], (27, C, C), (27 * C) ** -0.5, 0.0546875, ((1, 8),)),
        "query_weight": draw_query_weight(jax.random.fold_in(key_list[6], 71), 0),
        "key_weight": draw_key_weight(jax.random.fold_in(key_list[6], 71), 0),
        "value_weight": noise(key_list[4], (C, C), C ** -0.5, 0.25),
        "out_weight": noise(key_list[5], (C, C), (C // 36) ** -0.5, 1.5),
    }


epsilon = 1e-06

def frame_block(window, conv_weight, query_weight, key_weight, value_weight, out_weight):
    totals = jnp.zeros((H * W, C), jnp.float32)
    for tap_index in range(27):
        frame_lag = tap_index // 9
        row_lag = tap_index // 3 % 3
        col_lag = tap_index % 3
        patches = window[frame_lag, row_lag:row_lag + H, col_lag:col_lag + W, :].reshape(H * W, C)
        totals = totals + jnp.dot(patches, conv_weight[tap_index], preferred_element_type=jnp.float32)
    convolved = totals.astype(jnp.bfloat16)
    grouped = convolved.astype(jnp.float32).reshape(H * W, G, C // G)
    average = lax.optimization_barrier(jnp.mean(grouped, axis=(0, 2)))
    centered = grouped - average[None, :, None]
    variance = lax.optimization_barrier(jnp.mean(centered * centered, axis=(0, 2)))
    normed = (centered * lax.rsqrt(variance + epsilon)[None, :, None]).reshape(H * W, C).astype(jnp.bfloat16)
    queries = jnp.dot(normed, query_weight, preferred_element_type=jnp.float32).astype(jnp.bfloat16)
    keys = jnp.dot(normed, key_weight, preferred_element_type=jnp.float32).astype(jnp.bfloat16)
    values = jnp.dot(normed, value_weight, preferred_element_type=jnp.float32).astype(jnp.bfloat16)
    scores = jnp.dot(queries, keys.T, preferred_element_type=jnp.float32) * C ** (-0.5)
    row_max = lax.optimization_barrier(jnp.max(scores, axis=1, keepdims=True))
    exp_weights = jnp.exp(scores - row_max).astype(jnp.bfloat16)
    denominator = lax.optimization_barrier(jnp.sum(exp_weights.astype(jnp.float32), axis=1, keepdims=True))
    numerator = jnp.dot(exp_weights, values, preferred_element_type=jnp.float32)
    attended = (numerator / denominator).astype(jnp.bfloat16)
    summed = convolved.astype(jnp.float32) + jnp.dot(attended, out_weight, preferred_element_type=jnp.float32)
    return summed.astype(jnp.bfloat16).reshape(H, W, C)

def reference(latents, conv_weight, query_weight, key_weight, value_weight, out_weight):
    padded = jnp.pad(latents, ((2, 0), (1, 1), (1, 1), (0, 0)))

    def one_frame(frame_index):
        window = lax.dynamic_slice_in_dim(padded, frame_index, 3, 0)
        return frame_block(window, conv_weight, query_weight, key_weight, value_weight, out_weight)
    return lax.map(one_frame, jnp.arange(FRAMES, dtype=jnp.int32))
```

```python
import jax
import jax.numpy as jnp
from jax import lax
from jax.sharding import PartitionSpec as P

G = 32
LANES = 128
CORES = 2

epsilon = 1e-06

BOTH = ("tm", "rows")


def everywhere(sizes, target):
    devices, depth = sizes
    pairs = []
    for t in range(devices):
        for z in range(depth):
            to = target(t, z)
            if to is not None:
                pairs.append((t * depth + z, to[0] * depth + to[1]))
    return pairs


def body(latents, conv_weight, query_weight, key_weight, value_weight, out_weight):
    frames, rows_here, columns, chans = latents.shape
    taps, chans_here, _ = conv_weight.shape
    devices, depth = lax.axis_size("tm"), lax.axis_size("rows")
    sizes = (devices, depth)
    group = LANES // chans_here
    parts = devices // group
    width = group * chans_here
    t_index, z_index = lax.axis_index("tm"), lax.axis_index("rows")
    part, member = t_index // group, t_index % group

    def permute(block, target):
        return lax.ppermute(block, BOTH, everywhere(sizes, target))

    kernel_parts = [conv_weight]
    for step in range(1, group):
        kernel_parts.append(
            permute(
                conv_weight, lambda t, z: (t // group * group + (t + step) % group, z)
            )
        )
    order = (member - jnp.arange(group)) % group
    kernel = jnp.take(jnp.stack(kernel_parts), order, axis=0)
    kernel = jnp.moveaxis(kernel, 0, 1).reshape(taps, width, chans)

    above = permute(latents[:, -1:], lambda t, z: (t, z + 1) if z + 1 < depth else None)
    below = permute(latents[:, :1], lambda t, z: (t, z - 1) if z else None)
    framed = jnp.concatenate([above, latents, below], axis=1)

    held = []
    for s in range(parts):
        piece = lax.dynamic_slice_in_dim(framed, (part ^ s) * width, width, axis=3)
        if s:
            piece = permute(piece, lambda t, z: ((t // group ^ s) * group + t % group, z))
        held.append(piece)
    held = jnp.stack(held)

    earlier = permute(held, lambda t, z: (t // group * group + (t + 1) % group, z))
    place = jnp.arange(parts)
    wrapped = jnp.take(earlier, part ^ jnp.maximum((part ^ place) - 1, 0), axis=0)
    wrapped = jnp.where(((part ^ place) == 0)[:, None, None, None, None], 0, wrapped)
    earlier = jnp.where(member == 0, wrapped, earlier)

    window = jnp.concatenate([earlier, held], axis=1)
    side = round(taps ** (1 / 3))
    partial = lax.conv_general_dilated(
        window,
        kernel.reshape(side, side, side, width, chans),
        (1, 1, 1),
        ((0, 0), (0, 0), (1, 1)),
        dimension_numbers=("NDHWC", "DHWIO", "NDHWC"),
        preferred_element_type=jnp.float32,
    ).astype(jnp.bfloat16)
    total = partial[0].astype(jnp.float32)
    for s in range(1, parts):
        total = total + permute(
            partial[s], lambda t, z: ((t // group ^ s) * group + t % group, z)
        ).astype(jnp.float32)
    convolved = total.astype(jnp.bfloat16)

    share = depth // frames
    per_block = rows_here * columns

    def frame_home(t, z, p):
        frame = t % CORES * frames + (z + p) % frames
        m = z // frames
        slot = frame * share + m
        return (t // CORES * CORES + slot % CORES, slot // CORES)

    blocks = []
    for p in range(frames):
        mine = lax.dynamic_index_in_dim(convolved, (z_index + p) % frames, 0, keepdims=False)
        blocks.append(permute(mine, lambda t, z: frame_home(t, z, p)))
    own = jnp.stack(blocks).reshape(frames * per_block, chans)

    def next_in_frame(t, z, step):
        slot = z * CORES + t % CORES
        slot = slot // share * share + (slot + step) % share
        return (t // CORES * CORES + slot % CORES, slot // CORES)

    whole = [own]
    for step in range(1, share):
        whole.append(permute(own, lambda t, z: next_in_frame(t, z, step)))
    whole = jnp.concatenate(whole)
    tokens = whole.shape[0]

    per_group = chans // G
    spread = (jnp.arange(chans)[:, None] // per_group == jnp.arange(G)[None, :]).astype(jnp.float32)
    wide = whole.astype(jnp.float32)
    entries = tokens * per_group
    average = jnp.dot(jnp.sum(wide, axis=0), spread, precision="highest") / entries
    average = jnp.dot(average, spread.T, precision="highest")
    centered = wide - average
    variance = jnp.dot(jnp.sum(centered * centered, axis=0), spread, precision="highest") / entries
    scale = jnp.dot(lax.rsqrt(variance + epsilon), spread.T, precision="highest")
    normed = (centered * scale).astype(jnp.bfloat16)

    def project(x, w):
        return jnp.dot(x, w, preferred_element_type=jnp.float32).astype(jnp.bfloat16)

    queries = project(normed[: frames * per_block], query_weight)
    keys = project(normed, key_weight)
    values = project(normed, value_weight)
    scores = jnp.dot(queries, keys.T, preferred_element_type=jnp.float32) * chans ** (-0.5)
    row_max = jnp.max(scores, axis=1, keepdims=True)
    exp_weights = jnp.exp(scores - row_max).astype(jnp.bfloat16)
    denominator = jnp.sum(exp_weights.astype(jnp.float32), axis=1, keepdims=True)
    numerator = jnp.dot(exp_weights, values, preferred_element_type=jnp.float32)
    attended = (numerator / denominator).astype(jnp.bfloat16)
    summed = own.astype(jnp.float32) + jnp.dot(
        attended, out_weight, preferred_element_type=jnp.float32
    )
    summed = summed.astype(jnp.bfloat16).reshape(frames, rows_here, columns, chans)

    back = []
    for p in range(frames):
        pairs = [(b, a) for a, b in everywhere(sizes, lambda t, z: frame_home(t, z, p))]
        back.append(lax.ppermute(summed[p], BOTH, pairs))
    return jnp.take(jnp.stack(back), (jnp.arange(frames) - z_index) % frames, axis=0)


def solution(mesh):
    placed = (P("tm", "rows", None, None), P(None, "tm", None), P(), P(), P(), P())
    return jax.shard_map(
        body, mesh=mesh, in_specs=placed, out_specs=P("tm", "rows", None, None), check_vma=False
    )
```

```python
import functools

import jax
import jax.numpy as jnp
from jax import lax
from jax.experimental import pallas as pl
from jax.experimental.pallas import tpu as pltpu
from jax.sharding import PartitionSpec as P

G = 32
LANES = 128
CORES = 2

epsilon = 1e-06

BOTH = ("tm", "rows")
VMEM_LIMIT = 48 * 1024 * 1024


def everywhere(sizes, target):
    devices, depth = sizes
    pairs = []
    for t in range(devices):
        for z in range(depth):
            to = target(t, z)
            if to is not None:
                pairs.append((t * depth + z, to[0] * depth + to[1]))
    return pairs


def in_vmem(count):
    return [pl.BlockSpec(memory_space=pltpu.VMEM)] * count


def conv_kernel(dests, parts, group, rim, out_type, frames, *refs):
    meta = refs[0]
    weight_refs = refs[1 : 1 + group]
    refs = refs[1 + group :]
    held, refs = refs[: len(dests)], refs[len(dests) :]
    before, refs = refs[:parts], refs[parts:]
    if rim:
        (above, below), refs = refs[:2], refs[2:]
    outs, (weights, raw, sems) = refs[: len(dests)], refs[len(dests) :]
    part, member, z = meta[0], meta[1], meta[2]
    lags = weights.shape[0]
    width, chans = weights.shape[2:]
    chans_here = width // group
    _, rows_here, columns, _ = held[0].shape

    copies = []
    for lag in range(lags):
        for step in range(group):
            owner = lax.rem(member - step + group, group)
            copies.append(
                pltpu.make_async_copy(
                    weight_refs[step].at[:, lag],
                    weights.at[lag, :, pl.ds(pl.multiple_of(owner * chans_here, 16), chans_here)],
                    sems.at[lag, step],
                )
            )
    for copy in copies:
        copy.start()

    skip = 1 if rim else 0
    for n, s in enumerate(dests):
        to = lax.bitwise_xor(part, s)
        wraps = member == 0
        place = jnp.where(wraps, lax.bitwise_xor(part, jnp.maximum(to - 1, 0)), s)
        valid = jnp.logical_or(jnp.logical_not(wraps), to > 0)
        raw[n, frames:, skip : skip + rows_here] = held[n][...]
        if rim:
            raw[n, frames:, 0] = above[s]
            raw[n, frames:, skip + rows_here] = below[s]
            raw[n, :frames, 0] = above[parts + place]
            raw[n, :frames, skip + rows_here] = below[parts + place]
        for i in range(parts):

            @pl.when(place == i)
            def _():
                raw[n, :frames, skip : skip + rows_here] = before[i][...]

        @pl.when(jnp.logical_not(valid))
        def _():
            raw[n, :frames] = jnp.zeros_like(raw[n, :frames])

    side = 3
    count = outs[0].shape[0]
    column = lax.broadcasted_iota(jnp.int32, (count, chans), 0) % columns

    def patches(n):
        whole = []
        for a in range(side):
            for b in range(side):
                pieces = []
                for p in range(frames):
                    f = lax.rem(z + p, frames) + a
                    if rim:
                        pieces.append(raw[n, f, b])
                        pieces.append(raw[n, f, rows_here - 1 + b])
                    else:
                        inner = raw[n, f, b : b + rows_here - 2]
                        pieces.append(inner.reshape(-1, width))
                whole.append(jnp.concatenate(pieces, axis=0))
        return jnp.concatenate(whole, axis=1)

    for n in range(len(dests)):
        lhs = patches(n)
        total = None
        for lag in (1, 0, 2):
            if n == 0:
                for step in range(group):
                    copies[lag * group + step].wait()
            product = jnp.dot(
                lhs,
                weights[lag].reshape(-1, chans),
                preferred_element_type=jnp.float32,
            )
            if lag == 1:
                total = product
            elif lag == 0:
                moved = pltpu.roll(product, 1, 0)
                total = total + jnp.where(column == 0, 0.0, moved)
            else:
                moved = pltpu.roll(product, count - 1, 0)
                total = total + jnp.where(column == columns - 1, 0.0, moved)
        outs[n][...] = total.astype(out_type)


def conv_call(dests, meta, weights, held, before, halos, frames, out_type):
    group, parts = len(weights), len(held)
    _, rows_here, columns, width = held[0].shape
    taps, _, _, chans = weights[0].shape
    lags = weights[0].shape[1]
    rim = halos is not None
    rows = 2 if rim else rows_here - 2
    count = frames * rows * columns
    out = jax.ShapeDtypeStruct((count, chans), out_type)
    operands = [meta, *weights, *[held[s] for s in dests], *before, *(halos or ())]
    specs = [pl.BlockSpec(memory_space=pltpu.SMEM)]
    specs += [pl.BlockSpec(memory_space=pl.ANY)] * group
    specs += in_vmem(len(operands) - 1 - group)
    return pl.pallas_call(
        functools.partial(conv_kernel, dests, parts, group, rim, out_type, frames),
        out_shape=[out] * len(dests),
        in_specs=specs,
        out_specs=in_vmem(len(dests)),
        scratch_shapes=[
            pltpu.VMEM((lags, taps, width, chans), jnp.bfloat16),
            pltpu.VMEM(
                (len(dests), 2 * frames, rows_here + (2 if rim else 0), columns, width),
                jnp.bfloat16,
            ),
            pltpu.SemaphoreType.DMA((lags, group)),
        ],
        compiler_params=pltpu.CompilerParams(vmem_limit_bytes=VMEM_LIMIT),
        cost_estimate=pl.CostEstimate(
            flops=2 * len(dests) * count * taps * lags * width * chans,
            bytes_accessed=2 * taps * lags * width * chans,
            transcendentals=0,
        ),
        name="conv_rim" if rim else "conv_inner",
    )(*operands)


def sum_call(pieces, frames):
    count, chans = pieces[0].shape
    out = jax.ShapeDtypeStruct((count // frames, chans), jnp.bfloat16)

    def kernel(*refs):
        ins, outs = refs[: len(pieces)], refs[len(pieces) :]
        for p, out_ref in enumerate(outs):
            size = out_ref.shape[0]
            total = ins[0][pl.ds(p * size, size)].astype(jnp.float32)
            for ref in ins[1:]:
                total = total + ref[pl.ds(p * size, size)].astype(jnp.float32)
            out_ref[...] = total.astype(out_ref.dtype)

    return pl.pallas_call(
        kernel,
        out_shape=[out] * frames,
        in_specs=in_vmem(len(pieces)),
        out_specs=in_vmem(frames),
        compiler_params=pltpu.CompilerParams(vmem_limit_bytes=VMEM_LIMIT),
        name="sum_parts",
    )(*pieces)


def attend_kernel(frames, share, chunks, *refs):
    own_count = frames * chunks
    all_count = own_count * share
    tokens, refs = refs[:all_count], refs[all_count:]
    (wq, wk, wv, wo), refs = refs[:4], refs[4:]
    outs, (normed, keys, values) = refs[:frames], refs[frames:]
    size, chans = normed.shape
    per_group = chans // G

    tile_row = lax.broadcasted_iota(jnp.int32, (LANES, LANES), 0) // per_group
    tile_col = lax.broadcasted_iota(jnp.int32, (LANES, LANES), 1) // per_group
    same = (tile_row == tile_col).astype(jnp.float32).astype(jnp.bfloat16)

    def group_mean(sums):
        first = sums.astype(jnp.bfloat16)
        rest = sums - first.astype(jnp.float32)
        second = rest.astype(jnp.bfloat16)
        third = rest - second.astype(jnp.float32)
        tiles = []
        for tile in range(chans // LANES):
            lanes = slice(tile * LANES, (tile + 1) * LANES)
            stacked = jnp.concatenate(
                [
                    first.astype(jnp.float32)[:, lanes],
                    second.astype(jnp.float32)[:, lanes],
                    third[:, lanes],
                ],
                axis=0,
            ).astype(jnp.bfloat16)
            spread = jnp.dot(stacked, same, preferred_element_type=jnp.float32)
            tiles.append(jnp.sum(spread, axis=0, keepdims=True))
        return jnp.concatenate(tiles, axis=1) / (size * per_group)

    def folded(x):
        return jnp.sum(x.reshape(-1, 8, chans), axis=0)

    average = group_mean(sum(folded(ref[...].astype(jnp.float32)) for ref in tokens))

    def spread_of(ref):
        centered = ref[...].astype(jnp.float32) - average
        return folded(centered * centered)

    scale = lax.rsqrt(group_mean(sum(spread_of(ref) for ref in tokens)) + epsilon)
    place = 0
    for ref in tokens:
        rows = ref.shape[0]
        normed[pl.ds(place, rows)] = (
            (ref[...].astype(jnp.float32) - average) * scale
        ).astype(jnp.bfloat16)
        place += rows

    step = min(256, size)
    for start in range(0, size, step):
        x = normed[pl.ds(start, step)]
        keys[pl.ds(start, step)] = jnp.dot(
            x, wk[...], preferred_element_type=jnp.float32
        ).astype(jnp.bfloat16)
        values[pl.ds(start, step)] = jnp.dot(
            x, wv[...], preferred_element_type=jnp.float32
        ).astype(jnp.bfloat16)

    place = 0
    for index in range(own_count):
        ref = tokens[index]
        rows = ref.shape[0]
        queries = jnp.dot(
            normed[pl.ds(place, rows)], wq[...], preferred_element_type=jnp.float32
        ).astype(jnp.bfloat16)
        place += rows
        scores = lax.dot_general(
            queries, keys[...], (((1,), (1,)), ((), ())), preferred_element_type=jnp.float32
        ) * chans ** (-0.5)
        row_max = jnp.max(scores, axis=1, keepdims=True)
        exp_weights = jnp.exp(scores - row_max).astype(jnp.bfloat16)
        denominator = jnp.sum(exp_weights.astype(jnp.float32), axis=1, keepdims=True)
        numerator = jnp.dot(exp_weights, values[...], preferred_element_type=jnp.float32)
        attended = (numerator / denominator).astype(jnp.bfloat16)
        summed = ref[...].astype(jnp.float32) + jnp.dot(
            attended, wo[...], preferred_element_type=jnp.float32
        )
        summed = summed.astype(jnp.bfloat16)
        out = outs[index // chunks]
        rows_here, columns, _ = out.shape
        if index % chunks == 0:
            out[1 : rows_here - 1] = summed.reshape(rows_here - 2, columns, chans)
        else:
            out[0] = summed[:columns]
            out[rows_here - 1] = summed[columns:]


def attend_call(own, others, weights, frames, rows_here, columns):
    chunks = len(own) // frames
    share = 1 + len(others) // len(own)
    chans = own[0].shape[1]
    size = sum(x.shape[0] for x in own) * share
    mine = size // share
    out = jax.ShapeDtypeStruct((rows_here, columns, chans), jnp.bfloat16)
    operands = [*own, *others, *weights]
    return pl.pallas_call(
        functools.partial(attend_kernel, frames, share, chunks),
        out_shape=[out] * frames,
        in_specs=in_vmem(len(operands)),
        out_specs=in_vmem(frames),
        scratch_shapes=[pltpu.VMEM((size, chans), jnp.bfloat16)] * 3,
        compiler_params=pltpu.CompilerParams(vmem_limit_bytes=VMEM_LIMIT),
        cost_estimate=pl.CostEstimate(
            flops=2 * (2 * size * chans * chans + 2 * mine * chans * (chans + size)),
            bytes_accessed=8 * chans * chans + 2 * size * chans,
            transcendentals=mine * size,
        ),
        name="attend",
    )(*operands)


def place_kernel(meta, *refs):
    parts, out, sems = refs[:-2], refs[-2], refs[-1]
    frames = len(parts)
    copies = [
        pltpu.make_async_copy(ref, out.at[lax.rem(meta[2] + p, frames)], sems.at[p])
        for p, ref in enumerate(parts)
    ]
    for copy in copies:
        copy.start()
    for copy in copies:
        copy.wait()


def place_call(meta, parts):
    frames = len(parts)
    anywhere = pl.BlockSpec(memory_space=pl.ANY)
    return pl.pallas_call(
        place_kernel,
        out_shape=jax.ShapeDtypeStruct((frames, *parts[0].shape), parts[0].dtype),
        in_specs=[pl.BlockSpec(memory_space=pltpu.SMEM)] + [anywhere] * frames,
        out_specs=anywhere,
        scratch_shapes=[pltpu.SemaphoreType.DMA((frames,))],
        name="place_frames",
    )(meta, *parts)


def body(latents, conv_weight, query_weight, key_weight, value_weight, out_weight):
    frames, rows_here, columns, chans = latents.shape
    taps, chans_here, _ = conv_weight.shape
    devices, depth = lax.axis_size("tm"), lax.axis_size("rows")
    sizes = (devices, depth)
    group = LANES // chans_here
    parts = devices // group
    width = group * chans_here
    t_index, z_index = lax.axis_index("tm"), lax.axis_index("rows")
    part, member = t_index // group, t_index % group
    meta = jnp.stack([part, member, z_index]).astype(jnp.int32)

    def permute(block, target):
        return lax.ppermute(block, BOTH, everywhere(sizes, target))

    def to_part(s):
        return lambda t, z: ((t // group ^ s) * group + t % group, z)

    def to_member(step):
        return lambda t, z: (t // group * group + (t + step) % group, z)

    held, before = [None] * parts, [None] * parts
    for s in reversed(range(parts)):
        piece = lax.dynamic_slice_in_dim(latents, (part ^ s) * width, width, axis=3)
        held[s] = permute(piece, to_part(s)) if s else piece
    for s in range(parts):
        before[s] = permute(held[s], to_member(1))

    split = conv_weight.reshape(taps // 3, 3, chans_here, chans)
    weights = [split] + [permute(split, to_member(step)) for step in range(1, group)]

    last = jnp.stack([x[:, rows_here - 1] for x in (*held, *before)])
    first = jnp.stack([x[:, 0] for x in (*held, *before)])
    halos = (
        permute(last, lambda t, z: (t, z + 1) if z + 1 < depth else None),
        permute(first, lambda t, z: (t, z - 1) if z else None),
    )

    away = list(reversed(range(1, parts)))
    sums = []
    for halo in (None, halos):
        call = functools.partial(conv_call, meta=meta, weights=weights, held=held, before=before)
        call = functools.partial(call, halos=halo, frames=frames)
        if halo is None:
            sent = call(away[:1], out_type=jnp.bfloat16) + call(away[1:], out_type=jnp.bfloat16)
        else:
            sent = call(away, out_type=jnp.bfloat16)
        got = [permute(x, to_part(s)) for s, x in zip(away, sent)]
        (mine,) = call([0], out_type=jnp.float32)
        sums.append(sum_call([mine, *got], frames))

    share = depth // frames

    def frame_home(t, z, p):
        frame = t % CORES * frames + (z + p) % frames
        slot = frame * share + z // frames
        return (t // CORES * CORES + slot % CORES, slot // CORES)

    def next_in_frame(t, z, step):
        slot = z * CORES + t % CORES
        slot = slot // share * share + (slot + step) % share
        return (t // CORES * CORES + slot % CORES, slot // CORES)

    own = []
    for p in range(frames):
        for chunk in sums:
            own.append(permute(chunk[p], lambda t, z: frame_home(t, z, p)))
    others = []
    for step in range(1, share):
        others += [permute(x, lambda t, z: next_in_frame(t, z, step)) for x in own]

    done = attend_call(
        own,
        others,
        (query_weight, key_weight, value_weight, out_weight),
        frames,
        rows_here,
        columns,
    )
    back = []
    for p in range(frames):
        pairs = [(b, a) for a, b in everywhere(sizes, lambda t, z: frame_home(t, z, p))]
        back.append(lax.ppermute(done[p], BOTH, pairs))
    return place_call(meta, back)


def solution(mesh):
    placed = (P("tm", "rows", None, None), P(None, "tm", None), P(), P(), P(), P())
    return jax.shard_map(
        body, mesh=mesh, in_specs=placed, out_specs=P("tm", "rows", None, None), check_vma=False
    )
```

```python
import functools

import jax
import jax.numpy as jnp
from jax import lax
from jax.experimental import pallas as pl
from jax.experimental.pallas import tpu as pltpu
from jax.sharding import PartitionSpec as P

G = 32
LANES = 128
CORES = 2

epsilon = 1e-06

BOTH = ("tm", "rows")
VMEM_LIMIT = 32 * 1024 * 1024


def everywhere(sizes, target):
    devices, depth = sizes
    pairs = []
    for t in range(devices):
        for z in range(depth):
            to = target(t, z)
            if to is not None:
                pairs.append((t * depth + z, to[0] * depth + to[1]))
    return pairs


def in_vmem(count):
    return [pl.BlockSpec(memory_space=pltpu.VMEM)] * count


def merge_kernel(group, *refs):
    meta, refs = refs[0], refs[1:]
    slices, out, sems = refs[:group], refs[group], refs[group + 1]
    chans_here = slices[0].shape[2]
    copies = []
    for lag in range(out.shape[0]):
        for step in range(group):
            owner = lax.rem(meta[1] - step + group, group)
            rows = pl.ds(pl.multiple_of(owner * chans_here, 16), chans_here)
            copies.append(
                pltpu.make_async_copy(
                    slices[step].at[:, lag], out.at[lag, :, rows], sems.at[lag, step]
                )
            )
    for copy in copies:
        copy.start()
    for copy in copies:
        copy.wait()


def merge_call(meta, slices):
    group = len(slices)
    taps, lags, chans_here, chans = slices[0].shape
    return pl.pallas_call(
        functools.partial(merge_kernel, group),
        out_shape=jax.ShapeDtypeStruct((lags, taps, group * chans_here, chans), jnp.bfloat16),
        in_specs=[pl.BlockSpec(memory_space=pltpu.SMEM)]
        + [pl.BlockSpec(memory_space=pl.ANY)] * group,
        out_specs=pl.BlockSpec(memory_space=pltpu.VMEM),
        scratch_shapes=[pltpu.SemaphoreType.DMA((lags, group))],
        compiler_params=pltpu.CompilerParams(vmem_limit_bytes=VMEM_LIMIT),
        name="merge_kernel_slices",
    )(meta, *slices)


def halo_call(pieces, after):
    frames, rows_here, columns, width = pieces[0].shape
    out = jax.ShapeDtypeStruct((len(pieces), frames, columns, width), jnp.bfloat16)

    def kernel(*refs):
        first, last = refs[-2:]
        for i in range(len(pieces)):
            first[i] = refs[i][:, 0]
            last[i] = refs[i][:, rows_here - 1]

    return pl.pallas_call(
        kernel,
        out_shape=[out] * 2,
        in_specs=in_vmem(len(pieces)) + [pl.BlockSpec(memory_space=pl.ANY)],
        out_specs=in_vmem(2),
        compiler_params=pltpu.CompilerParams(vmem_limit_bytes=VMEM_LIMIT),
        name="halo_rows",
    )(*pieces, after)


def conv_kernel(jobs, parts, frames, *refs):
    meta, weights, refs = refs[0], refs[1], refs[2:]
    dests = sorted({s for s, _ in jobs})
    any_rim = any(rim for _, rim in jobs)
    held, refs = refs[: len(dests)], refs[len(dests) :]
    before, refs = refs[:parts], refs[parts:]
    if any_rim:
        (above, below), refs = refs[:2], refs[2:]
    outs, raw = refs[-1 - len(jobs) : -1], refs[-1]
    part, member, z = meta[0], meta[1], meta[2]
    lags, _, width, chans = weights.shape
    _, rows_here, columns, _ = held[0].shape

    for n, s in enumerate(dests):
        to = lax.bitwise_xor(part, s)
        wraps = member == 0
        place = jnp.where(wraps, lax.bitwise_xor(part, jnp.maximum(to - 1, 0)), s)
        valid = jnp.logical_or(jnp.logical_not(wraps), to > 0)
        raw[n, frames:, 1 : 1 + rows_here] = held[n][...]
        if any_rim:
            raw[n, frames:, 0] = above[s]
            raw[n, frames:, 1 + rows_here] = below[s]
            raw[n, :frames, 0] = above[parts + place]
            raw[n, :frames, 1 + rows_here] = below[parts + place]
        for i in range(parts):

            @pl.when(place == i)
            def _():
                raw[n, :frames, 1 : 1 + rows_here] = before[i][...]

        @pl.when(jnp.logical_not(valid))
        def _():
            raw[n, :frames] = jnp.zeros_like(raw[n, :frames])

    side = 3

    def patches(a, b):
        pieces = []
        for s, rim in jobs:
            n = dests.index(s)
            for p in range(frames):
                f = lax.rem(z + p, frames) + a
                if rim:
                    pieces.append(raw[n, f, b])
                    pieces.append(raw[n, f, rows_here - 1 + b])
                else:
                    pieces.append(raw[n, f, 1 + b : b + rows_here - 1].reshape(-1, width))
        return jnp.concatenate(pieces, axis=0)

    lhs = jnp.concatenate([patches(a, b) for a in range(side) for b in range(side)], axis=1)
    count = lhs.shape[0]
    column = lax.broadcasted_iota(jnp.int32, (count, chans), 0) % columns
    total = None
    for lag in (1, 0, 2):
        product = jnp.dot(
            lhs, weights[lag].reshape(-1, chans), preferred_element_type=jnp.float32
        )
        if lag == 1:
            total = product
        elif lag == 0:
            total = total + jnp.where(column == 0, 0.0, pltpu.roll(product, 1, 0))
        else:
            moved = pltpu.roll(product, count - 1, 0)
            total = total + jnp.where(column == columns - 1, 0.0, moved)
    place = 0
    for out in outs:
        out[...] = total[place : place + out.shape[0]].astype(out.dtype)
        place += out.shape[0]


def conv_call(jobs, meta, weights, held, before, halos, frames, out_type, after=()):
    parts = len(held)
    dests = sorted({s for s, _ in jobs})
    _, rows_here, columns, width = held[0].shape
    lags, taps, _, chans = weights.shape
    any_rim = any(rim for _, rim in jobs)
    counts = [frames * (2 if rim else rows_here - 2) * columns for _, rim in jobs]
    operands = [weights, *[held[s] for s in dests], *before, *(halos if any_rim else ())]
    specs = [pl.BlockSpec(memory_space=pltpu.SMEM)] + in_vmem(len(operands))
    specs += [pl.BlockSpec(memory_space=pl.ANY)] * len(after)
    return pl.pallas_call(
        functools.partial(conv_kernel, tuple(jobs), parts, frames),
        out_shape=[jax.ShapeDtypeStruct((count, chans), out_type) for count in counts],
        in_specs=specs,
        out_specs=in_vmem(len(jobs)),
        scratch_shapes=[
            pltpu.VMEM((len(dests), 2 * frames, rows_here + 2, columns, width), jnp.bfloat16)
        ],
        compiler_params=pltpu.CompilerParams(vmem_limit_bytes=VMEM_LIMIT),
        cost_estimate=pl.CostEstimate(
            flops=2 * sum(counts) * taps * lags * width * chans,
            bytes_accessed=2 * taps * lags * width * chans,
            transcendentals=0,
        ),
        name="conv_rim" if any_rim else "conv_inner",
    )(meta, *operands, *after)


def sum_call(pieces, frames):
    count, chans = pieces[0].shape
    out = jax.ShapeDtypeStruct((count // frames, chans), jnp.bfloat16)

    def kernel(*refs):
        ins, outs = refs[: len(pieces)], refs[len(pieces) :]
        for p, out_ref in enumerate(outs):
            size = out_ref.shape[0]
            total = ins[0][pl.ds(p * size, size)].astype(jnp.float32)
            for ref in ins[1:]:
                total = total + ref[pl.ds(p * size, size)].astype(jnp.float32)
            out_ref[...] = total.astype(out_ref.dtype)

    return pl.pallas_call(
        kernel,
        out_shape=[out] * frames,
        in_specs=in_vmem(len(pieces)),
        out_specs=in_vmem(frames),
        compiler_params=pltpu.CompilerParams(vmem_limit_bytes=VMEM_LIMIT),
        name="sum_parts",
    )(*pieces)


def attend_kernel(frames, share, chunks, *refs):
    own_count = frames * chunks
    all_count = own_count * share
    tokens, refs = refs[:all_count], refs[all_count:]
    (wq, wk, wv, wo), refs = refs[:4], refs[4:]
    outs, (normed, keys, values) = refs[:frames], refs[frames:]
    size, chans = normed.shape
    per_group = chans // G

    tile_row = lax.broadcasted_iota(jnp.int32, (LANES, LANES), 0) // per_group
    tile_col = lax.broadcasted_iota(jnp.int32, (LANES, LANES), 1) // per_group
    same = (tile_row == tile_col).astype(jnp.float32).astype(jnp.bfloat16)

    def group_mean(sums):
        first = sums.astype(jnp.bfloat16)
        rest = sums - first.astype(jnp.float32)
        second = rest.astype(jnp.bfloat16)
        third = rest - second.astype(jnp.float32)
        tiles = []
        for tile in range(chans // LANES):
            lanes = slice(tile * LANES, (tile + 1) * LANES)
            stacked = jnp.concatenate(
                [
                    first.astype(jnp.float32)[:, lanes],
                    second.astype(jnp.float32)[:, lanes],
                    third[:, lanes],
                ],
                axis=0,
            ).astype(jnp.bfloat16)
            spread = jnp.dot(stacked, same, preferred_element_type=jnp.float32)
            tiles.append(jnp.sum(spread, axis=0, keepdims=True))
        return jnp.concatenate(tiles, axis=1) / (size * per_group)

    def folded(x):
        return jnp.sum(x.reshape(-1, 8, chans), axis=0)

    average = group_mean(sum(folded(ref[...].astype(jnp.float32)) for ref in tokens))

    def spread_of(ref):
        centered = ref[...].astype(jnp.float32) - average
        return folded(centered * centered)

    scale = lax.rsqrt(group_mean(sum(spread_of(ref) for ref in tokens)) + epsilon)
    place = 0
    for ref in tokens:
        rows = ref.shape[0]
        normed[pl.ds(place, rows)] = (
            (ref[...].astype(jnp.float32) - average) * scale
        ).astype(jnp.bfloat16)
        place += rows

    step = min(256, size)
    for start in range(0, size, step):
        x = normed[pl.ds(start, step)]
        keys[pl.ds(start, step)] = jnp.dot(
            x, wk[...], preferred_element_type=jnp.float32
        ).astype(jnp.bfloat16)
        values[pl.ds(start, step)] = jnp.dot(
            x, wv[...], preferred_element_type=jnp.float32
        ).astype(jnp.bfloat16)

    place = 0
    for index in range(own_count):
        ref = tokens[index]
        rows = ref.shape[0]
        queries = jnp.dot(
            normed[pl.ds(place, rows)], wq[...], preferred_element_type=jnp.float32
        ).astype(jnp.bfloat16)
        place += rows
        scores = lax.dot_general(
            queries, keys[...], (((1,), (1,)), ((), ())), preferred_element_type=jnp.float32
        ) * chans ** (-0.5)
        row_max = jnp.max(scores, axis=1, keepdims=True)
        exp_weights = jnp.exp(scores - row_max).astype(jnp.bfloat16)
        denominator = jnp.sum(exp_weights.astype(jnp.float32), axis=1, keepdims=True)
        numerator = jnp.dot(exp_weights, values[...], preferred_element_type=jnp.float32)
        attended = (numerator / denominator).astype(jnp.bfloat16)
        summed = ref[...].astype(jnp.float32) + jnp.dot(
            attended, wo[...], preferred_element_type=jnp.float32
        )
        summed = summed.astype(jnp.bfloat16)
        out = outs[index // chunks]
        rows_here, columns, _ = out.shape
        if index % chunks == 0:
            out[1 : rows_here - 1] = summed.reshape(rows_here - 2, columns, chans)
        else:
            out[0] = summed[:columns]
            out[rows_here - 1] = summed[columns:]


def attend_call(own, others, weights, frames, rows_here, columns):
    chunks = len(own) // frames
    share = 1 + len(others) // len(own)
    chans = own[0].shape[1]
    size = sum(x.shape[0] for x in own) * share
    mine = size // share
    out = jax.ShapeDtypeStruct((rows_here, columns, chans), jnp.bfloat16)
    operands = [*own, *others, *weights]
    return pl.pallas_call(
        functools.partial(attend_kernel, frames, share, chunks),
        out_shape=[out] * frames,
        in_specs=in_vmem(len(operands)),
        out_specs=in_vmem(frames),
        scratch_shapes=[pltpu.VMEM((size, chans), jnp.bfloat16)] * 3,
        compiler_params=pltpu.CompilerParams(vmem_limit_bytes=VMEM_LIMIT),
        cost_estimate=pl.CostEstimate(
            flops=2 * (2 * size * chans * chans + 2 * mine * chans * (chans + size)),
            bytes_accessed=8 * chans * chans + 2 * size * chans,
            transcendentals=mine * size,
        ),
        name="attend",
    )(*operands)


def place_kernel(meta, *refs):
    parts, out, sems = refs[:-2], refs[-2], refs[-1]
    frames = len(parts)
    copies = [
        pltpu.make_async_copy(ref, out.at[lax.rem(meta[2] + p, frames)], sems.at[p])
        for p, ref in enumerate(parts)
    ]
    for copy in copies:
        copy.start()
    for copy in copies:
        copy.wait()


def place_call(meta, parts):
    frames = len(parts)
    return pl.pallas_call(
        place_kernel,
        out_shape=jax.ShapeDtypeStruct((frames, *parts[0].shape), parts[0].dtype),
        in_specs=[pl.BlockSpec(memory_space=pltpu.SMEM)] + in_vmem(frames),
        out_specs=pl.BlockSpec(memory_space=pl.ANY),
        scratch_shapes=[pltpu.SemaphoreType.DMA((frames,))],
        name="place_frames",
    )(meta, *parts)


def body(latents, conv_weight, query_weight, key_weight, value_weight, out_weight):
    frames, rows_here, columns, chans = latents.shape
    taps, chans_here, _ = conv_weight.shape
    devices, depth = lax.axis_size("tm"), lax.axis_size("rows")
    sizes = (devices, depth)
    group = LANES // chans_here
    parts = devices // group
    width = group * chans_here
    t_index, z_index = lax.axis_index("tm"), lax.axis_index("rows")
    part, member = t_index // group, t_index % group
    meta = jnp.stack([part, member, z_index]).astype(jnp.int32)

    def permute(block, target):
        return lax.ppermute(block, BOTH, everywhere(sizes, target))

    def to_part(s):
        return lambda t, z: ((t // group ^ s) * group + t % group, z)

    def to_member(step):
        return lambda t, z: (t // group * group + (t + step) % group, z)

    held, before = [None] * parts, [None] * parts
    for s in reversed(range(parts)):
        piece = lax.dynamic_slice_in_dim(latents, (part ^ s) * width, width, axis=3)
        held[s] = permute(piece, to_part(s)) if s else piece
    for s in range(parts):
        before[s] = permute(held[s], to_member(1))

    split = conv_weight.reshape(taps // 3, 3, chans_here, chans)
    slices = [split] + [permute(split, to_member(step)) for step in range(1, group)]
    weights = merge_call(meta, slices)

    away = list(reversed(range(1, parts)))
    conv = functools.partial(
        conv_call, meta=meta, weights=weights, held=held, before=before, frames=frames
    )
    inner = conv([(s, False) for s in away[:1]], halos=None, out_type=jnp.bfloat16)
    first, last = halo_call([*held, *before], inner[0])
    halos = (
        permute(last, lambda t, z: (t, z + 1) if z + 1 < depth else None),
        permute(first, lambda t, z: (t, z - 1) if z else None),
    )
    inner += conv([(s, False) for s in away[1:]], halos=None, out_type=jnp.bfloat16)
    rim = conv([(s, True) for s in away], halos=halos, out_type=jnp.bfloat16, after=inner[-1:])
    mine = conv([(0, False), (0, True)], halos=halos, out_type=jnp.float32, after=rim[-1:])
    sums = []
    for sent, own_part in ((inner, mine[0]), (rim, mine[1])):
        got = [permute(x, to_part(s)) for s, x in zip(away, sent)]
        sums.append(sum_call([own_part, *got], frames))

    share = depth // frames

    def frame_home(t, z, p):
        frame = t % CORES * frames + (z + p) % frames
        slot = frame * share + z // frames
        return (t // CORES * CORES + slot % CORES, slot // CORES)

    def next_in_frame(t, z, step):
        slot = z * CORES + t % CORES
        slot = slot // share * share + (slot + step) % share
        return (t // CORES * CORES + slot % CORES, slot // CORES)

    own = []
    for p in range(frames):
        for chunk in sums:
            own.append(permute(chunk[p], lambda t, z: frame_home(t, z, p)))
    others = []
    for step in range(1, share):
        others += [permute(x, lambda t, z: next_in_frame(t, z, step)) for x in own]

    done = attend_call(
        own,
        others,
        (query_weight, key_weight, value_weight, out_weight),
        frames,
        rows_here,
        columns,
    )
    back = []
    for p in range(frames):
        pairs = [(b, a) for a, b in everywhere(sizes, lambda t, z: frame_home(t, z, p))]
        back.append(lax.ppermute(done[p], BOTH, pairs))
    return place_call(meta, back)


def solution(mesh):
    placed = (P("tm", "rows", None, None), P(None, "tm", None), P(), P(), P(), P())
    return jax.shard_map(
        body, mesh=mesh, in_specs=placed, out_specs=P("tm", "rows", None, None), check_vma=False
    )
```

```python
import functools

import jax
import jax.numpy as jnp
from jax import lax
from jax.experimental import pallas as pl
from jax.experimental.pallas import tpu as pltpu
from jax.sharding import PartitionSpec as P

G = 32
LANES = 128
CORES = 2

epsilon = 1e-06

BOTH = ("tm", "rows")
VMEM_LIMIT = 32 * 1024 * 1024


def everywhere(sizes, target):
    devices, depth = sizes
    pairs = []
    for t in range(devices):
        for z in range(depth):
            to = target(t, z)
            if to is not None:
                pairs.append((t * depth + z, to[0] * depth + to[1]))
    return pairs


def in_vmem(count):
    return [pl.BlockSpec(memory_space=pltpu.VMEM)] * count


def merge_kernel(group, *refs):
    meta, refs = refs[0], refs[1:]
    slices, out, sems = refs[:group], refs[group], refs[group + 1]
    chans_here = slices[0].shape[2]
    copies = []
    for lag in range(out.shape[0]):
        for step in range(group):
            owner = lax.rem(meta[1] - step + group, group)
            rows = pl.ds(pl.multiple_of(owner * chans_here, 16), chans_here)
            copies.append(
                pltpu.make_async_copy(
                    slices[step].at[:, lag], out.at[lag, :, rows], sems.at[lag, step]
                )
            )
    for copy in copies:
        copy.start()
    for copy in copies:
        copy.wait()


def merge_call(meta, slices):
    group = len(slices)
    taps, lags, chans_here, chans = slices[0].shape
    return pl.pallas_call(
        functools.partial(merge_kernel, group),
        out_shape=jax.ShapeDtypeStruct((lags, taps, group * chans_here, chans), jnp.bfloat16),
        in_specs=[pl.BlockSpec(memory_space=pltpu.SMEM)]
        + [pl.BlockSpec(memory_space=pl.ANY)] * group,
        out_specs=pl.BlockSpec(memory_space=pltpu.VMEM),
        scratch_shapes=[pltpu.SemaphoreType.DMA((lags, group))],
        compiler_params=pltpu.CompilerParams(vmem_limit_bytes=VMEM_LIMIT),
        name="merge_kernel_slices",
    )(meta, *slices)


def partner(member, place):
    odd = member % 2 == 1
    if isinstance(member, int) and isinstance(place, int):
        return 3 - place if odd and place in (1, 2) else place
    swapped = jnp.where(jnp.logical_or(place == 1, place == 2), 3 - place, place)
    return jnp.where(odd, swapped, place)


def split_call(meta, above, below, parts):
    frames, columns, chans = above.shape
    width = chans // parts

    def kernel(meta, above, below, *outs):
        for place, out in enumerate(outs):
            to = lax.bitwise_xor(meta[0], partner(meta[1], jnp.int32(place)))
            lanes = pl.ds(pl.multiple_of(to * width, width), width)
            out[0] = above[:, :, lanes]
            out[1] = below[:, :, lanes]

    return pl.pallas_call(
        kernel,
        out_shape=[jax.ShapeDtypeStruct((2, frames, columns, width), above.dtype)] * parts,
        in_specs=[pl.BlockSpec(memory_space=pltpu.SMEM)] + in_vmem(2),
        out_specs=in_vmem(parts),
        compiler_params=pltpu.CompilerParams(vmem_limit_bytes=VMEM_LIMIT),
        name="split_halo_rows",
    )(meta, above, below)


def stack_call(pieces, after):
    def kernel(*refs):
        for i in range(len(pieces)):
            refs[-1][i] = refs[i][...]

    return pl.pallas_call(
        kernel,
        out_shape=jax.ShapeDtypeStruct((len(pieces), *pieces[0].shape), pieces[0].dtype),
        in_specs=in_vmem(len(pieces)) + [pl.BlockSpec(memory_space=pl.ANY)],
        out_specs=pl.BlockSpec(memory_space=pltpu.VMEM),
        compiler_params=pltpu.CompilerParams(vmem_limit_bytes=VMEM_LIMIT),
        name="stack_halo_rows",
    )(*pieces, after)


def conv_kernel(jobs, parts, group, frames, out_count, *refs):
    meta, weights, refs = refs[0], refs[1], refs[2:]
    dests = sorted({s for s, _ in jobs})
    any_rim = any(rim for _, rim in jobs)
    held, refs = refs[: len(dests)], refs[len(dests) :]
    before, refs = refs[:parts], refs[parts:]
    if any_rim:
        (rims, rims_before), refs = refs[:2], refs[2:]
    outs, raw = refs[:-1], refs[-1]
    outs = outs[len(outs) - out_count :]
    part, member, z = meta[0], meta[1], meta[2]
    lags, _, width, chans = weights.shape
    _, rows_here, columns, _ = held[0].shape

    first = member == 0
    for n, where in enumerate(dests):
        to = lax.bitwise_xor(part, partner(member, jnp.int32(where)))
        valid = jnp.logical_or(jnp.logical_not(first), to > 0)
        sender = jnp.where(first, group - 1, member - 1)
        want = jnp.where(first, jnp.maximum(to - 1, 0), to)
        place = partner(sender, lax.bitwise_xor(part, want))
        raw[n, frames:, 1 : 1 + rows_here] = held[n][...]
        if any_rim:
            raw[n, frames:, 0] = rims[where, 0]
            raw[n, frames:, 1 + rows_here] = rims[where, 1]
            raw[n, :frames, 0] = rims_before[place, 0]
            raw[n, :frames, 1 + rows_here] = rims_before[place, 1]
        for i in range(parts):

            @pl.when(place == i)
            def _():
                raw[n, :frames, 1 : 1 + rows_here] = before[i][...]

        @pl.when(jnp.logical_not(valid))
        def _():
            raw[n, :frames] = jnp.zeros_like(raw[n, :frames])

    side = 3

    def patches(a, b):
        pieces = []
        for s, rim in jobs:
            n = dests.index(s)
            for p in range(frames):
                f = lax.rem(z + p, frames) + a
                if rim:
                    pieces.append(raw[n, f, b])
                    pieces.append(raw[n, f, rows_here - 1 + b])
                else:
                    pieces.append(raw[n, f, 1 + b : b + rows_here - 1].reshape(-1, width))
        return jnp.concatenate(pieces, axis=0)

    lhs = jnp.concatenate([patches(a, b) for a in range(side) for b in range(side)], axis=1)
    count = lhs.shape[0]
    column = lax.broadcasted_iota(jnp.int32, (count, chans), 0) % columns
    total = None
    for lag in (1, 0, 2):
        product = jnp.dot(
            lhs, weights[lag].reshape(-1, chans), preferred_element_type=jnp.float32
        )
        if lag == 1:
            total = product
        elif lag == 0:
            total = total + jnp.where(column == 0, 0.0, pltpu.roll(product, 1, 0))
        else:
            moved = pltpu.roll(product, count - 1, 0)
            total = total + jnp.where(column == columns - 1, 0.0, moved)
    place = 0
    for out in outs:
        out[...] = total[place : place + out.shape[0]].astype(out.dtype)
        place += out.shape[0]


def conv_call(jobs, meta, weights, held, before, rims, group, frames, joined, after=()):
    parts = len(held)
    dests = sorted({place for place, _ in jobs})
    _, rows_here, columns, width = held[0].shape
    lags, taps, _, chans = weights.shape
    any_rim = any(rim for _, rim in jobs)
    counts = [frames * (2 if rim else rows_here - 2) * columns for _, rim in jobs]
    total = sum(counts)
    operands = [weights, *[held[n] for n in dests], *before, *(rims if any_rim else ())]
    specs = [pl.BlockSpec(memory_space=pltpu.SMEM)] + in_vmem(len(operands))
    specs += [pl.BlockSpec(memory_space=pl.ANY)] * len(after)
    if joined:
        outs = [jax.ShapeDtypeStruct((total, chans), jnp.bfloat16)]
    else:
        outs = [jax.ShapeDtypeStruct((count, chans), jnp.float32) for count in counts]
    return pl.pallas_call(
        functools.partial(conv_kernel, tuple(jobs), parts, group, frames, len(outs)),
        out_shape=outs,
        in_specs=specs,
        out_specs=in_vmem(len(outs)),
        scratch_shapes=[
            pltpu.VMEM((len(dests), 2 * frames, rows_here + 2, columns, width), jnp.bfloat16)
        ],
        compiler_params=pltpu.CompilerParams(vmem_limit_bytes=VMEM_LIMIT),
        cost_estimate=pl.CostEstimate(
            flops=2 * total * taps * lags * width * chans,
            bytes_accessed=2 * taps * lags * width * chans,
            transcendentals=0,
        ),
        name="conv_rim" if any_rim else "conv_inner",
    )(meta, *operands, *after)


def sum_call(pieces, splits, after=()):
    count = pieces[0][0].shape[0]
    chans = pieces[0][0].shape[1]
    size = count // splits
    out = jax.ShapeDtypeStruct((size, chans), jnp.bfloat16)

    def kernel(*refs):
        for p, out_ref in enumerate(refs[len(refs) - splits :]):
            total = None
            for (_, start), ref in zip(pieces, refs):
                rows = ref[start + p * size : start + (p + 1) * size].astype(jnp.float32)
                total = rows if total is None else total + rows
            out_ref[...] = total.astype(out_ref.dtype)

    return pl.pallas_call(
        kernel,
        out_shape=[out] * splits,
        in_specs=in_vmem(len(pieces)) + [pl.BlockSpec(memory_space=pl.ANY)] * len(after),
        out_specs=in_vmem(splits),
        compiler_params=pltpu.CompilerParams(vmem_limit_bytes=VMEM_LIMIT),
        name="sum_parts",
    )(*[array for array, _ in pieces], *after)


def attend_kernel(frames, share, chunks, *refs):
    own_count = frames * chunks
    all_count = own_count * share
    tokens, refs = refs[:all_count], refs[all_count:]
    (wq, wk, wv, wo), refs = refs[:4], refs[4:]
    outs, (normed, keys, values) = refs[:frames], refs[frames:]
    size, chans = normed.shape
    per_group = chans // G

    tile_row = lax.broadcasted_iota(jnp.int32, (LANES, LANES), 0) // per_group
    tile_col = lax.broadcasted_iota(jnp.int32, (LANES, LANES), 1) // per_group
    same = (tile_row == tile_col).astype(jnp.float32).astype(jnp.bfloat16)

    def group_mean(sums):
        first = sums.astype(jnp.bfloat16)
        rest = sums - first.astype(jnp.float32)
        second = rest.astype(jnp.bfloat16)
        third = rest - second.astype(jnp.float32)
        tiles = []
        for tile in range(chans // LANES):
            lanes = slice(tile * LANES, (tile + 1) * LANES)
            stacked = jnp.concatenate(
                [
                    first.astype(jnp.float32)[:, lanes],
                    second.astype(jnp.float32)[:, lanes],
                    third[:, lanes],
                ],
                axis=0,
            ).astype(jnp.bfloat16)
            spread = jnp.dot(stacked, same, preferred_element_type=jnp.float32)
            tiles.append(jnp.sum(spread, axis=0, keepdims=True))
        return jnp.concatenate(tiles, axis=1) / (size * per_group)

    def folded(x):
        return jnp.sum(x.reshape(-1, 8, chans), axis=0)

    average = group_mean(sum(folded(ref[...].astype(jnp.float32)) for ref in tokens))

    def spread_of(ref):
        centered = ref[...].astype(jnp.float32) - average
        return folded(centered * centered)

    scale = lax.rsqrt(group_mean(sum(spread_of(ref) for ref in tokens)) + epsilon)
    place = 0
    for ref in tokens:
        rows = ref.shape[0]
        normed[pl.ds(place, rows)] = (
            (ref[...].astype(jnp.float32) - average) * scale
        ).astype(jnp.bfloat16)
        place += rows

    step = min(256, size)
    for start in range(0, size, step):
        x = normed[pl.ds(start, step)]
        keys[pl.ds(start, step)] = jnp.dot(
            x, wk[...], preferred_element_type=jnp.float32
        ).astype(jnp.bfloat16)
        values[pl.ds(start, step)] = jnp.dot(
            x, wv[...], preferred_element_type=jnp.float32
        ).astype(jnp.bfloat16)

    place = 0
    for p, out in enumerate(outs):
        mine = tokens[p * chunks : (p + 1) * chunks]
        rows = sum(ref.shape[0] for ref in mine)
        queries = jnp.dot(
            normed[pl.ds(place, rows)], wq[...], preferred_element_type=jnp.float32
        ).astype(jnp.bfloat16)
        place += rows
        scores = lax.dot_general(
            queries, keys[...], (((1,), (1,)), ((), ())), preferred_element_type=jnp.float32
        ) * chans ** (-0.5)
        row_max = jnp.max(scores, axis=1, keepdims=True)
        exp_weights = jnp.exp(scores - row_max).astype(jnp.bfloat16)
        denominator = jnp.sum(exp_weights.astype(jnp.float32), axis=1, keepdims=True)
        numerator = jnp.dot(exp_weights, values[...], preferred_element_type=jnp.float32)
        attended = (numerator / denominator).astype(jnp.bfloat16)
        added = jnp.dot(attended, wo[...], preferred_element_type=jnp.float32)
        rows_here, columns, _ = out.shape
        inner = mine[0].shape[0]
        first = mine[0][...].astype(jnp.float32) + added[:inner]
        out[1 : rows_here - 1] = first.astype(jnp.bfloat16).reshape(rows_here - 2, columns, chans)
        second = (mine[1][...].astype(jnp.float32) + added[inner:]).astype(jnp.bfloat16)
        out[0] = second[:columns]
        out[rows_here - 1] = second[columns:]


def attend_call(own, others, weights, frames, rows_here, columns):
    chunks = len(own) // frames
    share = 1 + len(others) // len(own)
    chans = own[0].shape[1]
    size = sum(x.shape[0] for x in own) * share
    mine = size // share
    out = jax.ShapeDtypeStruct((rows_here, columns, chans), jnp.bfloat16)
    operands = [*own, *others, *weights]
    return pl.pallas_call(
        functools.partial(attend_kernel, frames, share, chunks),
        out_shape=[out] * frames,
        in_specs=in_vmem(len(operands)),
        out_specs=in_vmem(frames),
        scratch_shapes=[pltpu.VMEM((size, chans), jnp.bfloat16)] * 3,
        compiler_params=pltpu.CompilerParams(vmem_limit_bytes=VMEM_LIMIT),
        cost_estimate=pl.CostEstimate(
            flops=2 * (2 * size * chans * chans + 2 * mine * chans * (chans + size)),
            bytes_accessed=8 * chans * chans + 2 * size * chans,
            transcendentals=mine * size,
        ),
        name="attend",
    )(*operands)


def body(latents, conv_weight, query_weight, key_weight, value_weight, out_weight):
    frames, rows_here, columns, chans = latents.shape
    taps, chans_here, _ = conv_weight.shape
    devices, depth = lax.axis_size("tm"), lax.axis_size("rows")
    sizes = (devices, depth)
    group = LANES // chans_here
    parts = devices // group
    width = group * chans_here
    t_index, z_index = lax.axis_index("tm"), lax.axis_index("rows")
    part, member = t_index // group, t_index % group
    meta = jnp.stack([part, member, z_index]).astype(jnp.int32)

    def permute(block, target):
        return lax.ppermute(block, BOTH, everywhere(sizes, target))

    def to_place(place):
        return lambda t, z: ((t // group ^ partner(t % group, place)) * group + t % group, z)

    def to_member(step):
        return lambda t, z: (t // group * group + (t + step) % group, z)

    split = conv_weight.reshape(taps // 3, 3, chans_here, chans)
    slices = [split] + [permute(split, to_member(step)) for step in range(1, group)]
    weights = merge_call(meta, slices)

    above = permute(latents[:, -1], lambda t, z: (t, z + 1) if z + 1 < depth else None)
    below = permute(latents[:, 0], lambda t, z: (t, z - 1) if z else None)

    held, before = [None] * parts, [None] * parts
    order = [0, 3, 1, 2]
    for place in order:
        start = (part ^ partner(member, jnp.int32(place))) * width
        piece = lax.dynamic_slice_in_dim(latents, start, width, axis=3)
        held[place] = permute(piece, to_place(place)) if place else piece
    rims = split_call(meta, above, below, parts)
    rims = [permute(x, to_place(place)) if place else x for place, x in enumerate(rims)]
    held[2], weights = lax.optimization_barrier((held[2], weights))
    for place in order:
        before[place] = permute(held[place], to_member(1))

    conv = functools.partial(
        conv_call,
        meta=meta,
        weights=weights,
        held=held,
        before=before,
        group=group,
        frames=frames,
    )

    (inner_sent,) = conv([(1, False), (3, False)], rims=None, joined=True)
    rims = stack_call(rims, inner_sent)
    rims = (rims, permute(rims, to_member(1)))
    (rim_sent,) = conv([(1, True), (3, True)], rims=rims, joined=True)
    inner_got = permute(inner_sent, to_place(1))
    rim_got = permute(rim_sent, to_place(1))
    inner_on, inner_own = conv(
        [(2, False), (0, False)], rims=None, joined=False, after=(rim_sent,)
    )
    half = inner_on.shape[0]
    (inner_relay,) = sum_call([(inner_on, 0), (inner_got, half)], 1)
    rim_on, rim_own = conv([(2, True), (0, True)], rims=rims, joined=False, after=(inner_relay,))
    (rim_relay,) = sum_call([(rim_on, 0), (rim_got, rim_on.shape[0])], 1)
    inner_last = permute(inner_relay, to_place(2))
    rim_last = permute(rim_relay, to_place(2))
    sums = [
        sum_call([(inner_own, 0), (inner_got, 0), (inner_last, 0)], frames, after=(rim_relay,)),
        sum_call([(rim_own, 0), (rim_got, 0), (rim_last, 0)], frames),
    ]

    share = depth // frames

    def frame_home(t, z, p):
        frame = t % CORES * frames + (z + p) % frames
        slot = frame * share + z // frames
        return (t // CORES * CORES + slot % CORES, slot // CORES)

    def next_in_frame(t, z, step):
        slot = z * CORES + t % CORES
        slot = slot // share * share + (slot + step) % share
        return (t // CORES * CORES + slot % CORES, slot // CORES)

    own = []
    for p in range(frames):
        for chunk in sums:
            own.append(permute(chunk[p], lambda t, z: frame_home(t, z, p)))
    others = []
    for step in range(1, share):
        others += [permute(x, lambda t, z: next_in_frame(t, z, step)) for x in own]

    done = attend_call(
        own,
        others,
        (query_weight, key_weight, value_weight, out_weight),
        frames,
        rows_here,
        columns,
    )
    back = []
    for p in range(frames):
        pairs = [(b, a) for a, b in everywhere(sizes, lambda t, z: frame_home(t, z, p))]
        back.append(lax.ppermute(done[p], BOTH, pairs))
    return jnp.stack(
        [
            functools.reduce(
                lambda rest, p: jnp.where((z_index + p) % frames == f, back[p], rest),
                range(1, frames),
                back[0],
            )
            for f in range(frames)
        ]
    )


def solution(mesh):
    placed = (P("tm", "rows", None, None), P(None, "tm", None), P(), P(), P(), P())
    return jax.shard_map(
        body, mesh=mesh, in_specs=placed, out_specs=P("tm", "rows", None, None), check_vma=False
    )
```

```python
import functools

import jax
import jax.numpy as jnp
from jax import lax
from jax.experimental import pallas as pl
from jax.experimental.pallas import tpu as pltpu
from jax.sharding import PartitionSpec as P

G = 32
LANES = 128
CORES = 2

epsilon = 1e-06

BOTH = ("tm", "rows")
VMEM_LIMIT = 32 * 1024 * 1024


def everywhere(sizes, target):
    devices, depth = sizes
    pairs = []
    for t in range(devices):
        for z in range(depth):
            to = target(t, z)
            if to is not None:
                pairs.append((t * depth + z, to[0] * depth + to[1]))
    return pairs


def in_vmem(count):
    return [pl.BlockSpec(memory_space=pltpu.VMEM)] * count


def merge_kernel(group, *refs):
    meta, refs = refs[0], refs[1:]
    slices, out, sems = refs[:group], refs[group], refs[group + 1]
    chans_here = slices[0].shape[2]
    copies = []
    for lag in range(out.shape[0]):
        for step in range(group):
            owner = lax.rem(meta[1] - step + group, group)
            rows = pl.ds(pl.multiple_of(owner * chans_here, 16), chans_here)
            copies.append(
                pltpu.make_async_copy(
                    slices[step].at[:, lag], out.at[lag, :, rows], sems.at[lag, step]
                )
            )
    for copy in copies:
        copy.start()
    for copy in copies:
        copy.wait()


def merge_call(meta, slices):
    group = len(slices)
    taps, lags, chans_here, chans = slices[0].shape
    return pl.pallas_call(
        functools.partial(merge_kernel, group),
        out_shape=jax.ShapeDtypeStruct((lags, taps, group * chans_here, chans), jnp.bfloat16),
        in_specs=[pl.BlockSpec(memory_space=pltpu.SMEM)]
        + [pl.BlockSpec(memory_space=pltpu.HBM)]
        + [pl.BlockSpec(memory_space=pl.ANY)] * (group - 1),
        out_specs=pl.BlockSpec(memory_space=pltpu.VMEM),
        scratch_shapes=[pltpu.SemaphoreType.DMA((lags, group))],
        compiler_params=pltpu.CompilerParams(vmem_limit_bytes=VMEM_LIMIT),
        name="merge_kernel_slices",
    )(meta, *slices)


def partner(member, place):
    odd = member % 2 == 1
    if isinstance(member, int) and isinstance(place, int):
        return 3 - place if odd and place in (1, 2) else place
    swapped = jnp.where(jnp.logical_or(place == 1, place == 2), 3 - place, place)
    return jnp.where(odd, swapped, place)


def split_call(meta, above, below, parts):
    frames, columns, chans = above.shape
    width = chans // parts

    def kernel(meta, above, below, *outs):
        for place, out in enumerate(outs):
            to = lax.bitwise_xor(meta[0], partner(meta[1], jnp.int32(place)))
            lanes = pl.ds(pl.multiple_of(to * width, width), width)
            out[0] = above[:, :, lanes]
            out[1] = below[:, :, lanes]

    return pl.pallas_call(
        kernel,
        out_shape=[jax.ShapeDtypeStruct((2, frames, columns, width), above.dtype)] * parts,
        in_specs=[pl.BlockSpec(memory_space=pltpu.SMEM)] + in_vmem(2),
        out_specs=in_vmem(parts),
        compiler_params=pltpu.CompilerParams(vmem_limit_bytes=VMEM_LIMIT),
        name="split_halo_rows",
    )(meta, above, below)


def stack_call(pieces, after):
    def kernel(*refs):
        for i in range(len(pieces)):
            refs[-1][i] = refs[i][...]

    return pl.pallas_call(
        kernel,
        out_shape=jax.ShapeDtypeStruct((len(pieces), *pieces[0].shape), pieces[0].dtype),
        in_specs=in_vmem(len(pieces) + 1),
        out_specs=pl.BlockSpec(memory_space=pltpu.VMEM),
        compiler_params=pltpu.CompilerParams(vmem_limit_bytes=VMEM_LIMIT),
        name="stack_halo_rows",
    )(*pieces, after)


def conv_kernel(jobs, parts, group, frames, out_count, *refs):
    meta, weights, refs = refs[0], refs[1], refs[2:]
    dests = sorted({s for s, _ in jobs})
    any_rim = any(rim for _, rim in jobs)
    held, refs = refs[: len(dests)], refs[len(dests) :]
    before, refs = refs[:parts], refs[parts:]
    if any_rim:
        (rims, rims_before), refs = refs[:2], refs[2:]
    outs, raw = refs[:-1], refs[-1]
    outs = outs[len(outs) - out_count :]
    part, member, z = meta[0], meta[1], meta[2]
    lags, _, width, chans = weights.shape
    _, rows_here, columns, _ = held[0].shape

    first = member == 0
    for n, where in enumerate(dests):
        to = lax.bitwise_xor(part, partner(member, jnp.int32(where)))
        valid = jnp.logical_or(jnp.logical_not(first), to > 0)
        sender = jnp.where(first, group - 1, member - 1)
        want = jnp.where(first, jnp.maximum(to - 1, 0), to)
        place = partner(sender, lax.bitwise_xor(part, want))
        raw[n, frames:, 1 : 1 + rows_here] = held[n][...]
        if any_rim:
            raw[n, frames:, 0] = rims[where, 0]
            raw[n, frames:, 1 + rows_here] = rims[where, 1]
            raw[n, :frames, 0] = rims_before[place, 0]
            raw[n, :frames, 1 + rows_here] = rims_before[place, 1]
        for i in range(parts):

            @pl.when(place == i)
            def _():
                raw[n, :frames, 1 : 1 + rows_here] = before[i][...]

        @pl.when(jnp.logical_not(valid))
        def _():
            raw[n, :frames] = jnp.zeros_like(raw[n, :frames])

    side = 3

    def patches(a, b):
        pieces = []
        for s, rim in jobs:
            n = dests.index(s)
            for p in range(frames):
                f = lax.rem(z + p, frames) + a
                if rim:
                    pieces.append(raw[n, f, b])
                    pieces.append(raw[n, f, rows_here - 1 + b])
                else:
                    pieces.append(raw[n, f, 1 + b : b + rows_here - 1].reshape(-1, width))
        return jnp.concatenate(pieces, axis=0)

    lhs = jnp.concatenate([patches(a, b) for a in range(side) for b in range(side)], axis=1)
    count = lhs.shape[0]
    column = lax.broadcasted_iota(jnp.int32, (count, chans), 0) % columns
    total = None
    for lag in (1, 0, 2):
        product = jnp.dot(
            lhs, weights[lag].reshape(-1, chans), preferred_element_type=jnp.float32
        )
        if lag == 1:
            total = product
        elif lag == 0:
            total = total + jnp.where(column == 0, 0.0, pltpu.roll(product, 1, 0))
        else:
            moved = pltpu.roll(product, count - 1, 0)
            total = total + jnp.where(column == columns - 1, 0.0, moved)
    place = 0
    for out in outs:
        out[...] = total[place : place + out.shape[0]].astype(out.dtype)
        place += out.shape[0]


def conv_call(jobs, meta, weights, held, before, rims, group, frames, out_type, after=()):
    parts = len(held)
    dests = sorted({place for place, _ in jobs})
    _, rows_here, columns, width = held[0].shape
    lags, taps, _, chans = weights.shape
    any_rim = any(rim for _, rim in jobs)
    counts = [frames * (2 if rim else rows_here - 2) * columns for _, rim in jobs]
    total = sum(counts)
    operands = [weights, *[held[n] for n in dests], *before, *(rims if any_rim else ())]
    specs = [pl.BlockSpec(memory_space=pltpu.SMEM)] + in_vmem(len(operands))
    specs += in_vmem(len(after))
    outs = [jax.ShapeDtypeStruct((count, chans), out_type) for count in counts]
    return pl.pallas_call(
        functools.partial(conv_kernel, tuple(jobs), parts, group, frames, len(outs)),
        out_shape=outs,
        in_specs=specs,
        out_specs=in_vmem(len(outs)),
        scratch_shapes=[
            pltpu.VMEM((len(dests), 2 * frames, rows_here + 2, columns, width), jnp.bfloat16)
        ],
        compiler_params=pltpu.CompilerParams(vmem_limit_bytes=VMEM_LIMIT),
        cost_estimate=pl.CostEstimate(flops=10**11, bytes_accessed=1000, transcendentals=0),
        name="conv_rim" if any_rim else "conv_inner",
    )(meta, *operands, *after)


def sum_call(pieces, splits, after=()):
    count, chans = pieces[0].shape
    size = count // splits

    def kernel(*refs):
        for p, out_ref in enumerate(refs[len(refs) - splits :]):
            total = None
            for ref in refs[: len(pieces)]:
                rows = ref[p * size : (p + 1) * size].astype(jnp.float32)
                total = rows if total is None else total + rows
            out_ref[...] = total.astype(out_ref.dtype)

    return pl.pallas_call(
        kernel,
        out_shape=[jax.ShapeDtypeStruct((size, chans), jnp.bfloat16)] * splits,
        in_specs=in_vmem(len(pieces) + len(after)),
        out_specs=in_vmem(splits),
        compiler_params=pltpu.CompilerParams(vmem_limit_bytes=VMEM_LIMIT),
        name="sum_parts",
    )(*pieces, *after)


def attend_kernel(frames, share, chunks, *refs):
    own_count = frames * chunks
    all_count = own_count * share
    tokens, refs = refs[:all_count], refs[all_count:]
    (wq, wk, wv, wo), refs = refs[:4], refs[4:]
    outs, (normed, keys, values) = refs[:frames], refs[frames:]
    size, chans = normed.shape
    per_group = chans // G

    tile_row = lax.broadcasted_iota(jnp.int32, (LANES, LANES), 0) // per_group
    tile_col = lax.broadcasted_iota(jnp.int32, (LANES, LANES), 1) // per_group
    same = (tile_row == tile_col).astype(jnp.float32).astype(jnp.bfloat16)

    def group_mean(sums):
        first = sums.astype(jnp.bfloat16)
        rest = sums - first.astype(jnp.float32)
        second = rest.astype(jnp.bfloat16)
        third = rest - second.astype(jnp.float32)
        tiles = []
        for tile in range(chans // LANES):
            lanes = slice(tile * LANES, (tile + 1) * LANES)
            stacked = jnp.concatenate(
                [
                    first.astype(jnp.float32)[:, lanes],
                    second.astype(jnp.float32)[:, lanes],
                    third[:, lanes],
                ],
                axis=0,
            ).astype(jnp.bfloat16)
            spread = jnp.dot(stacked, same, preferred_element_type=jnp.float32)
            tiles.append(jnp.sum(spread, axis=0, keepdims=True))
        return jnp.concatenate(tiles, axis=1) / (size * per_group)

    def folded(x):
        return jnp.sum(x.reshape(-1, 8, chans), axis=0)

    average = group_mean(sum(folded(ref[...].astype(jnp.float32)) for ref in tokens))

    def spread_of(ref):
        centered = ref[...].astype(jnp.float32) - average
        return folded(centered * centered)

    scale = lax.rsqrt(group_mean(sum(spread_of(ref) for ref in tokens)) + epsilon)
    place = 0
    for ref in tokens:
        rows = ref.shape[0]
        normed[pl.ds(place, rows)] = (
            (ref[...].astype(jnp.float32) - average) * scale
        ).astype(jnp.bfloat16)
        place += rows

    step = min(256, size)
    for start in range(0, size, step):
        x = normed[pl.ds(start, step)]
        keys[pl.ds(start, step)] = jnp.dot(
            x, wk[...], preferred_element_type=jnp.float32
        ).astype(jnp.bfloat16)
        values[pl.ds(start, step)] = jnp.dot(
            x, wv[...], preferred_element_type=jnp.float32
        ).astype(jnp.bfloat16)

    place = 0
    for p, out in enumerate(outs):
        mine = tokens[p * chunks : (p + 1) * chunks]
        rows = sum(ref.shape[0] for ref in mine)
        queries = jnp.dot(
            normed[pl.ds(place, rows)], wq[...], preferred_element_type=jnp.float32
        ).astype(jnp.bfloat16)
        place += rows
        scores = lax.dot_general(
            queries, keys[...], (((1,), (1,)), ((), ())), preferred_element_type=jnp.float32
        ) * chans ** (-0.5)
        row_max = jnp.max(scores, axis=1, keepdims=True)
        exp_weights = jnp.exp(scores - row_max).astype(jnp.bfloat16)
        denominator = jnp.sum(exp_weights.astype(jnp.float32), axis=1, keepdims=True)
        numerator = jnp.dot(exp_weights, values[...], preferred_element_type=jnp.float32)
        attended = (numerator / denominator).astype(jnp.bfloat16)
        added = jnp.dot(attended, wo[...], preferred_element_type=jnp.float32)
        rows_here, columns, _ = out.shape
        inner = mine[0].shape[0]
        first = mine[0][...].astype(jnp.float32) + added[:inner]
        out[1 : rows_here - 1] = first.astype(jnp.bfloat16).reshape(rows_here - 2, columns, chans)
        second = (mine[1][...].astype(jnp.float32) + added[inner:]).astype(jnp.bfloat16)
        out[0] = second[:columns]
        out[rows_here - 1] = second[columns:]


def attend_call(own, others, weights, frames, rows_here, columns):
    chunks = len(own) // frames
    share = 1 + len(others) // len(own)
    chans = own[0].shape[1]
    size = sum(x.shape[0] for x in own) * share
    mine = size // share
    out = jax.ShapeDtypeStruct((rows_here, columns, chans), jnp.bfloat16)
    operands = [*own, *others, *weights]
    return pl.pallas_call(
        functools.partial(attend_kernel, frames, share, chunks),
        out_shape=[out] * frames,
        in_specs=in_vmem(len(operands)),
        out_specs=in_vmem(frames),
        scratch_shapes=[pltpu.VMEM((size, chans), jnp.bfloat16)] * 3,
        compiler_params=pltpu.CompilerParams(vmem_limit_bytes=VMEM_LIMIT),
        cost_estimate=pl.CostEstimate(
            flops=2 * (2 * size * chans * chans + 2 * mine * chans * (chans + size)),
            bytes_accessed=8 * chans * chans + 2 * size * chans,
            transcendentals=mine * size,
        ),
        name="attend",
    )(*operands)


def body(latents, conv_weight, query_weight, key_weight, value_weight, out_weight):
    frames, rows_here, columns, chans = latents.shape
    taps, chans_here, _ = conv_weight.shape
    devices, depth = lax.axis_size("tm"), lax.axis_size("rows")
    sizes = (devices, depth)
    group = LANES // chans_here
    parts = devices // group
    width = group * chans_here
    t_index, z_index = lax.axis_index("tm"), lax.axis_index("rows")
    part, member = t_index // group, t_index % group
    meta = jnp.stack([part, member, z_index]).astype(jnp.int32)

    def permute(block, target):
        return lax.ppermute(block, BOTH, everywhere(sizes, target))

    def to_place(place):
        return lambda t, z: ((t // group ^ partner(t % group, place)) * group + t % group, z)

    def to_member(step):
        return lambda t, z: (t // group * group + (t + step) % group, z)

    split = conv_weight.reshape(taps // 3, 3, chans_here, chans)
    slices = [split] + [permute(split, to_member(step)) for step in range(1, group)]
    weights = merge_call(meta, slices)

    above = permute(latents[:, -1], lambda t, z: (t, z + 1) if z + 1 < depth else None)
    below = permute(latents[:, 0], lambda t, z: (t, z - 1) if z else None)

    held, before = [None] * parts, [None] * parts
    order = [0, 3, 1, 2]
    for place in order:
        start = (part ^ partner(member, jnp.int32(place))) * width
        piece = lax.dynamic_slice_in_dim(latents, start, width, axis=3)
        held[place] = permute(piece, to_place(place)) if place else piece
    held[2], weights = lax.optimization_barrier((held[2], weights))
    for place in order:
        before[place] = permute(held[place], to_member(1))

    conv = functools.partial(
        conv_call,
        meta=meta,
        weights=weights,
        held=held,
        before=before,
        group=group,
        frames=frames,
    )

    def hop(pieces):
        return [permute(x, to_place(1)) for x in pieces]

    rims = split_call(meta, above, below, parts)
    inner_sent = conv(
        [(3, False), (1, False)], rims=None, out_type=jnp.bfloat16, after=rims[:1]
    )
    inner_got = hop(inner_sent)
    inner_on, inner_own = conv(
        [(2, False), (0, False)], rims=None, out_type=jnp.float32, after=inner_sent[:1]
    )
    rims, _ = lax.optimization_barrier((rims, inner_sent[0]))
    rims = [permute(x, to_place(place)) if place else x for place, x in enumerate(rims)]
    rims = stack_call(rims, inner_on)
    rims = (rims, permute(rims, to_member(1)))
    (inner_relay,) = sum_call([inner_on, inner_got[0]], 1, after=inner_got[1:])
    rim_sent = conv(
        [(3, True), (1, True)], rims=rims, out_type=jnp.bfloat16, after=(inner_relay,)
    )
    rim_got = hop(rim_sent)
    inner_last = permute(inner_relay, to_place(2))
    rim_on, rim_own = conv(
        [(2, True), (0, True)], rims=rims, out_type=jnp.float32, after=rim_sent[:1]
    )
    (rim_relay,) = sum_call([rim_on, rim_got[0]], 1, after=rim_got[1:])
    rim_last = permute(rim_relay, to_place(2))
    sums = [
        sum_call([inner_own, inner_got[1], inner_last], frames),
        sum_call([rim_own, rim_got[1], rim_last], frames),
    ]

    share = depth // frames

    def frame_home(t, z, p):
        frame = t % CORES * frames + (z + p) % frames
        slot = frame * share + z // frames
        return (t // CORES * CORES + slot % CORES, slot // CORES)

    def next_in_frame(t, z, step):
        slot = z * CORES + t % CORES
        slot = slot // share * share + (slot + step) % share
        return (t // CORES * CORES + slot % CORES, slot // CORES)

    own = []
    for p in range(frames):
        for chunk in sums:
            own.append(permute(chunk[p], lambda t, z: frame_home(t, z, p)))
    others = []
    for step in range(1, share):
        others += [permute(x, lambda t, z: next_in_frame(t, z, step)) for x in own]

    done = attend_call(
        own,
        others,
        (query_weight, key_weight, value_weight, out_weight),
        frames,
        rows_here,
        columns,
    )
    back = []
    for p in range(frames):
        pairs = [(b, a) for a, b in everywhere(sizes, lambda t, z: frame_home(t, z, p))]
        back.append(lax.ppermute(done[p], BOTH, pairs))
    return jnp.stack(
        [
            functools.reduce(
                lambda rest, p: jnp.where((z_index + p) % frames == f, back[p], rest),
                range(1, frames),
                back[0],
            )
            for f in range(frames)
        ]
    )


def solution(mesh):
    placed = (P("tm", "rows", None, None), P(None, "tm", None), P(), P(), P(), P())
    return jax.shard_map(
        body, mesh=mesh, in_specs=placed, out_specs=P("tm", "rows", None, None), check_vma=False
    )
```

```python
import functools

import jax
import jax.numpy as jnp
from jax import lax
from jax.experimental import pallas as pl
from jax.experimental.pallas import tpu as pltpu
from jax.sharding import PartitionSpec as P

G = 32
LANES = 128
CORES = 2

epsilon = 1e-06

BOTH = ("tm", "rows")
VMEM_LIMIT = 16 * 1024 * 1024


def everywhere(sizes, target):
    devices, depth = sizes
    pairs = []
    for t in range(devices):
        for z in range(depth):
            to = target(t, z)
            if to is not None:
                pairs.append((t * depth + z, to[0] * depth + to[1]))
    return pairs


def in_vmem(count):
    return [pl.BlockSpec(memory_space=pltpu.VMEM)] * count


def merge_kernel(group, *refs):
    meta, refs = refs[0], refs[1:]
    slices, out, sems = refs[:group], refs[group], refs[group + 1]
    chans_here = slices[0].shape[2]
    copies = []
    for lag in range(out.shape[0]):
        for step in range(group):
            owner = lax.rem(meta[1] - step + group, group)
            rows = pl.ds(pl.multiple_of(owner * chans_here, 16), chans_here)
            copies.append(
                pltpu.make_async_copy(
                    slices[step].at[:, lag], out.at[lag, :, rows], sems.at[lag, step]
                )
            )
    for copy in copies:
        copy.start()
    for copy in copies:
        copy.wait()


def merge_call(meta, slices):
    group = len(slices)
    taps, lags, chans_here, chans = slices[0].shape
    return pl.pallas_call(
        functools.partial(merge_kernel, group),
        out_shape=jax.ShapeDtypeStruct((lags, taps, group * chans_here, chans), jnp.bfloat16),
        in_specs=[pl.BlockSpec(memory_space=pltpu.SMEM)]
        + [pl.BlockSpec(memory_space=pltpu.HBM)]
        + [pl.BlockSpec(memory_space=pl.ANY)] * (group - 1),
        out_specs=pl.BlockSpec(memory_space=pltpu.VMEM),
        scratch_shapes=[pltpu.SemaphoreType.DMA((lags, group))],
        compiler_params=pltpu.CompilerParams(vmem_limit_bytes=VMEM_LIMIT),
        name="merge_kernel_slices",
    )(meta, *slices)


def partner(member, place):
    odd = member % 2 == 1
    if isinstance(member, int) and isinstance(place, int):
        return 3 - place if odd and place in (1, 2) else place
    swapped = jnp.where(jnp.logical_or(place == 1, place == 2), 3 - place, place)
    return jnp.where(odd, swapped, place)


def frame_call(meta, latents, above, below, parts):
    frames, rows_here, columns, chans = latents.shape
    width = chans // parts

    def kernel(meta, latents, above, below, *outs):
        for place, out in enumerate(outs):
            to = lax.bitwise_xor(meta[0], partner(meta[1], jnp.int32(place)))
            lanes = pl.ds(pl.multiple_of(to * width, width), width)
            out[:, 0] = above[:, :, lanes]
            out[:, 1 : 1 + rows_here] = latents[:, :, :, lanes]
            out[:, 1 + rows_here] = below[:, :, lanes]

    return pl.pallas_call(
        kernel,
        out_shape=[
            jax.ShapeDtypeStruct((frames, rows_here + 2, columns, width), latents.dtype)
        ]
        * parts,
        in_specs=[pl.BlockSpec(memory_space=pltpu.SMEM)] + in_vmem(3),
        out_specs=in_vmem(parts),
        compiler_params=pltpu.CompilerParams(vmem_limit_bytes=VMEM_LIMIT),
        name="frame_parts",
    )(meta, latents, above, below)


def conv_kernel(jobs, parts, group, frames, *refs):
    meta, weights, refs = refs[0], refs[1], refs[2:]
    dests = sorted({place for place, _ in jobs})
    held, refs = refs[: len(dests)], refs[len(dests) :]
    before, refs = refs[:parts], refs[parts:]
    outs, raw = refs[-1 - len(jobs) : -1], refs[-1]
    part, member, z = meta[0], meta[1], meta[2]
    lags, _, width, chans = weights.shape
    _, rows_framed, columns, _ = held[0].shape
    rows_here = rows_framed - 2

    first = member == 0
    for n, where in enumerate(dests):
        to = lax.bitwise_xor(part, partner(member, jnp.int32(where)))
        valid = jnp.logical_or(jnp.logical_not(first), to > 0)
        sender = jnp.where(first, group - 1, member - 1)
        want = jnp.where(first, jnp.maximum(to - 1, 0), to)
        place = partner(sender, lax.bitwise_xor(part, want))
        raw[n, frames:] = held[n][...]
        for i in range(parts):

            @pl.when(place == i)
            def _():
                raw[n, :frames] = before[i][...]

        @pl.when(jnp.logical_not(valid))
        def _():
            raw[n, :frames] = jnp.zeros_like(raw[n, :frames])

    side = 3

    def patches(a, b):
        pieces = []
        for where, p in jobs:
            f = lax.rem(z + p, frames) + a
            pieces.append(raw[dests.index(where), f, b : b + rows_here].reshape(-1, width))
        return jnp.concatenate(pieces, axis=0)

    lhs = jnp.concatenate([patches(a, b) for a in range(side) for b in range(side)], axis=1)
    count = lhs.shape[0]
    column = lax.broadcasted_iota(jnp.int32, (count, chans), 0) % columns
    total = None
    for lag in (1, 0, 2):
        product = jnp.dot(
            lhs, weights[lag].reshape(-1, chans), preferred_element_type=jnp.float32
        )
        if lag == 1:
            total = product
        elif lag == 0:
            total = total + jnp.where(column == 0, 0.0, pltpu.roll(product, 1, 0))
        else:
            moved = pltpu.roll(product, count - 1, 0)
            total = total + jnp.where(column == columns - 1, 0.0, moved)
    size = rows_here * columns
    for n, out in enumerate(outs):
        out[...] = total[n * size : (n + 1) * size].astype(out.dtype)


def conv_call(jobs, meta, weights, held, before, group, frames, out_type, after=()):
    parts = len(held)
    dests = sorted({place for place, _ in jobs})
    _, rows_framed, columns, width = held[0].shape
    lags, taps, _, chans = weights.shape
    count = (rows_framed - 2) * columns
    operands = [weights, *[held[n] for n in dests], *before, *after]
    return pl.pallas_call(
        functools.partial(conv_kernel, tuple(jobs), parts, group, frames),
        out_shape=[jax.ShapeDtypeStruct((count, chans), out_type)] * len(jobs),
        in_specs=[pl.BlockSpec(memory_space=pltpu.SMEM)] + in_vmem(len(operands)),
        out_specs=in_vmem(len(jobs)),
        scratch_shapes=[
            pltpu.VMEM((len(dests), 2 * frames, rows_framed, columns, width), jnp.bfloat16)
        ],
        compiler_params=pltpu.CompilerParams(vmem_limit_bytes=VMEM_LIMIT),
        cost_estimate=pl.CostEstimate(
            flops=10**11, bytes_accessed=2 * taps * lags * width * chans, transcendentals=0
        ),
        name="conv_sums",
    )(meta, *operands)


def sum_call(pieces, after=()):
    def kernel(*refs):
        total = refs[0][...].astype(jnp.float32)
        for ref in refs[1 : len(pieces)]:
            total = total + ref[...].astype(jnp.float32)
        refs[-1][...] = total.astype(refs[-1].dtype)

    return pl.pallas_call(
        kernel,
        out_shape=jax.ShapeDtypeStruct(pieces[0].shape, jnp.bfloat16),
        in_specs=in_vmem(len(pieces) + len(after)),
        out_specs=pl.BlockSpec(memory_space=pltpu.VMEM),
        compiler_params=pltpu.CompilerParams(vmem_limit_bytes=VMEM_LIMIT),
        name="sum_parts",
    )(*pieces, *after)


def attend_kernel(frames, share, *refs):
    all_count = frames * share
    tokens, refs = refs[:all_count], refs[all_count:]
    (wq, wk, wv, wo), refs = refs[:4], refs[4:]
    outs, (normed, keys, values) = refs[:frames], refs[frames:]
    size, chans = normed.shape
    per_group = chans // G

    tile_row = lax.broadcasted_iota(jnp.int32, (LANES, LANES), 0) // per_group
    tile_col = lax.broadcasted_iota(jnp.int32, (LANES, LANES), 1) // per_group
    same = (tile_row == tile_col).astype(jnp.float32).astype(jnp.bfloat16)

    def group_mean(sums):
        first = sums.astype(jnp.bfloat16)
        rest = sums - first.astype(jnp.float32)
        second = rest.astype(jnp.bfloat16)
        third = rest - second.astype(jnp.float32)
        tiles = []
        for tile in range(chans // LANES):
            lanes = slice(tile * LANES, (tile + 1) * LANES)
            stacked = jnp.concatenate(
                [
                    first.astype(jnp.float32)[:, lanes],
                    second.astype(jnp.float32)[:, lanes],
                    third[:, lanes],
                ],
                axis=0,
            ).astype(jnp.bfloat16)
            spread = jnp.dot(stacked, same, preferred_element_type=jnp.float32)
            tiles.append(jnp.sum(spread, axis=0, keepdims=True))
        return jnp.concatenate(tiles, axis=1) / (size * per_group)

    def folded(x):
        return jnp.sum(x.reshape(-1, 8, chans), axis=0)

    average = group_mean(sum(folded(ref[...].astype(jnp.float32)) for ref in tokens))

    def spread_of(ref):
        centered = ref[...].astype(jnp.float32) - average
        return folded(centered * centered)

    scale = lax.rsqrt(group_mean(sum(spread_of(ref) for ref in tokens)) + epsilon)
    place = 0
    for ref in tokens:
        rows = ref.shape[0]
        normed[pl.ds(place, rows)] = (
            (ref[...].astype(jnp.float32) - average) * scale
        ).astype(jnp.bfloat16)
        place += rows

    step = min(256, size)
    for start in range(0, size, step):
        x = normed[pl.ds(start, step)]
        keys[pl.ds(start, step)] = jnp.dot(
            x, wk[...], preferred_element_type=jnp.float32
        ).astype(jnp.bfloat16)
        values[pl.ds(start, step)] = jnp.dot(
            x, wv[...], preferred_element_type=jnp.float32
        ).astype(jnp.bfloat16)

    rows = tokens[0].shape[0]
    for p, out in enumerate(outs):
        queries = jnp.dot(
            normed[pl.ds(p * rows, rows)], wq[...], preferred_element_type=jnp.float32
        ).astype(jnp.bfloat16)
        scores = lax.dot_general(
            queries, keys[...], (((1,), (1,)), ((), ())), preferred_element_type=jnp.float32
        ) * chans ** (-0.5)
        row_max = jnp.max(scores, axis=1, keepdims=True)
        exp_weights = jnp.exp(scores - row_max).astype(jnp.bfloat16)
        denominator = jnp.sum(exp_weights.astype(jnp.float32), axis=1, keepdims=True)
        numerator = jnp.dot(exp_weights, values[...], preferred_element_type=jnp.float32)
        attended = (numerator / denominator).astype(jnp.bfloat16)
        summed = tokens[p][...].astype(jnp.float32) + jnp.dot(
            attended, wo[...], preferred_element_type=jnp.float32
        )
        out[...] = summed.astype(jnp.bfloat16)


def attend_call(own, others, weights):
    frames = len(own)
    share = 1 + len(others) // len(own)
    chans = own[0].shape[1]
    size = sum(x.shape[0] for x in own) * share
    mine = size // share
    out = jax.ShapeDtypeStruct(own[0].shape, jnp.bfloat16)
    operands = [*own, *others, *weights]
    return pl.pallas_call(
        functools.partial(attend_kernel, frames, share),
        out_shape=[out] * frames,
        in_specs=in_vmem(len(operands)),
        out_specs=in_vmem(frames),
        scratch_shapes=[pltpu.VMEM((size, chans), jnp.bfloat16)] * 3,
        compiler_params=pltpu.CompilerParams(vmem_limit_bytes=VMEM_LIMIT),
        cost_estimate=pl.CostEstimate(
            flops=2 * (2 * size * chans * chans + 2 * mine * chans * (chans + size)),
            bytes_accessed=8 * chans * chans + 2 * size * chans,
            transcendentals=mine * size,
        ),
        name="attend",
    )(*operands)


def body(latents, conv_weight, query_weight, key_weight, value_weight, out_weight):
    frames, rows_here, columns, chans = latents.shape
    taps, chans_here, _ = conv_weight.shape
    devices, depth = lax.axis_size("tm"), lax.axis_size("rows")
    sizes = (devices, depth)
    group = LANES // chans_here
    parts = devices // group
    width = group * chans_here
    t_index, z_index = lax.axis_index("tm"), lax.axis_index("rows")
    part, member = t_index // group, t_index % group
    meta = jnp.stack([part, member, z_index]).astype(jnp.int32)

    def permute(block, target):
        return lax.ppermute(block, BOTH, everywhere(sizes, target))

    def to_place(place):
        return lambda t, z: ((t // group ^ partner(t % group, place)) * group + t % group, z)

    def to_member(step):
        return lambda t, z: (t // group * group + (t + step) % group, z)

    split = conv_weight.reshape(taps // 3, 3, chans_here, chans)
    slices = [split] + [permute(split, to_member(step)) for step in range(1, group)]
    weights = merge_call(meta, slices)

    above = permute(latents[:, -1], lambda t, z: (t, z + 1) if z + 1 < depth else None)
    below = permute(latents[:, 0], lambda t, z: (t, z - 1) if z else None)

    above, weights = lax.optimization_barrier((above, weights))
    held = frame_call(meta, latents, above, below, parts)
    held = [permute(x, to_place(place)) if place else x for place, x in enumerate(held)]
    before = [permute(x, to_member(1)) for x in held]

    conv = functools.partial(
        conv_call,
        meta=meta,
        weights=weights,
        held=held,
        before=before,
        group=group,
        frames=frames,
    )

    sent, got = [], []
    for p in range(frames):
        sent.append(
            conv([(3, p), (1, p)], out_type=jnp.bfloat16, after=sent[-1][:1] if sent else ())
        )
        got.append([permute(x, to_place(1)) for x in sent[p]])
    token = sent[-1][0]
    kept, relays = [], []
    for p in range(frames):
        on, own_part = conv([(2, p), (0, p)], out_type=jnp.float32, after=(token,))
        token = sum_call([on, got[p][0]], after=got[p][1:])
        kept.append(own_part)
        relays.append(permute(token, to_place(2)))
    sums = [sum_call([kept[p], got[p][1], relays[p]]) for p in range(frames)]

    share = depth // frames

    def frame_home(t, z, p):
        frame = t % CORES * frames + (z + p) % frames
        slot = frame * share + z // frames
        return (t // CORES * CORES + slot % CORES, slot // CORES)

    def next_in_frame(t, z, step):
        slot = z * CORES + t % CORES
        slot = slot // share * share + (slot + step) % share
        return (t // CORES * CORES + slot % CORES, slot // CORES)

    own = [permute(x, lambda t, z: frame_home(t, z, p)) for p, x in enumerate(sums)]
    others = []
    for step in range(1, share):
        others += [permute(x, lambda t, z: next_in_frame(t, z, step)) for x in own]

    done = attend_call(own, others, (query_weight, key_weight, value_weight, out_weight))
    done = [x.reshape(rows_here, columns, chans) for x in done]
    back = []
    for p in range(frames):
        pairs = [(b, a) for a, b in everywhere(sizes, lambda t, z: frame_home(t, z, p))]
        back.append(lax.ppermute(done[p], BOTH, pairs))
    return jnp.stack(
        [
            functools.reduce(
                lambda rest, p: jnp.where((z_index + p) % frames == f, back[p], rest),
                range(1, frames),
                back[0],
            )
            for f in range(frames)
        ]
    )


def solution(mesh):
    placed = (P("tm", "rows", None, None), P(None, "tm", None), P(), P(), P(), P())
    return jax.shard_map(
        body, mesh=mesh, in_specs=placed, out_specs=P("tm", "rows", None, None), check_vma=False
    )
```

```python
import functools

import jax
import jax.numpy as jnp
from jax import lax
from jax.experimental import pallas as pl
from jax.experimental.pallas import tpu as pltpu
from jax.sharding import PartitionSpec as P

G = 32
LANES = 128
CORES = 2

epsilon = 1e-06

BOTH = ("tm", "rows")
VMEM_LIMIT = 16 * 1024 * 1024


def everywhere(sizes, target):
    devices, depth = sizes
    pairs = []
    for t in range(devices):
        for z in range(depth):
            to = target(t, z)
            if to is not None:
                pairs.append((t * depth + z, to[0] * depth + to[1]))
    return pairs


def in_vmem(count):
    return [pl.BlockSpec(memory_space=pltpu.VMEM)] * count


def merge_kernel(group, *refs):
    meta, refs = refs[0], refs[1:]
    slices, out, sems = refs[:group], refs[group], refs[group + 1]
    chans_here = slices[0].shape[2]
    copies = []
    for lag in range(out.shape[0]):
        for step in range(group):
            owner = lax.rem(meta[1] - step + group, group)
            rows = pl.ds(pl.multiple_of(owner * chans_here, 16), chans_here)
            copies.append(
                pltpu.make_async_copy(
                    slices[step].at[:, lag], out.at[lag, :, rows], sems.at[lag, step]
                )
            )
    for copy in copies:
        copy.start()
    for copy in copies:
        copy.wait()


def merge_call(meta, slices):
    group = len(slices)
    taps, lags, chans_here, chans = slices[0].shape
    return pl.pallas_call(
        functools.partial(merge_kernel, group),
        out_shape=jax.ShapeDtypeStruct((lags, taps, group * chans_here, chans), jnp.bfloat16),
        in_specs=[pl.BlockSpec(memory_space=pltpu.SMEM)]
        + [pl.BlockSpec(memory_space=pltpu.HBM)]
        + [pl.BlockSpec(memory_space=pl.ANY)] * (group - 1),
        out_specs=pl.BlockSpec(memory_space=pltpu.VMEM),
        scratch_shapes=[pltpu.SemaphoreType.DMA((lags, group))],
        compiler_params=pltpu.CompilerParams(vmem_limit_bytes=VMEM_LIMIT),
        name="merge_kernel_slices",
    )(meta, *slices)


def partner(member, place):
    odd = member % 2 == 1
    if isinstance(member, int) and isinstance(place, int):
        return 3 - place if odd and place in (1, 2) else place
    swapped = jnp.where(jnp.logical_or(place == 1, place == 2), 3 - place, place)
    return jnp.where(odd, swapped, place)


def frame_call(meta, latents, above, below, parts):
    frames, rows_here, columns, chans = latents.shape
    width = chans // parts

    def kernel(meta, latents, above, below, *outs):
        for place, out in enumerate(outs):
            to = lax.bitwise_xor(meta[0], partner(meta[1], jnp.int32(place)))
            lanes = pl.ds(pl.multiple_of(to * width, width), width)
            out[:, 0] = above[:, :, lanes]
            out[:, 1 : 1 + rows_here] = latents[:, :, :, lanes]
            out[:, 1 + rows_here] = below[:, :, lanes]

    return pl.pallas_call(
        kernel,
        out_shape=[
            jax.ShapeDtypeStruct((frames, rows_here + 2, columns, width), latents.dtype)
        ]
        * parts,
        in_specs=[pl.BlockSpec(memory_space=pltpu.SMEM)] + in_vmem(3),
        out_specs=in_vmem(parts),
        compiler_params=pltpu.CompilerParams(vmem_limit_bytes=VMEM_LIMIT),
        name="frame_parts",
    )(meta, latents, above, below)


def conv_kernel(jobs, parts, group, frames, *refs):
    meta, weights, refs = refs[0], refs[1], refs[2:]
    dests = sorted({place for place, _ in jobs})
    held, refs = refs[: len(dests)], refs[len(dests) :]
    before, refs = refs[:parts], refs[parts:]
    outs, raw = refs[-1 - len(jobs) : -1], refs[-1]
    part, member, z = meta[0], meta[1], meta[2]
    lags, _, width, chans = weights.shape
    _, rows_framed, columns, _ = held[0].shape
    rows_here = rows_framed - 2

    first = member == 0
    for n, where in enumerate(dests):
        to = lax.bitwise_xor(part, partner(member, jnp.int32(where)))
        valid = jnp.logical_or(jnp.logical_not(first), to > 0)
        sender = jnp.where(first, group - 1, member - 1)
        want = jnp.where(first, jnp.maximum(to - 1, 0), to)
        place = partner(sender, lax.bitwise_xor(part, want))
        raw[n, frames:] = held[n][...]
        for i in range(parts):

            @pl.when(place == i)
            def _():
                raw[n, :frames] = before[i][...]

        @pl.when(jnp.logical_not(valid))
        def _():
            raw[n, :frames] = jnp.zeros_like(raw[n, :frames])

    side = 3

    def patches(a, b):
        pieces = []
        for where, p in jobs:
            f = lax.rem(z + p, frames) + a
            pieces.append(raw[dests.index(where), f, b : b + rows_here].reshape(-1, width))
        return jnp.concatenate(pieces, axis=0)

    lhs = jnp.concatenate([patches(a, b) for a in range(side) for b in range(side)], axis=1)
    count = lhs.shape[0]
    column = lax.broadcasted_iota(jnp.int32, (count, chans), 0) % columns
    total = None
    for lag in (1, 0, 2):
        product = jnp.dot(
            lhs, weights[lag].reshape(-1, chans), preferred_element_type=jnp.float32
        )
        if lag == 1:
            total = product
        elif lag == 0:
            total = total + jnp.where(column == 0, 0.0, pltpu.roll(product, 1, 0))
        else:
            moved = pltpu.roll(product, count - 1, 0)
            total = total + jnp.where(column == columns - 1, 0.0, moved)
    size = rows_here * columns
    for n, out in enumerate(outs):
        out[...] = total[n * size : (n + 1) * size].astype(out.dtype)


def conv_call(jobs, meta, weights, held, before, group, frames, out_type, after=()):
    parts = len(held)
    dests = sorted({place for place, _ in jobs})
    _, rows_framed, columns, width = held[0].shape
    lags, taps, _, chans = weights.shape
    count = (rows_framed - 2) * columns
    operands = [weights, *[held[n] for n in dests], *before, *after]
    return pl.pallas_call(
        functools.partial(conv_kernel, tuple(jobs), parts, group, frames),
        out_shape=[jax.ShapeDtypeStruct((count, chans), out_type)] * len(jobs),
        in_specs=[pl.BlockSpec(memory_space=pltpu.SMEM)] + in_vmem(len(operands)),
        out_specs=in_vmem(len(jobs)),
        scratch_shapes=[
            pltpu.VMEM((len(dests), 2 * frames, rows_framed, columns, width), jnp.bfloat16)
        ],
        compiler_params=pltpu.CompilerParams(vmem_limit_bytes=VMEM_LIMIT),
        cost_estimate=pl.CostEstimate(
            flops=2 * len(jobs) * count * taps * lags * width * chans,
            bytes_accessed=2 * taps * lags * width * chans,
            transcendentals=0,
        ),
        name="conv_sums",
    )(meta, *operands)


def sum_call(pieces, after=()):
    def kernel(*refs):
        total = refs[0][...].astype(jnp.float32)
        for ref in refs[1 : len(pieces)]:
            total = total + ref[...].astype(jnp.float32)
        refs[-1][...] = total.astype(refs[-1].dtype)

    return pl.pallas_call(
        kernel,
        out_shape=jax.ShapeDtypeStruct(pieces[0].shape, jnp.bfloat16),
        in_specs=in_vmem(len(pieces) + len(after)),
        out_specs=pl.BlockSpec(memory_space=pltpu.VMEM),
        compiler_params=pltpu.CompilerParams(vmem_limit_bytes=VMEM_LIMIT),
        name="sum_parts",
    )(*pieces, *after)


def attend_kernel(frames, share, *refs):
    all_count = frames * share
    tokens, refs = refs[:all_count], refs[all_count:]
    (wq, wk, wv, wo), refs = refs[:4], refs[4:]
    outs, (normed, keys, values) = refs[:frames], refs[frames:]
    size, chans = normed.shape
    per_group = chans // G

    tile_row = lax.broadcasted_iota(jnp.int32, (LANES, LANES), 0) // per_group
    tile_col = lax.broadcasted_iota(jnp.int32, (LANES, LANES), 1) // per_group
    same = (tile_row == tile_col).astype(jnp.float32).astype(jnp.bfloat16)

    def group_mean(sums):
        first = sums.astype(jnp.bfloat16)
        rest = sums - first.astype(jnp.float32)
        second = rest.astype(jnp.bfloat16)
        third = rest - second.astype(jnp.float32)
        tiles = []
        for tile in range(chans // LANES):
            lanes = slice(tile * LANES, (tile + 1) * LANES)
            stacked = jnp.concatenate(
                [
                    first.astype(jnp.float32)[:, lanes],
                    second.astype(jnp.float32)[:, lanes],
                    third[:, lanes],
                ],
                axis=0,
            ).astype(jnp.bfloat16)
            spread = jnp.dot(stacked, same, preferred_element_type=jnp.float32)
            tiles.append(jnp.sum(spread, axis=0, keepdims=True))
        return jnp.concatenate(tiles, axis=1) / (size * per_group)

    def folded(x):
        return jnp.sum(x.reshape(-1, 8, chans), axis=0)

    average = group_mean(sum(folded(ref[...].astype(jnp.float32)) for ref in tokens))

    def spread_of(ref):
        centered = ref[...].astype(jnp.float32) - average
        return folded(centered * centered)

    scale = lax.rsqrt(group_mean(sum(spread_of(ref) for ref in tokens)) + epsilon)
    place = 0
    for ref in tokens:
        rows = ref.shape[0]
        normed[pl.ds(place, rows)] = (
            (ref[...].astype(jnp.float32) - average) * scale
        ).astype(jnp.bfloat16)
        place += rows

    step = min(256, size)
    for start in range(0, size, step):
        x = normed[pl.ds(start, step)]
        keys[pl.ds(start, step)] = jnp.dot(
            x, wk[...], preferred_element_type=jnp.float32
        ).astype(jnp.bfloat16)
        values[pl.ds(start, step)] = jnp.dot(
            x, wv[...], preferred_element_type=jnp.float32
        ).astype(jnp.bfloat16)

    rows = tokens[0].shape[0]
    for p, out in enumerate(outs):
        queries = jnp.dot(
            normed[pl.ds(p * rows, rows)], wq[...], preferred_element_type=jnp.float32
        ).astype(jnp.bfloat16)
        scores = lax.dot_general(
            queries, keys[...], (((1,), (1,)), ((), ())), preferred_element_type=jnp.float32
        ) * chans ** (-0.5)
        row_max = jnp.max(scores, axis=1, keepdims=True)
        exp_weights = jnp.exp(scores - row_max).astype(jnp.bfloat16)
        denominator = jnp.sum(exp_weights.astype(jnp.float32), axis=1, keepdims=True)
        numerator = jnp.dot(exp_weights, values[...], preferred_element_type=jnp.float32)
        attended = (numerator / denominator).astype(jnp.bfloat16)
        summed = tokens[p][...].astype(jnp.float32) + jnp.dot(
            attended, wo[...], preferred_element_type=jnp.float32
        )
        out[...] = summed.astype(jnp.bfloat16)


def attend_call(own, others, weights):
    frames = len(own)
    share = 1 + len(others) // len(own)
    chans = own[0].shape[1]
    size = sum(x.shape[0] for x in own) * share
    mine = size // share
    out = jax.ShapeDtypeStruct(own[0].shape, jnp.bfloat16)
    operands = [*own, *others, *weights]
    return pl.pallas_call(
        functools.partial(attend_kernel, frames, share),
        out_shape=[out] * frames,
        in_specs=in_vmem(len(operands)),
        out_specs=in_vmem(frames),
        scratch_shapes=[pltpu.VMEM((size, chans), jnp.bfloat16)] * 3,
        compiler_params=pltpu.CompilerParams(vmem_limit_bytes=VMEM_LIMIT),
        cost_estimate=pl.CostEstimate(
            flops=2 * (2 * size * chans * chans + 2 * mine * chans * (chans + size)),
            bytes_accessed=8 * chans * chans + 2 * size * chans,
            transcendentals=mine * size,
        ),
        name="attend",
    )(*operands)


def body(latents, conv_weight, query_weight, key_weight, value_weight, out_weight):
    frames, rows_here, columns, chans = latents.shape
    taps, chans_here, _ = conv_weight.shape
    devices, depth = lax.axis_size("tm"), lax.axis_size("rows")
    sizes = (devices, depth)
    group = LANES // chans_here
    parts = devices // group
    width = group * chans_here
    t_index, z_index = lax.axis_index("tm"), lax.axis_index("rows")
    part, member = t_index // group, t_index % group
    meta = jnp.stack([part, member, z_index]).astype(jnp.int32)

    def permute(block, target):
        return lax.ppermute(block, BOTH, everywhere(sizes, target))

    def to_place(place):
        return lambda t, z: ((t // group ^ partner(t % group, place)) * group + t % group, z)

    def to_member(step):
        return lambda t, z: (t // group * group + (t + step) % group, z)

    split = conv_weight.reshape(taps // 3, 3, chans_here, chans)
    slices = [split] + [permute(split, to_member(step)) for step in range(1, group)]
    weights = merge_call(meta, slices)

    above = permute(latents[:, -1], lambda t, z: (t, z + 1) if z + 1 < depth else None)
    below = permute(latents[:, 0], lambda t, z: (t, z - 1) if z else None)

    above, weights = lax.optimization_barrier((above, weights))
    held = frame_call(meta, latents, above, below, parts)
    held = [permute(x, to_place(place)) if place else x for place, x in enumerate(held)]
    before = [permute(x, to_member(1)) for x in held]

    conv = functools.partial(
        conv_call,
        meta=meta,
        weights=weights,
        held=held,
        before=before,
        group=group,
        frames=frames,
    )

    sent, got = [], []
    for p in range(frames):
        sent.append(
            conv([(3, p), (1, p)], out_type=jnp.bfloat16, after=sent[-1][:1] if sent else ())
        )
        got.append([permute(x, to_place(1)) for x in sent[p]])
    token = sent[-1][0]
    kept, relays = [], []
    for p in range(frames):
        on, own_part = conv([(2, p), (0, p)], out_type=jnp.float32, after=(token,))
        token = sum_call([on, got[p][0]], after=got[p][1:])
        kept.append(own_part)
        relays.append(permute(token, to_place(2)))
    sums = [sum_call([kept[p], got[p][1], relays[p]]) for p in range(frames)]

    share = depth // frames

    def frame_home(t, z, p):
        frame = t % CORES * frames + (z + p) % frames
        slot = frame * share + z // frames
        return (t // CORES * CORES + slot % CORES, slot // CORES)

    def next_in_frame(t, z, step):
        slot = z * CORES + t % CORES
        slot = slot // share * share + (slot + step) % share
        return (t // CORES * CORES + slot % CORES, slot // CORES)

    own = [permute(x, lambda t, z: frame_home(t, z, p)) for p, x in enumerate(sums)]
    others = []
    for step in range(1, share):
        others += [permute(x, lambda t, z: next_in_frame(t, z, step)) for x in own]

    done = attend_call(own, others, (query_weight, key_weight, value_weight, out_weight))
    done = [x.reshape(rows_here, columns, chans) for x in done]
    back = []
    for p in range(frames):
        pairs = [(b, a) for a, b in everywhere(sizes, lambda t, z: frame_home(t, z, p))]
        back.append(lax.ppermute(done[p], BOTH, pairs))
    return jnp.stack(
        [
            functools.reduce(
                lambda rest, p: jnp.where((z_index + p) % frames == f, back[p], rest),
                range(1, frames),
                back[0],
            )
            for f in range(frames)
        ]
    )


def solution(mesh):
    placed = (P("tm", "rows", None, None), P(None, "tm", None), P(), P(), P(), P())
    return jax.shard_map(
        body, mesh=mesh, in_specs=placed, out_specs=P("tm", "rows", None, None), check_vma=False
    )
```

```python
import functools

import jax
import jax.numpy as jnp
from jax import lax
from jax.experimental import pallas as pl
from jax.experimental.pallas import tpu as pltpu
from jax.sharding import PartitionSpec as P

G = 32
LANES = 128
CORES = 2

epsilon = 1e-06

BOTH = ("tm", "rows")
VMEM_LIMIT = 32 * 1024 * 1024


def everywhere(sizes, target):
    devices, depth = sizes
    pairs = []
    for t in range(devices):
        for z in range(depth):
            to = target(t, z)
            if to is not None:
                pairs.append((t * depth + z, to[0] * depth + to[1]))
    return pairs


def in_vmem(count):
    return [pl.BlockSpec(memory_space=pltpu.VMEM)] * count


def merge_kernel(group, *refs):
    meta, refs = refs[0], refs[1:]
    slices, out, sems = refs[:group], refs[group], refs[group + 1]
    chans_here = slices[0].shape[2]
    copies = []
    for lag in range(out.shape[0]):
        for step in range(group):
            owner = lax.rem(meta[1] - step + group, group)
            rows = pl.ds(pl.multiple_of(owner * chans_here, 16), chans_here)
            copies.append(
                pltpu.make_async_copy(
                    slices[step].at[:, lag], out.at[lag, :, rows], sems.at[lag, step]
                )
            )
    for copy in copies:
        copy.start()
    for copy in copies:
        copy.wait()


def merge_call(meta, slices):
    group = len(slices)
    taps, lags, chans_here, chans = slices[0].shape
    return pl.pallas_call(
        functools.partial(merge_kernel, group),
        out_shape=jax.ShapeDtypeStruct((lags, taps, group * chans_here, chans), jnp.bfloat16),
        in_specs=[pl.BlockSpec(memory_space=pltpu.SMEM)]
        + [pl.BlockSpec(memory_space=pl.ANY)] * group,
        out_specs=pl.BlockSpec(memory_space=pltpu.VMEM),
        scratch_shapes=[pltpu.SemaphoreType.DMA((lags, group))],
        compiler_params=pltpu.CompilerParams(vmem_limit_bytes=VMEM_LIMIT),
        name="merge_kernel_slices",
    )(meta, *slices)


def halo_call(pieces, after):
    frames, rows_here, columns, width = pieces[0].shape
    out = jax.ShapeDtypeStruct((len(pieces), frames, columns, width), jnp.bfloat16)

    def kernel(*refs):
        first, last = refs[-2:]
        for i in range(len(pieces)):
            first[i] = refs[i][:, 0]
            last[i] = refs[i][:, rows_here - 1]

    return pl.pallas_call(
        kernel,
        out_shape=[out] * 2,
        in_specs=in_vmem(len(pieces) + 1),
        out_specs=in_vmem(2),
        compiler_params=pltpu.CompilerParams(vmem_limit_bytes=VMEM_LIMIT),
        name="halo_rows",
    )(*pieces, after)


def conv_kernel(jobs, parts, frames, *refs):
    meta, weights, refs = refs[0], refs[1], refs[2:]
    dests = sorted({s for s, _ in jobs})
    any_rim = any(rim for _, rim in jobs)
    held, refs = refs[: len(dests)], refs[len(dests) :]
    before, refs = refs[:parts], refs[parts:]
    if any_rim:
        (above, below), refs = refs[:2], refs[2:]
    outs, raw = refs[-1 - len(jobs) : -1], refs[-1]
    part, member, z = meta[0], meta[1], meta[2]
    lags, _, width, chans = weights.shape
    _, rows_here, columns, _ = held[0].shape

    for n, s in enumerate(dests):
        to = lax.bitwise_xor(part, s)
        wraps = member == 0
        place = jnp.where(wraps, lax.bitwise_xor(part, jnp.maximum(to - 1, 0)), s)
        valid = jnp.logical_or(jnp.logical_not(wraps), to > 0)
        raw[n, frames:, 1 : 1 + rows_here] = held[n][...]
        if any_rim:
            raw[n, frames:, 0] = above[s]
            raw[n, frames:, 1 + rows_here] = below[s]
            raw[n, :frames, 0] = above[parts + place]
            raw[n, :frames, 1 + rows_here] = below[parts + place]
        for i in range(parts):

            @pl.when(place == i)
            def _():
                raw[n, :frames, 1 : 1 + rows_here] = before[i][...]

        @pl.when(jnp.logical_not(valid))
        def _():
            raw[n, :frames] = jnp.zeros_like(raw[n, :frames])

    side = 3

    def patches(a, b):
        pieces = []
        for s, rim in jobs:
            n = dests.index(s)
            for p in range(frames):
                f = lax.rem(z + p, frames) + a
                if rim:
                    pieces.append(raw[n, f, b])
                    pieces.append(raw[n, f, rows_here - 1 + b])
                else:
                    pieces.append(raw[n, f, 1 + b : b + rows_here - 1].reshape(-1, width))
        return jnp.concatenate(pieces, axis=0)

    lhs = jnp.concatenate([patches(a, b) for a in range(side) for b in range(side)], axis=1)
    count = lhs.shape[0]
    column = lax.broadcasted_iota(jnp.int32, (count, chans), 0) % columns
    total = None
    for lag in (1, 0, 2):
        product = jnp.dot(
            lhs, weights[lag].reshape(-1, chans), preferred_element_type=jnp.float32
        )
        if lag == 1:
            total = product
        elif lag == 0:
            total = total + jnp.where(column == 0, 0.0, pltpu.roll(product, 1, 0))
        else:
            moved = pltpu.roll(product, count - 1, 0)
            total = total + jnp.where(column == columns - 1, 0.0, moved)
    place = 0
    for out in outs:
        out[...] = total[place : place + out.shape[0]].astype(out.dtype)
        place += out.shape[0]


def conv_call(jobs, meta, weights, held, before, halos, frames, out_type, after=()):
    parts = len(held)
    dests = sorted({s for s, _ in jobs})
    _, rows_here, columns, width = held[0].shape
    lags, taps, _, chans = weights.shape
    any_rim = any(rim for _, rim in jobs)
    counts = [frames * (2 if rim else rows_here - 2) * columns for _, rim in jobs]
    operands = [weights, *[held[s] for s in dests], *before, *(halos if any_rim else ())]
    specs = [pl.BlockSpec(memory_space=pltpu.SMEM)] + in_vmem(len(operands))
    specs += in_vmem(len(after))
    return pl.pallas_call(
        functools.partial(conv_kernel, tuple(jobs), parts, frames),
        out_shape=[jax.ShapeDtypeStruct((count, chans), out_type) for count in counts],
        in_specs=specs,
        out_specs=in_vmem(len(jobs)),
        scratch_shapes=[
            pltpu.VMEM((len(dests), 2 * frames, rows_here + 2, columns, width), jnp.bfloat16)
        ],
        compiler_params=pltpu.CompilerParams(vmem_limit_bytes=VMEM_LIMIT),
        cost_estimate=pl.CostEstimate(
            flops=20 * sum(counts) * taps * lags * width * chans,
            bytes_accessed=2 * taps * lags * width * chans,
            transcendentals=0,
        ),
        name="conv_rim" if any_rim else "conv_inner",
    )(meta, *operands, *after)


def sum_call(pieces, splits, after=()):
    count, chans = pieces[0].shape
    size = count // splits

    def kernel(*refs):
        for p, out_ref in enumerate(refs[len(refs) - splits :]):
            total = None
            for ref in refs[: len(pieces)]:
                rows = ref[p * size : (p + 1) * size].astype(jnp.float32)
                total = rows if total is None else total + rows
            out_ref[...] = total.astype(out_ref.dtype)

    return pl.pallas_call(
        kernel,
        out_shape=[jax.ShapeDtypeStruct((size, chans), jnp.bfloat16)] * splits,
        in_specs=in_vmem(len(pieces) + len(after)),
        out_specs=in_vmem(splits),
        compiler_params=pltpu.CompilerParams(vmem_limit_bytes=VMEM_LIMIT),
        name="sum_parts",
    )(*pieces, *after)


def attend_kernel(frames, share, chunks, *refs):
    own_count = frames * chunks
    all_count = own_count * share
    tokens, refs = refs[:all_count], refs[all_count:]
    (wq, wk, wv, wo), refs = refs[:4], refs[4:]
    outs, (normed, keys, values) = refs[:frames], refs[frames:]
    size, chans = normed.shape
    per_group = chans // G

    tile_row = lax.broadcasted_iota(jnp.int32, (LANES, LANES), 0) // per_group
    tile_col = lax.broadcasted_iota(jnp.int32, (LANES, LANES), 1) // per_group
    same = (tile_row == tile_col).astype(jnp.float32).astype(jnp.bfloat16)

    def group_mean(sums):
        first = sums.astype(jnp.bfloat16)
        rest = sums - first.astype(jnp.float32)
        second = rest.astype(jnp.bfloat16)
        third = rest - second.astype(jnp.float32)
        tiles = []
        for tile in range(chans // LANES):
            lanes = slice(tile * LANES, (tile + 1) * LANES)
            stacked = jnp.concatenate(
                [
                    first.astype(jnp.float32)[:, lanes],
                    second.astype(jnp.float32)[:, lanes],
                    third[:, lanes],
                ],
                axis=0,
            ).astype(jnp.bfloat16)
            spread = jnp.dot(stacked, same, preferred_element_type=jnp.float32)
            tiles.append(jnp.sum(spread, axis=0, keepdims=True))
        return jnp.concatenate(tiles, axis=1) / (size * per_group)

    def folded(x):
        return jnp.sum(x.reshape(-1, 8, chans), axis=0)

    average = group_mean(sum(folded(ref[...].astype(jnp.float32)) for ref in tokens))

    def spread_of(ref):
        centered = ref[...].astype(jnp.float32) - average
        return folded(centered * centered)

    scale = lax.rsqrt(group_mean(sum(spread_of(ref) for ref in tokens)) + epsilon)
    place = 0
    for ref in tokens:
        rows = ref.shape[0]
        normed[pl.ds(place, rows)] = (
            (ref[...].astype(jnp.float32) - average) * scale
        ).astype(jnp.bfloat16)
        place += rows

    step = min(256, size)
    for start in range(0, size, step):
        x = normed[pl.ds(start, step)]
        keys[pl.ds(start, step)] = jnp.dot(
            x, wk[...], preferred_element_type=jnp.float32
        ).astype(jnp.bfloat16)
        values[pl.ds(start, step)] = jnp.dot(
            x, wv[...], preferred_element_type=jnp.float32
        ).astype(jnp.bfloat16)

    place = 0
    for p, out in enumerate(outs):
        mine = tokens[p * chunks : (p + 1) * chunks]
        rows = sum(ref.shape[0] for ref in mine)
        queries = jnp.dot(
            normed[pl.ds(place, rows)], wq[...], preferred_element_type=jnp.float32
        ).astype(jnp.bfloat16)
        place += rows
        scores = lax.dot_general(
            queries, keys[...], (((1,), (1,)), ((), ())), preferred_element_type=jnp.float32
        ) * chans ** (-0.5)
        row_max = jnp.max(scores, axis=1, keepdims=True)
        exp_weights = jnp.exp(scores - row_max).astype(jnp.bfloat16)
        denominator = jnp.sum(exp_weights.astype(jnp.float32), axis=1, keepdims=True)
        numerator = jnp.dot(exp_weights, values[...], preferred_element_type=jnp.float32)
        attended = (numerator / denominator).astype(jnp.bfloat16)
        added = jnp.dot(attended, wo[...], preferred_element_type=jnp.float32)
        rows_here, columns, _ = out.shape
        inner = mine[0].shape[0]
        first = mine[0][...].astype(jnp.float32) + added[:inner]
        out[1 : rows_here - 1] = first.astype(jnp.bfloat16).reshape(rows_here - 2, columns, chans)
        second = (mine[1][...].astype(jnp.float32) + added[inner:]).astype(jnp.bfloat16)
        out[0] = second[:columns]
        out[rows_here - 1] = second[columns:]


def attend_call(own, others, weights, frames, rows_here, columns):
    chunks = len(own) // frames
    share = 1 + len(others) // len(own)
    chans = own[0].shape[1]
    size = sum(x.shape[0] for x in own) * share
    mine = size // share
    out = jax.ShapeDtypeStruct((rows_here, columns, chans), jnp.bfloat16)
    operands = [*own, *others, *weights]
    return pl.pallas_call(
        functools.partial(attend_kernel, frames, share, chunks),
        out_shape=[out] * frames,
        in_specs=in_vmem(len(operands)),
        out_specs=in_vmem(frames),
        scratch_shapes=[pltpu.VMEM((size, chans), jnp.bfloat16)] * 3,
        compiler_params=pltpu.CompilerParams(vmem_limit_bytes=VMEM_LIMIT),
        cost_estimate=pl.CostEstimate(
            flops=2 * (2 * size * chans * chans + 2 * mine * chans * (chans + size)),
            bytes_accessed=8 * chans * chans + 2 * size * chans,
            transcendentals=mine * size,
        ),
        name="attend",
    )(*operands)


def body(latents, conv_weight, query_weight, key_weight, value_weight, out_weight):
    frames, rows_here, columns, chans = latents.shape
    taps, chans_here, _ = conv_weight.shape
    devices, depth = lax.axis_size("tm"), lax.axis_size("rows")
    sizes = (devices, depth)
    group = LANES // chans_here
    parts = devices // group
    width = group * chans_here
    t_index, z_index = lax.axis_index("tm"), lax.axis_index("rows")
    part, member = t_index // group, t_index % group
    meta = jnp.stack([part, member, z_index]).astype(jnp.int32)

    def permute(block, target):
        return lax.ppermute(block, BOTH, everywhere(sizes, target))

    def to_part(s):
        return lambda t, z: ((t // group ^ s) * group + t % group, z)

    def to_member(step):
        return lambda t, z: (t // group * group + (t + step) % group, z)

    held, before = [None] * parts, [None] * parts
    for s in reversed(range(parts)):
        piece = lax.dynamic_slice_in_dim(latents, (part ^ s) * width, width, axis=3)
        held[s] = permute(piece, to_part(s)) if s else piece
    for s in range(parts):
        before[s] = permute(held[s], to_member(1))

    split = conv_weight.reshape(taps // 3, 3, chans_here, chans)
    slices = [split] + [permute(split, to_member(step)) for step in range(1, group)]
    weights = merge_call(meta, slices)

    away = list(reversed(range(1, parts)))
    conv = functools.partial(
        conv_call, meta=meta, weights=weights, held=held, before=before, frames=frames
    )
    inner = conv([(s, False) for s in away[:1]], halos=None, out_type=jnp.bfloat16)
    inner += conv(
        [(s, False) for s in away[1:]], halos=None, out_type=jnp.bfloat16, after=inner[:1]
    )
    first, last = halo_call([*held, *before], inner[-1])
    halos = (
        permute(last, lambda t, z: (t, z + 1) if z + 1 < depth else None),
        permute(first, lambda t, z: (t, z - 1) if z else None),
    )
    inner_own = conv([(0, False)], halos=None, out_type=jnp.float32, after=(first,))
    rim = conv([(s, True) for s in away], halos=halos, out_type=jnp.bfloat16, after=inner_own)
    rim_own = conv([(0, True)], halos=halos, out_type=jnp.float32, after=rim[-1:])
    sums = []
    for sent, own_part in ((inner, inner_own), (rim, rim_own)):
        got = [permute(x, to_part(s)) for s, x in zip(away, sent)]
        sums.append(sum_call([*own_part, *got], frames, after=rim_own))

    share = depth // frames

    def frame_home(t, z, p):
        frame = t % CORES * frames + (z + p) % frames
        slot = frame * share + z // frames
        return (t // CORES * CORES + slot % CORES, slot // CORES)

    def next_in_frame(t, z, step):
        slot = z * CORES + t % CORES
        slot = slot // share * share + (slot + step) % share
        return (t // CORES * CORES + slot % CORES, slot // CORES)

    own = []
    for p in range(frames):
        for chunk in sums:
            own.append(permute(chunk[p], lambda t, z: frame_home(t, z, p)))
    others = []
    for step in range(1, share):
        others += [permute(x, lambda t, z: next_in_frame(t, z, step)) for x in own]

    done = attend_call(
        own,
        others,
        (query_weight, key_weight, value_weight, out_weight),
        frames,
        rows_here,
        columns,
    )
    back = []
    for p in range(frames):
        pairs = [(b, a) for a, b in everywhere(sizes, lambda t, z: frame_home(t, z, p))]
        back.append(lax.ppermute(done[p], BOTH, pairs))
    return jnp.stack(
        [
            functools.reduce(
                lambda rest, p: jnp.where((z_index + p) % frames == f, back[p], rest),
                range(1, frames),
                back[0],
            )
            for f in range(frames)
        ]
    )


def solution(mesh):
    placed = (P("tm", "rows", None, None), P(None, "tm", None), P(), P(), P(), P())
    return jax.shard_map(
        body, mesh=mesh, in_specs=placed, out_specs=P("tm", "rows", None, None), check_vma=False
    )
```

```python
import functools

import jax
import jax.numpy as jnp
from jax import lax
from jax.experimental import pallas as pl
from jax.experimental.pallas import tpu as pltpu
from jax.sharding import PartitionSpec as P

G = 32
LANES = 128
CORES = 2

epsilon = 1e-06

BOTH = ("tm", "rows")
VMEM_LIMIT = 32 * 1024 * 1024


def everywhere(sizes, target):
    devices, depth = sizes
    pairs = []
    for t in range(devices):
        for z in range(depth):
            to = target(t, z)
            if to is not None:
                pairs.append((t * depth + z, to[0] * depth + to[1]))
    return pairs


def in_vmem(count):
    return [pl.BlockSpec(memory_space=pltpu.VMEM)] * count


def merge_kernel(group, *refs):
    meta, refs = refs[0], refs[1:]
    slices, out, sems = refs[:group], refs[group], refs[group + 1]
    chans_here = slices[0].shape[2]
    copies = []
    for lag in range(out.shape[0]):
        for step in range(group):
            owner = lax.rem(meta[1] - step + group, group)
            rows = pl.ds(pl.multiple_of(owner * chans_here, 16), chans_here)
            copies.append(
                pltpu.make_async_copy(
                    slices[step].at[:, lag], out.at[lag, :, rows], sems.at[lag, step]
                )
            )
    for copy in copies:
        copy.start()
    for copy in copies:
        copy.wait()


def merge_call(meta, slices):
    group = len(slices)
    taps, lags, chans_here, chans = slices[0].shape
    return pl.pallas_call(
        functools.partial(merge_kernel, group),
        out_shape=jax.ShapeDtypeStruct((lags, taps, group * chans_here, chans), jnp.bfloat16),
        in_specs=[pl.BlockSpec(memory_space=pltpu.SMEM)]
        + [pl.BlockSpec(memory_space=pl.ANY)] * group,
        out_specs=pl.BlockSpec(memory_space=pltpu.VMEM),
        scratch_shapes=[pltpu.SemaphoreType.DMA((lags, group))],
        compiler_params=pltpu.CompilerParams(vmem_limit_bytes=VMEM_LIMIT),
        name="merge_kernel_slices",
    )(meta, *slices)


def conv_kernel(jobs, any_rim, frames, *refs):
    meta, weights, held, before, refs = refs[0], refs[1], refs[2], refs[3], refs[4:]
    dests = sorted({s for s, _ in jobs})
    if any_rim:
        (rims, rims_before), refs = refs[:2], refs[2:]
    outs, raw = refs[-1 - len(jobs) : -1], refs[-1]
    part, member, z = meta[0], meta[1], meta[2]
    lags, _, width, chans = weights.shape
    _, _, rows_here, columns, _ = held.shape

    for n, s in enumerate(dests):
        to = lax.bitwise_xor(part, s)
        first = member == 0
        want = jnp.where(first, jnp.maximum(to - 1, 0), to)
        raw[n, frames:, 1 : 1 + rows_here] = held[to]
        raw[n, :frames, 1 : 1 + rows_here] = before[want]
        if any_rim:
            raw[n, frames:, 0] = rims[to, 0]
            raw[n, frames:, 1 + rows_here] = rims[to, 1]
            raw[n, :frames, 0] = rims_before[want, 0]
            raw[n, :frames, 1 + rows_here] = rims_before[want, 1]

        @pl.when(jnp.logical_and(first, to == 0))
        def _():
            raw[n, :frames] = jnp.zeros_like(raw[n, :frames])

    side = 3

    def patches(a, b):
        pieces = []
        for s, rim in jobs:
            n = dests.index(s)
            for p in range(frames):
                f = lax.rem(z + p, frames) + a
                if rim:
                    pieces.append(raw[n, f, b])
                    pieces.append(raw[n, f, rows_here - 1 + b])
                else:
                    pieces.append(raw[n, f, 1 + b : b + rows_here - 1].reshape(-1, width))
        return jnp.concatenate(pieces, axis=0)

    lhs = jnp.concatenate([patches(a, b) for a in range(side) for b in range(side)], axis=1)
    count = lhs.shape[0]
    column = lax.broadcasted_iota(jnp.int32, (count, chans), 0) % columns
    total = None
    for lag in (1, 0, 2):
        product = jnp.dot(
            lhs, weights[lag].reshape(-1, chans), preferred_element_type=jnp.float32
        )
        if lag == 1:
            total = product
        elif lag == 0:
            total = total + jnp.where(column == 0, 0.0, pltpu.roll(product, 1, 0))
        else:
            moved = pltpu.roll(product, count - 1, 0)
            total = total + jnp.where(column == columns - 1, 0.0, moved)
    place = 0
    for out in outs:
        out[...] = total[place : place + out.shape[0]].astype(out.dtype)
        place += out.shape[0]


def conv_call(jobs, meta, weights, held, before, rims, frames, out_type, after=()):
    dests = sorted({s for s, _ in jobs})
    _, _, rows_here, columns, width = held.shape
    lags, taps, _, chans = weights.shape
    any_rim = rims is not None
    counts = [frames * (2 if rim else rows_here - 2) * columns for _, rim in jobs]
    operands = [weights, held, before, *(rims if any_rim else ())]
    specs = [pl.BlockSpec(memory_space=pltpu.SMEM)] + in_vmem(len(operands))
    specs += in_vmem(len(after))
    return pl.pallas_call(
        functools.partial(conv_kernel, tuple(jobs), any_rim, frames),
        out_shape=[jax.ShapeDtypeStruct((count, chans), out_type) for count in counts],
        in_specs=specs,
        out_specs=in_vmem(len(jobs)),
        scratch_shapes=[
            pltpu.VMEM((len(dests), 2 * frames, rows_here + 2, columns, width), jnp.bfloat16)
        ],
        compiler_params=pltpu.CompilerParams(vmem_limit_bytes=VMEM_LIMIT),
        cost_estimate=pl.CostEstimate(
            flops=20 * sum(counts) * taps * lags * width * chans,
            bytes_accessed=2 * taps * lags * width * chans,
            transcendentals=0,
        ),
        name="conv_rim" if any_rim else "conv_inner",
    )(meta, *operands, *after)


def sum_call(pieces, splits, after=()):
    count, chans = pieces[0].shape
    size = count // splits

    def kernel(*refs):
        for p, out_ref in enumerate(refs[len(refs) - splits :]):
            total = None
            for ref in refs[: len(pieces)]:
                rows = ref[p * size : (p + 1) * size].astype(jnp.float32)
                total = rows if total is None else total + rows
            out_ref[...] = total.astype(out_ref.dtype)

    return pl.pallas_call(
        kernel,
        out_shape=[jax.ShapeDtypeStruct((size, chans), jnp.bfloat16)] * splits,
        in_specs=in_vmem(len(pieces) + len(after)),
        out_specs=in_vmem(splits),
        compiler_params=pltpu.CompilerParams(vmem_limit_bytes=VMEM_LIMIT),
        name="sum_parts",
    )(*pieces, *after)


def attend_kernel(frames, share, chunks, *refs):
    own_count = frames * chunks
    all_count = own_count * share
    tokens, refs = refs[:all_count], refs[all_count:]
    (wq, wk, wv, wo), refs = refs[:4], refs[4:]
    outs, (normed, keys, values) = refs[:frames], refs[frames:]
    size, chans = normed.shape
    per_group = chans // G

    tile_row = lax.broadcasted_iota(jnp.int32, (LANES, LANES), 0) // per_group
    tile_col = lax.broadcasted_iota(jnp.int32, (LANES, LANES), 1) // per_group
    same = (tile_row == tile_col).astype(jnp.float32).astype(jnp.bfloat16)

    def group_mean(sums):
        first = sums.astype(jnp.bfloat16)
        rest = sums - first.astype(jnp.float32)
        second = rest.astype(jnp.bfloat16)
        third = rest - second.astype(jnp.float32)
        tiles = []
        for tile in range(chans // LANES):
            lanes = slice(tile * LANES, (tile + 1) * LANES)
            stacked = jnp.concatenate(
                [
                    first.astype(jnp.float32)[:, lanes],
                    second.astype(jnp.float32)[:, lanes],
                    third[:, lanes],
                ],
                axis=0,
            ).astype(jnp.bfloat16)
            spread = jnp.dot(stacked, same, preferred_element_type=jnp.float32)
            tiles.append(jnp.sum(spread, axis=0, keepdims=True))
        return jnp.concatenate(tiles, axis=1) / (size * per_group)

    def folded(x):
        return jnp.sum(x.reshape(-1, 8, chans), axis=0)

    average = group_mean(sum(folded(ref[...].astype(jnp.float32)) for ref in tokens))

    def spread_of(ref):
        centered = ref[...].astype(jnp.float32) - average
        return folded(centered * centered)

    scale = lax.rsqrt(group_mean(sum(spread_of(ref) for ref in tokens)) + epsilon)
    place = 0
    for ref in tokens:
        rows = ref.shape[0]
        normed[pl.ds(place, rows)] = (
            (ref[...].astype(jnp.float32) - average) * scale
        ).astype(jnp.bfloat16)
        place += rows

    step = min(256, size)
    for start in range(0, size, step):
        x = normed[pl.ds(start, step)]
        keys[pl.ds(start, step)] = jnp.dot(
            x, wk[...], preferred_element_type=jnp.float32
        ).astype(jnp.bfloat16)
        values[pl.ds(start, step)] = jnp.dot(
            x, wv[...], preferred_element_type=jnp.float32
        ).astype(jnp.bfloat16)

    place = 0
    for p, out in enumerate(outs):
        mine = tokens[p * chunks : (p + 1) * chunks]
        rows = sum(ref.shape[0] for ref in mine)
        queries = jnp.dot(
            normed[pl.ds(place, rows)], wq[...], preferred_element_type=jnp.float32
        ).astype(jnp.bfloat16)
        place += rows
        scores = lax.dot_general(
            queries, keys[...], (((1,), (1,)), ((), ())), preferred_element_type=jnp.float32
        ) * chans ** (-0.5)
        row_max = jnp.max(scores, axis=1, keepdims=True)
        exp_weights = jnp.exp(scores - row_max).astype(jnp.bfloat16)
        denominator = jnp.sum(exp_weights.astype(jnp.float32), axis=1, keepdims=True)
        numerator = jnp.dot(exp_weights, values[...], preferred_element_type=jnp.float32)
        attended = (numerator / denominator).astype(jnp.bfloat16)
        added = jnp.dot(attended, wo[...], preferred_element_type=jnp.float32)
        rows_here, columns, _ = out.shape
        inner = mine[0].shape[0]
        first = mine[0][...].astype(jnp.float32) + added[:inner]
        out[1 : rows_here - 1] = first.astype(jnp.bfloat16).reshape(rows_here - 2, columns, chans)
        second = (mine[1][...].astype(jnp.float32) + added[inner:]).astype(jnp.bfloat16)
        out[0] = second[:columns]
        out[rows_here - 1] = second[columns:]


def attend_call(own, others, weights, frames, rows_here, columns):
    chunks = len(own) // frames
    share = 1 + len(others) // len(own)
    chans = own[0].shape[1]
    size = sum(x.shape[0] for x in own) * share
    mine = size // share
    out = jax.ShapeDtypeStruct((rows_here, columns, chans), jnp.bfloat16)
    operands = [*own, *others, *weights]
    return pl.pallas_call(
        functools.partial(attend_kernel, frames, share, chunks),
        out_shape=[out] * frames,
        in_specs=in_vmem(len(operands)),
        out_specs=in_vmem(frames),
        scratch_shapes=[pltpu.VMEM((size, chans), jnp.bfloat16)] * 3,
        compiler_params=pltpu.CompilerParams(vmem_limit_bytes=VMEM_LIMIT),
        cost_estimate=pl.CostEstimate(
            flops=2 * (2 * size * chans * chans + 2 * mine * chans * (chans + size)),
            bytes_accessed=8 * chans * chans + 2 * size * chans,
            transcendentals=mine * size,
        ),
        name="attend",
    )(*operands)


def body(latents, conv_weight, query_weight, key_weight, value_weight, out_weight):
    frames, rows_here, columns, chans = latents.shape
    taps, chans_here, _ = conv_weight.shape
    devices, depth = lax.axis_size("tm"), lax.axis_size("rows")
    sizes = (devices, depth)
    group = LANES // chans_here
    parts = devices // group
    width = group * chans_here
    t_index, z_index = lax.axis_index("tm"), lax.axis_index("rows")
    part, member = t_index // group, t_index % group
    meta = jnp.stack([part, member, z_index]).astype(jnp.int32)

    def permute(block, target):
        return lax.ppermute(block, BOTH, everywhere(sizes, target))

    def to_part(s):
        return lambda t, z: ((t // group ^ s) * group + t % group, z)

    def to_member(step):
        return lambda t, z: (t // group * group + (t + step) % group, z)

    def across(block):
        groups = [[n * group + m for n in range(parts)] for m in range(group)]
        return lax.all_to_all(block, "tm", 0, 0, axis_index_groups=groups, tiled=True)

    def by_part(x):
        return jnp.moveaxis(x.reshape(*x.shape[:-1], parts, width), -2, 0)

    above = permute(latents[:, -1], lambda t, z: (t, z + 1) if z + 1 < depth else None)
    below = permute(latents[:, 0], lambda t, z: (t, z - 1) if z else None)

    held = across(by_part(latents))
    before = permute(held, to_member(1))

    split = conv_weight.reshape(taps // 3, 3, chans_here, chans)
    slices = [split] + [permute(split, to_member(step)) for step in range(1, group)]
    weights = merge_call(meta, slices)

    away = list(reversed(range(1, parts)))
    conv = functools.partial(
        conv_call, meta=meta, weights=weights, held=held, before=before, frames=frames
    )
    inner = conv([(s, False) for s in away[:1]], rims=None, out_type=jnp.bfloat16)
    inner += conv(
        [(s, False) for s in away[1:]], rims=None, out_type=jnp.bfloat16, after=inner[:1]
    )
    edges = by_part(jnp.stack([above, below]))
    edges, _ = lax.optimization_barrier((edges, inner[-1]))
    edges = across(edges)
    rims = (edges, permute(edges, to_member(1)))
    inner_own = conv([(0, False)], rims=None, out_type=jnp.float32, after=inner[-1:])
    rim = conv([(s, True) for s in away], rims=rims, out_type=jnp.bfloat16, after=inner_own)
    rim_own = conv([(0, True)], rims=rims, out_type=jnp.float32, after=rim[-1:])
    sums = []
    for sent, own_part in ((inner, inner_own), (rim, rim_own)):
        got = [permute(x, to_part(s)) for s, x in zip(away, sent)]
        sums.append(sum_call([*own_part, *got], frames, after=rim_own))

    share = depth // frames

    def frame_home(t, z, p):
        frame = t % CORES * frames + (z + p) % frames
        slot = frame * share + z // frames
        return (t // CORES * CORES + slot % CORES, slot // CORES)

    def next_in_frame(t, z, step):
        slot = z * CORES + t % CORES
        slot = slot // share * share + (slot + step) % share
        return (t // CORES * CORES + slot % CORES, slot // CORES)

    own = []
    for p in range(frames):
        for chunk in sums:
            own.append(permute(chunk[p], lambda t, z: frame_home(t, z, p)))
    others = []
    for step in range(1, share):
        others += [permute(x, lambda t, z: next_in_frame(t, z, step)) for x in own]

    done = attend_call(
        own,
        others,
        (query_weight, key_weight, value_weight, out_weight),
        frames,
        rows_here,
        columns,
    )
    back = []
    for p in range(frames):
        pairs = [(b, a) for a, b in everywhere(sizes, lambda t, z: frame_home(t, z, p))]
        back.append(lax.ppermute(done[p], BOTH, pairs))
    return jnp.stack(
        [
            functools.reduce(
                lambda rest, p: jnp.where((z_index + p) % frames == f, back[p], rest),
                range(1, frames),
                back[0],
            )
            for f in range(frames)
        ]
    )


def solution(mesh):
    placed = (P("tm", "rows", None, None), P(None, "tm", None), P(), P(), P(), P())
    return jax.shard_map(
        body, mesh=mesh, in_specs=placed, out_specs=P("tm", "rows", None, None), check_vma=False
    )
```

```python
import functools

import jax
import jax.numpy as jnp
from jax import lax
from jax.experimental import pallas as pl
from jax.experimental.pallas import tpu as pltpu
from jax.sharding import PartitionSpec as P

G = 32
LANES = 128
CORES = 2

epsilon = 1e-06

BOTH = ("tm", "rows")
VMEM_LIMIT = 32 * 1024 * 1024


def everywhere(sizes, target):
    devices, depth = sizes
    pairs = []
    for t in range(devices):
        for z in range(depth):
            to = target(t, z)
            if to is not None:
                pairs.append((t * depth + z, to[0] * depth + to[1]))
    return pairs


def in_vmem(count):
    return [pl.BlockSpec(memory_space=pltpu.VMEM)] * count


def merge_kernel(group, *refs):
    meta, refs = refs[0], refs[1:]
    slices, out, sems = refs[:group], refs[group], refs[group + 1]
    chans_here = slices[0].shape[2]
    copies = []
    for lag in range(out.shape[0]):
        for step in range(group):
            owner = lax.rem(meta[1] - step + group, group)
            rows = pl.ds(pl.multiple_of(owner * chans_here, 16), chans_here)
            copies.append(
                pltpu.make_async_copy(
                    slices[step].at[:, lag], out.at[lag, :, rows], sems.at[lag, step]
                )
            )
    for copy in copies:
        copy.start()
    for copy in copies:
        copy.wait()


def merge_call(meta, slices):
    group = len(slices)
    taps, lags, chans_here, chans = slices[0].shape
    return pl.pallas_call(
        functools.partial(merge_kernel, group),
        out_shape=jax.ShapeDtypeStruct((lags, taps, group * chans_here, chans), jnp.bfloat16),
        in_specs=[pl.BlockSpec(memory_space=pltpu.SMEM)]
        + [pl.BlockSpec(memory_space=pltpu.HBM)]
        + [pl.BlockSpec(memory_space=pl.ANY)] * (group - 1),
        out_specs=pl.BlockSpec(memory_space=pltpu.VMEM),
        scratch_shapes=[pltpu.SemaphoreType.DMA((lags, group))],
        compiler_params=pltpu.CompilerParams(vmem_limit_bytes=VMEM_LIMIT),
        name="merge_kernel_slices",
    )(meta, *slices)


def partner(member, place):
    odd = member % 2 == 1
    if isinstance(member, int) and isinstance(place, int):
        return 3 - place if odd and place in (1, 2) else place
    swapped = jnp.where(jnp.logical_or(place == 1, place == 2), 3 - place, place)
    return jnp.where(odd, swapped, place)


def split_call(meta, above, below, parts):
    frames, columns, chans = above.shape
    width = chans // parts

    def kernel(meta, above, below, *outs):
        for place, out in enumerate(outs):
            to = lax.bitwise_xor(meta[0], partner(meta[1], jnp.int32(place)))
            lanes = pl.ds(pl.multiple_of(to * width, width), width)
            out[0] = above[:, :, lanes]
            out[1] = below[:, :, lanes]

    return pl.pallas_call(
        kernel,
        out_shape=[jax.ShapeDtypeStruct((2, frames, columns, width), above.dtype)] * parts,
        in_specs=[pl.BlockSpec(memory_space=pltpu.SMEM)] + in_vmem(2),
        out_specs=in_vmem(parts),
        compiler_params=pltpu.CompilerParams(vmem_limit_bytes=VMEM_LIMIT),
        name="split_halo_rows",
    )(meta, above, below)


def stack_call(pieces, after):
    def kernel(*refs):
        for i in range(len(pieces)):
            refs[-1][i] = refs[i][...]

    return pl.pallas_call(
        kernel,
        out_shape=jax.ShapeDtypeStruct((len(pieces), *pieces[0].shape), pieces[0].dtype),
        in_specs=in_vmem(len(pieces) + 1),
        out_specs=pl.BlockSpec(memory_space=pltpu.VMEM),
        compiler_params=pltpu.CompilerParams(vmem_limit_bytes=VMEM_LIMIT),
        name="stack_halo_rows",
    )(*pieces, after)


def conv_kernel(jobs, parts, group, frames, out_count, *refs):
    meta, weights, refs = refs[0], refs[1], refs[2:]
    dests = sorted({s for s, _ in jobs})
    any_rim = any(rim for _, rim in jobs)
    held, refs = refs[: len(dests)], refs[len(dests) :]
    before, refs = refs[:parts], refs[parts:]
    if any_rim:
        (rims, rims_before), refs = refs[:2], refs[2:]
    outs, raw = refs[:-1], refs[-1]
    outs = outs[len(outs) - out_count :]
    part, member, z = meta[0], meta[1], meta[2]
    lags, _, width, chans = weights.shape
    _, rows_here, columns, _ = held[0].shape

    first = member == 0
    for n, where in enumerate(dests):
        to = lax.bitwise_xor(part, partner(member, jnp.int32(where)))
        valid = jnp.logical_or(jnp.logical_not(first), to > 0)
        sender = jnp.where(first, group - 1, member - 1)
        want = jnp.where(first, jnp.maximum(to - 1, 0), to)
        place = partner(sender, lax.bitwise_xor(part, want))
        raw[n, frames:, 1 : 1 + rows_here] = held[n][...]
        if any_rim:
            raw[n, frames:, 0] = rims[where, 0]
            raw[n, frames:, 1 + rows_here] = rims[where, 1]
            raw[n, :frames, 0] = rims_before[place, 0]
            raw[n, :frames, 1 + rows_here] = rims_before[place, 1]
        for i in range(parts):

            @pl.when(place == i)
            def _():
                raw[n, :frames, 1 : 1 + rows_here] = before[i][...]

        @pl.when(jnp.logical_not(valid))
        def _():
            raw[n, :frames] = jnp.zeros_like(raw[n, :frames])

    side = 3

    def patches(a, b):
        pieces = []
        for s, rim in jobs:
            n = dests.index(s)
            for p in range(frames):
                f = lax.rem(z + p, frames) + a
                if rim:
                    pieces.append(raw[n, f, b])
                    pieces.append(raw[n, f, rows_here - 1 + b])
                else:
                    pieces.append(raw[n, f, 1 + b : b + rows_here - 1].reshape(-1, width))
        return jnp.concatenate(pieces, axis=0)

    lhs = jnp.concatenate([patches(a, b) for a in range(side) for b in range(side)], axis=1)
    count = lhs.shape[0]
    column = lax.broadcasted_iota(jnp.int32, (count, chans), 0) % columns
    total = None
    for lag in (1, 0, 2):
        product = jnp.dot(
            lhs, weights[lag].reshape(-1, chans), preferred_element_type=jnp.float32
        )
        if lag == 1:
            total = product
        elif lag == 0:
            total = total + jnp.where(column == 0, 0.0, pltpu.roll(product, 1, 0))
        else:
            moved = pltpu.roll(product, count - 1, 0)
            total = total + jnp.where(column == columns - 1, 0.0, moved)
    place = 0
    for out in outs:
        out[...] = total[place : place + out.shape[0]].astype(out.dtype)
        place += out.shape[0]


def conv_call(jobs, meta, weights, held, before, rims, group, frames, out_type, after=()):
    parts = len(held)
    dests = sorted({place for place, _ in jobs})
    _, rows_here, columns, width = held[0].shape
    lags, taps, _, chans = weights.shape
    any_rim = any(rim for _, rim in jobs)
    counts = [frames * (2 if rim else rows_here - 2) * columns for _, rim in jobs]
    total = sum(counts)
    operands = [weights, *[held[n] for n in dests], *before, *(rims if any_rim else ())]
    specs = [pl.BlockSpec(memory_space=pltpu.SMEM)] + in_vmem(len(operands))
    specs += in_vmem(len(after))
    outs = [jax.ShapeDtypeStruct((count, chans), out_type) for count in counts]
    return pl.pallas_call(
        functools.partial(conv_kernel, tuple(jobs), parts, group, frames, len(outs)),
        out_shape=outs,
        in_specs=specs,
        out_specs=in_vmem(len(outs)),
        scratch_shapes=[
            pltpu.VMEM((len(dests), 2 * frames, rows_here + 2, columns, width), jnp.bfloat16)
        ],
        compiler_params=pltpu.CompilerParams(vmem_limit_bytes=VMEM_LIMIT),
        cost_estimate=pl.CostEstimate(
            flops=20 * total * taps * lags * width * chans,
            bytes_accessed=2 * taps * lags * width * chans,
            transcendentals=0,
        ),
        name="conv_rim" if any_rim else "conv_inner",
    )(meta, *operands, *after)


def sum_call(pieces, splits, after=()):
    count, chans = pieces[0].shape
    size = count // splits

    def kernel(*refs):
        for p, out_ref in enumerate(refs[len(refs) - splits :]):
            total = None
            for ref in refs[: len(pieces)]:
                rows = ref[p * size : (p + 1) * size].astype(jnp.float32)
                total = rows if total is None else total + rows
            out_ref[...] = total.astype(out_ref.dtype)

    return pl.pallas_call(
        kernel,
        out_shape=[jax.ShapeDtypeStruct((size, chans), jnp.bfloat16)] * splits,
        in_specs=in_vmem(len(pieces) + len(after)),
        out_specs=in_vmem(splits),
        compiler_params=pltpu.CompilerParams(vmem_limit_bytes=VMEM_LIMIT),
        name="sum_parts",
    )(*pieces, *after)


def attend_kernel(frames, share, chunks, *refs):
    own_count = frames * chunks
    all_count = own_count * share
    tokens, refs = refs[:all_count], refs[all_count:]
    (wq, wk, wv, wo), refs = refs[:4], refs[4:]
    outs, (normed, keys, values) = refs[:frames], refs[frames:]
    size, chans = normed.shape
    per_group = chans // G

    tile_row = lax.broadcasted_iota(jnp.int32, (LANES, LANES), 0) // per_group
    tile_col = lax.broadcasted_iota(jnp.int32, (LANES, LANES), 1) // per_group
    same = (tile_row == tile_col).astype(jnp.float32).astype(jnp.bfloat16)

    def group_mean(sums):
        first = sums.astype(jnp.bfloat16)
        rest = sums - first.astype(jnp.float32)
        second = rest.astype(jnp.bfloat16)
        third = rest - second.astype(jnp.float32)
        tiles = []
        for tile in range(chans // LANES):
            lanes = slice(tile * LANES, (tile + 1) * LANES)
            stacked = jnp.concatenate(
                [
                    first.astype(jnp.float32)[:, lanes],
                    second.astype(jnp.float32)[:, lanes],
                    third[:, lanes],
                ],
                axis=0,
            ).astype(jnp.bfloat16)
            spread = jnp.dot(stacked, same, preferred_element_type=jnp.float32)
            tiles.append(jnp.sum(spread, axis=0, keepdims=True))
        return jnp.concatenate(tiles, axis=1) / (size * per_group)

    def folded(x):
        return jnp.sum(x.reshape(-1, 8, chans), axis=0)

    average = group_mean(sum(folded(ref[...].astype(jnp.float32)) for ref in tokens))

    def spread_of(ref):
        centered = ref[...].astype(jnp.float32) - average
        return folded(centered * centered)

    scale = lax.rsqrt(group_mean(sum(spread_of(ref) for ref in tokens)) + epsilon)
    place = 0
    for ref in tokens:
        rows = ref.shape[0]
        normed[pl.ds(place, rows)] = (
            (ref[...].astype(jnp.float32) - average) * scale
        ).astype(jnp.bfloat16)
        place += rows

    step = min(256, size)
    for start in range(0, size, step):
        x = normed[pl.ds(start, step)]
        keys[pl.ds(start, step)] = jnp.dot(
            x, wk[...], preferred_element_type=jnp.float32
        ).astype(jnp.bfloat16)
        values[pl.ds(start, step)] = jnp.dot(
            x, wv[...], preferred_element_type=jnp.float32
        ).astype(jnp.bfloat16)

    place = 0
    for p, out in enumerate(outs):
        mine = tokens[p * chunks : (p + 1) * chunks]
        rows = sum(ref.shape[0] for ref in mine)
        queries = jnp.dot(
            normed[pl.ds(place, rows)], wq[...], preferred_element_type=jnp.float32
        ).astype(jnp.bfloat16)
        place += rows
        scores = lax.dot_general(
            queries, keys[...], (((1,), (1,)), ((), ())), preferred_element_type=jnp.float32
        ) * chans ** (-0.5)
        row_max = jnp.max(scores, axis=1, keepdims=True)
        exp_weights = jnp.exp(scores - row_max).astype(jnp.bfloat16)
        denominator = jnp.sum(exp_weights.astype(jnp.float32), axis=1, keepdims=True)
        numerator = jnp.dot(exp_weights, values[...], preferred_element_type=jnp.float32)
        attended = (numerator / denominator).astype(jnp.bfloat16)
        added = jnp.dot(attended, wo[...], preferred_element_type=jnp.float32)
        rows_here, columns, _ = out.shape
        inner = mine[0].shape[0]
        first = mine[0][...].astype(jnp.float32) + added[:inner]
        out[1 : rows_here - 1] = first.astype(jnp.bfloat16).reshape(rows_here - 2, columns, chans)
        second = (mine[1][...].astype(jnp.float32) + added[inner:]).astype(jnp.bfloat16)
        out[0] = second[:columns]
        out[rows_here - 1] = second[columns:]


def attend_call(own, others, weights, frames, rows_here, columns):
    chunks = len(own) // frames
    share = 1 + len(others) // len(own)
    chans = own[0].shape[1]
    size = sum(x.shape[0] for x in own) * share
    mine = size // share
    out = jax.ShapeDtypeStruct((rows_here, columns, chans), jnp.bfloat16)
    operands = [*own, *others, *weights]
    return pl.pallas_call(
        functools.partial(attend_kernel, frames, share, chunks),
        out_shape=[out] * frames,
        in_specs=in_vmem(len(operands)),
        out_specs=in_vmem(frames),
        scratch_shapes=[pltpu.VMEM((size, chans), jnp.bfloat16)] * 3,
        compiler_params=pltpu.CompilerParams(vmem_limit_bytes=VMEM_LIMIT),
        cost_estimate=pl.CostEstimate(
            flops=2 * (2 * size * chans * chans + 2 * mine * chans * (chans + size)),
            bytes_accessed=8 * chans * chans + 2 * size * chans,
            transcendentals=mine * size,
        ),
        name="attend",
    )(*operands)


def body(latents, conv_weight, query_weight, key_weight, value_weight, out_weight):
    frames, rows_here, columns, chans = latents.shape
    taps, chans_here, _ = conv_weight.shape
    devices, depth = lax.axis_size("tm"), lax.axis_size("rows")
    sizes = (devices, depth)
    group = LANES // chans_here
    parts = devices // group
    width = group * chans_here
    t_index, z_index = lax.axis_index("tm"), lax.axis_index("rows")
    part, member = t_index // group, t_index % group
    meta = jnp.stack([part, member, z_index]).astype(jnp.int32)

    def permute(block, target):
        return lax.ppermute(block, BOTH, everywhere(sizes, target))

    def to_place(place):
        return lambda t, z: ((t // group ^ partner(t % group, place)) * group + t % group, z)

    def to_member(step):
        return lambda t, z: (t // group * group + (t + step) % group, z)

    split = conv_weight.reshape(taps // 3, 3, chans_here, chans)
    slices = [split] + [permute(split, to_member(step)) for step in range(1, group)]
    weights = merge_call(meta, slices)

    above = permute(latents[:, -1], lambda t, z: (t, z + 1) if z + 1 < depth else None)
    below = permute(latents[:, 0], lambda t, z: (t, z - 1) if z else None)

    held, before = [None] * parts, [None] * parts
    order = [0, 3, 1, 2]
    for place in order:
        start = (part ^ partner(member, jnp.int32(place))) * width
        piece = lax.dynamic_slice_in_dim(latents, start, width, axis=3)
        held[place] = permute(piece, to_place(place)) if place else piece
    held[2], weights = lax.optimization_barrier((held[2], weights))
    for place in order:
        before[place] = permute(held[place], to_member(1))

    conv = functools.partial(
        conv_call,
        meta=meta,
        weights=weights,
        held=held,
        before=before,
        group=group,
        frames=frames,
    )

    def hop(pieces):
        return [permute(x, to_place(1)) for x in pieces]

    rims = split_call(meta, above, below, parts)
    inner_sent = conv(
        [(3, False), (1, False)], rims=None, out_type=jnp.bfloat16, after=rims[:1]
    )
    inner_got = hop(inner_sent)
    inner_on, inner_own = conv(
        [(2, False), (0, False)], rims=None, out_type=jnp.float32, after=inner_sent[:1]
    )
    rims, _ = lax.optimization_barrier((rims, inner_sent[0]))
    rims = [permute(x, to_place(place)) if place else x for place, x in enumerate(rims)]
    rims = stack_call(rims, inner_on)
    rims = (rims, permute(rims, to_member(1)))
    (inner_relay,) = sum_call([inner_on, inner_got[0]], 1, after=inner_got[1:])
    rim_sent = conv(
        [(3, True), (1, True)], rims=rims, out_type=jnp.bfloat16, after=(inner_relay,)
    )
    rim_got = hop(rim_sent)
    inner_last = permute(inner_relay, to_place(2))
    rim_on, rim_own = conv(
        [(2, True), (0, True)], rims=rims, out_type=jnp.float32, after=rim_sent[:1]
    )
    (rim_relay,) = sum_call([rim_on, rim_got[0]], 1, after=rim_got[1:])
    rim_last = permute(rim_relay, to_place(2))
    sums = [
        sum_call([inner_own, inner_got[1], inner_last], frames),
        sum_call([rim_own, rim_got[1], rim_last], frames),
    ]

    segments = depth // frames

    def frame_home(t, z, p, s):
        slot = t % CORES * frames + (z + p) % frames
        segment = (z // frames + s) % segments
        return (t // CORES * CORES + slot % CORES, segment * frames + slot // CORES)

    own, others = [None] * (frames * len(sums)), []
    for c, chunk in enumerate(sums):
        for s in reversed(range(segments)):
            for p in range(frames):
                block = permute(chunk[p], lambda t, z: frame_home(t, z, p, s))
                if s:
                    others.append(block)
                else:
                    own[p * len(sums) + c] = block

    done = attend_call(
        own,
        others,
        (query_weight, key_weight, value_weight, out_weight),
        frames,
        rows_here,
        columns,
    )
    back = []
    for p in range(frames):
        pairs = [(b, a) for a, b in everywhere(sizes, lambda t, z: frame_home(t, z, p, 0))]
        back.append(lax.ppermute(done[p], BOTH, pairs))
    return jnp.stack(
        [
            functools.reduce(
                lambda rest, p: jnp.where((z_index + p) % frames == f, back[p], rest),
                range(1, frames),
                back[0],
            )
            for f in range(frames)
        ]
    )


def solution(mesh):
    placed = (P("tm", "rows", None, None), P(None, "tm", None), P(), P(), P(), P())
    return jax.shard_map(
        body, mesh=mesh, in_specs=placed, out_specs=P("tm", "rows", None, None), check_vma=False
    )
```

```python
import functools

import jax
import jax.numpy as jnp
from jax import lax
from jax.experimental import pallas as pl
from jax.experimental.pallas import tpu as pltpu
from jax.sharding import PartitionSpec as P

G = 32
LANES = 128
CORES = 2

epsilon = 1e-06

BOTH = ("tm", "rows")
VMEM_LIMIT = 32 * 1024 * 1024


def everywhere(sizes, target):
    devices, depth = sizes
    pairs = []
    for t in range(devices):
        for z in range(depth):
            to = target(t, z)
            if to is not None:
                pairs.append((t * depth + z, to[0] * depth + to[1]))
    return pairs


def in_vmem(count):
    return [pl.BlockSpec(memory_space=pltpu.VMEM)] * count


def merge_kernel(group, *refs):
    meta, refs = refs[0], refs[1:]
    slices, out, sems = refs[:group], refs[group], refs[group + 1]
    chans_here = slices[0].shape[2]
    copies = []
    for lag in range(out.shape[0]):
        for step in range(group):
            owner = lax.rem(meta[1] - step + group, group)
            rows = pl.ds(pl.multiple_of(owner * chans_here, 16), chans_here)
            copies.append(
                pltpu.make_async_copy(
                    slices[step].at[:, lag], out.at[lag, :, rows], sems.at[lag, step]
                )
            )
    for copy in copies:
        copy.start()
    for copy in copies:
        copy.wait()


def merge_call(meta, slices):
    group = len(slices)
    taps, lags, chans_here, chans = slices[0].shape
    return pl.pallas_call(
        functools.partial(merge_kernel, group),
        out_shape=jax.ShapeDtypeStruct((lags, taps, group * chans_here, chans), jnp.bfloat16),
        in_specs=[pl.BlockSpec(memory_space=pltpu.SMEM)]
        + [pl.BlockSpec(memory_space=pl.ANY)] * group,
        out_specs=pl.BlockSpec(memory_space=pltpu.VMEM),
        scratch_shapes=[pltpu.SemaphoreType.DMA((lags, group))],
        compiler_params=pltpu.CompilerParams(vmem_limit_bytes=VMEM_LIMIT),
        name="merge_kernel_slices",
    )(meta, *slices)


def halo_call(pieces, after):
    frames, rows_here, columns, width = pieces[0].shape
    out = jax.ShapeDtypeStruct((len(pieces), frames, columns, width), jnp.bfloat16)

    def kernel(*refs):
        first, last = refs[-2:]
        for i in range(len(pieces)):
            first[i] = refs[i][:, 0]
            last[i] = refs[i][:, rows_here - 1]

    return pl.pallas_call(
        kernel,
        out_shape=[out] * 2,
        in_specs=in_vmem(len(pieces) + 1),
        out_specs=in_vmem(2),
        compiler_params=pltpu.CompilerParams(vmem_limit_bytes=VMEM_LIMIT),
        name="halo_rows",
    )(*pieces, after)


def conv_kernel(jobs, parts, frames, *refs):
    meta, weights, refs = refs[0], refs[1], refs[2:]
    dests = sorted({s for s, _ in jobs})
    any_rim = any(rim for _, rim in jobs)
    held, refs = refs[: len(dests)], refs[len(dests) :]
    before, refs = refs[:parts], refs[parts:]
    if any_rim:
        (above, below, above_before, below_before), refs = refs[:4], refs[4:]
    outs, raw = refs[-1 - len(jobs) : -1], refs[-1]
    part, member, z = meta[0], meta[1], meta[2]
    lags, _, width, chans = weights.shape
    _, rows_here, columns, _ = held[0].shape

    for n, s in enumerate(dests):
        to = lax.bitwise_xor(part, s)
        wraps = member == 0
        place = jnp.where(wraps, lax.bitwise_xor(part, jnp.maximum(to - 1, 0)), s)
        valid = jnp.logical_or(jnp.logical_not(wraps), to > 0)
        raw[n, frames:, 1 : 1 + rows_here] = held[n][...]
        if any_rim:
            raw[n, frames:, 0] = above[s]
            raw[n, frames:, 1 + rows_here] = below[s]
            raw[n, :frames, 0] = above_before[place]
            raw[n, :frames, 1 + rows_here] = below_before[place]
        for i in range(parts):

            @pl.when(place == i)
            def _():
                raw[n, :frames, 1 : 1 + rows_here] = before[i][...]

        @pl.when(jnp.logical_not(valid))
        def _():
            raw[n, :frames] = jnp.zeros_like(raw[n, :frames])

    side = 3

    def patches(a, b):
        pieces = []
        for s, rim in jobs:
            n = dests.index(s)
            for p in range(frames):
                f = lax.rem(z + p, frames) + a
                if rim:
                    pieces.append(raw[n, f, b])
                    pieces.append(raw[n, f, rows_here - 1 + b])
                else:
                    pieces.append(raw[n, f, 1 + b : b + rows_here - 1].reshape(-1, width))
        return jnp.concatenate(pieces, axis=0)

    lhs = jnp.concatenate([patches(a, b) for a in range(side) for b in range(side)], axis=1)
    count = lhs.shape[0]
    column = lax.broadcasted_iota(jnp.int32, (count, chans), 0) % columns
    total = None
    for lag in (1, 0, 2):
        product = jnp.dot(
            lhs, weights[lag].reshape(-1, chans), preferred_element_type=jnp.float32
        )
        if lag == 1:
            total = product
        elif lag == 0:
            total = total + jnp.where(column == 0, 0.0, pltpu.roll(product, 1, 0))
        else:
            moved = pltpu.roll(product, count - 1, 0)
            total = total + jnp.where(column == columns - 1, 0.0, moved)
    place = 0
    for out in outs:
        out[...] = total[place : place + out.shape[0]].astype(out.dtype)
        place += out.shape[0]


def conv_call(jobs, meta, weights, held, before, halos, frames, out_type, after=()):
    parts = len(held)
    dests = sorted({s for s, _ in jobs})
    _, rows_here, columns, width = held[0].shape
    lags, taps, _, chans = weights.shape
    any_rim = any(rim for _, rim in jobs)
    counts = [frames * (2 if rim else rows_here - 2) * columns for _, rim in jobs]
    operands = [weights, *[held[s] for s in dests], *before, *(halos if any_rim else ())]
    specs = [pl.BlockSpec(memory_space=pltpu.SMEM)] + in_vmem(len(operands))
    specs += in_vmem(len(after))
    return pl.pallas_call(
        functools.partial(conv_kernel, tuple(jobs), parts, frames),
        out_shape=[jax.ShapeDtypeStruct((count, chans), out_type) for count in counts],
        in_specs=specs,
        out_specs=in_vmem(len(jobs)),
        scratch_shapes=[
            pltpu.VMEM((len(dests), 2 * frames, rows_here + 2, columns, width), jnp.bfloat16)
        ],
        compiler_params=pltpu.CompilerParams(vmem_limit_bytes=VMEM_LIMIT),
        cost_estimate=pl.CostEstimate(
            flops=20 * sum(counts) * taps * lags * width * chans,
            bytes_accessed=2 * taps * lags * width * chans,
            transcendentals=0,
        ),
        name="conv_rim" if any_rim else "conv_inner",
    )(meta, *operands, *after)


def sum_call(pieces, splits, after=()):
    count, chans = pieces[0].shape
    size = count // splits

    def kernel(*refs):
        for p, out_ref in enumerate(refs[len(refs) - splits :]):
            total = None
            for ref in refs[: len(pieces)]:
                rows = ref[p * size : (p + 1) * size].astype(jnp.float32)
                total = rows if total is None else total + rows
            out_ref[...] = total.astype(out_ref.dtype)

    return pl.pallas_call(
        kernel,
        out_shape=[jax.ShapeDtypeStruct((size, chans), jnp.bfloat16)] * splits,
        in_specs=in_vmem(len(pieces) + len(after)),
        out_specs=in_vmem(splits),
        compiler_params=pltpu.CompilerParams(vmem_limit_bytes=VMEM_LIMIT),
        name="sum_parts",
    )(*pieces, *after)


def attend_kernel(frames, share, chunks, *refs):
    own_count = frames * chunks
    all_count = own_count * share
    tokens, refs = refs[:all_count], refs[all_count:]
    (wq, wk, wv, wo), refs = refs[:4], refs[4:]
    outs, (normed, keys, values) = refs[:frames], refs[frames:]
    size, chans = normed.shape
    per_group = chans // G

    tile_row = lax.broadcasted_iota(jnp.int32, (LANES, LANES), 0) // per_group
    tile_col = lax.broadcasted_iota(jnp.int32, (LANES, LANES), 1) // per_group
    same = (tile_row == tile_col).astype(jnp.float32).astype(jnp.bfloat16)

    def group_mean(sums):
        first = sums.astype(jnp.bfloat16)
        rest = sums - first.astype(jnp.float32)
        second = rest.astype(jnp.bfloat16)
        third = rest - second.astype(jnp.float32)
        tiles = []
        for tile in range(chans // LANES):
            lanes = slice(tile * LANES, (tile + 1) * LANES)
            stacked = jnp.concatenate(
                [
                    first.astype(jnp.float32)[:, lanes],
                    second.astype(jnp.float32)[:, lanes],
                    third[:, lanes],
                ],
                axis=0,
            ).astype(jnp.bfloat16)
            spread = jnp.dot(stacked, same, preferred_element_type=jnp.float32)
            tiles.append(jnp.sum(spread, axis=0, keepdims=True))
        return jnp.concatenate(tiles, axis=1) / (size * per_group)

    def folded(x):
        return jnp.sum(x.reshape(-1, 8, chans), axis=0)

    average = group_mean(sum(folded(ref[...].astype(jnp.float32)) for ref in tokens))

    def spread_of(ref):
        centered = ref[...].astype(jnp.float32) - average
        return folded(centered * centered)

    scale = lax.rsqrt(group_mean(sum(spread_of(ref) for ref in tokens)) + epsilon)
    place = 0
    for ref in tokens:
        rows = ref.shape[0]
        normed[pl.ds(place, rows)] = (
            (ref[...].astype(jnp.float32) - average) * scale
        ).astype(jnp.bfloat16)
        place += rows

    step = min(256, size)
    for start in range(0, size, step):
        x = normed[pl.ds(start, step)]
        keys[pl.ds(start, step)] = jnp.dot(
            x, wk[...], preferred_element_type=jnp.float32
        ).astype(jnp.bfloat16)
        values[pl.ds(start, step)] = jnp.dot(
            x, wv[...], preferred_element_type=jnp.float32
        ).astype(jnp.bfloat16)

    place = 0
    for p, out in enumerate(outs):
        mine = tokens[p * chunks : (p + 1) * chunks]
        rows = sum(ref.shape[0] for ref in mine)
        queries = jnp.dot(
            normed[pl.ds(place, rows)], wq[...], preferred_element_type=jnp.float32
        ).astype(jnp.bfloat16)
        place += rows
        scores = lax.dot_general(
            queries, keys[...], (((1,), (1,)), ((), ())), preferred_element_type=jnp.float32
        ) * chans ** (-0.5)
        row_max = jnp.max(scores, axis=1, keepdims=True)
        exp_weights = jnp.exp(scores - row_max).astype(jnp.bfloat16)
        denominator = jnp.sum(exp_weights.astype(jnp.float32), axis=1, keepdims=True)
        numerator = jnp.dot(exp_weights, values[...], preferred_element_type=jnp.float32)
        attended = (numerator / denominator).astype(jnp.bfloat16)
        added = jnp.dot(attended, wo[...], preferred_element_type=jnp.float32)
        rows_here, columns, _ = out.shape
        inner = mine[0].shape[0]
        first = mine[0][...].astype(jnp.float32) + added[:inner]
        out[1 : rows_here - 1] = first.astype(jnp.bfloat16).reshape(rows_here - 2, columns, chans)
        second = (mine[1][...].astype(jnp.float32) + added[inner:]).astype(jnp.bfloat16)
        out[0] = second[:columns]
        out[rows_here - 1] = second[columns:]


def attend_call(own, others, weights, frames, rows_here, columns):
    chunks = len(own) // frames
    share = 1 + len(others) // len(own)
    chans = own[0].shape[1]
    size = sum(x.shape[0] for x in own) * share
    mine = size // share
    out = jax.ShapeDtypeStruct((rows_here, columns, chans), jnp.bfloat16)
    operands = [*own, *others, *weights]
    return pl.pallas_call(
        functools.partial(attend_kernel, frames, share, chunks),
        out_shape=[out] * frames,
        in_specs=in_vmem(len(operands)),
        out_specs=in_vmem(frames),
        scratch_shapes=[pltpu.VMEM((size, chans), jnp.bfloat16)] * 3,
        compiler_params=pltpu.CompilerParams(vmem_limit_bytes=VMEM_LIMIT),
        cost_estimate=pl.CostEstimate(
            flops=2 * (2 * size * chans * chans + 2 * mine * chans * (chans + size)),
            bytes_accessed=8 * chans * chans + 2 * size * chans,
            transcendentals=mine * size,
        ),
        name="attend",
    )(*operands)


def body(latents, conv_weight, query_weight, key_weight, value_weight, out_weight):
    frames, rows_here, columns, chans = latents.shape
    taps, chans_here, _ = conv_weight.shape
    devices, depth = lax.axis_size("tm"), lax.axis_size("rows")
    sizes = (devices, depth)
    group = LANES // chans_here
    parts = devices // group
    width = group * chans_here
    t_index, z_index = lax.axis_index("tm"), lax.axis_index("rows")
    part, member = t_index // group, t_index % group
    meta = jnp.stack([part, member, z_index]).astype(jnp.int32)

    def permute(block, target):
        return lax.ppermute(block, BOTH, everywhere(sizes, target))

    def to_part(s):
        return lambda t, z: ((t // group ^ s) * group + t % group, z)

    def to_member(step):
        return lambda t, z: (t // group * group + (t + step) % group, z)

    split = conv_weight.reshape(taps // 3, 3, chans_here, chans)
    slices = [split] + [permute(split, to_member(step)) for step in range(1, group)]
    weights = merge_call(meta, slices)

    held, before = [None] * parts, [None] * parts
    for s in reversed(range(parts)):
        piece = lax.dynamic_slice_in_dim(latents, (part ^ s) * width, width, axis=3)
        held[s] = permute(piece, to_part(s)) if s else piece
    held[-1], weights = lax.optimization_barrier((held[-1], weights))
    for s in range(parts):
        before[s] = permute(held[s], to_member(1))

    away = list(reversed(range(1, parts)))
    conv = functools.partial(
        conv_call, meta=meta, weights=weights, held=held, before=before, frames=frames
    )
    inner = conv([(s, False) for s in away[:1]], halos=None, out_type=jnp.bfloat16)
    inner += conv(
        [(s, False) for s in away[1:]], halos=None, out_type=jnp.bfloat16, after=inner[:1]
    )
    inner_got = [permute(x, to_part(s)) for s, x in zip(away, inner)]
    first, last = halo_call(held, inner[-1])
    halos = (
        permute(last, lambda t, z: (t, z + 1) if z + 1 < depth else None),
        permute(first, lambda t, z: (t, z - 1) if z else None),
    )
    halos += tuple(permute(x, to_member(1)) for x in halos)
    inner_own = conv([(0, False)], halos=None, out_type=jnp.float32, after=(first, *inner_got[:1]))
    rim = conv([(s, True) for s in away], halos=halos, out_type=jnp.bfloat16, after=(*inner_own, *inner_got[:0]))
    rim_own = conv([(0, True)], halos=halos, out_type=jnp.float32, after=rim[-1:])
    rim_got = [permute(x, to_part(s)) for s, x in zip(away, rim)]
    sums = [
        sum_call([*own_part, *got], frames, after=rim_own)
        for own_part, got in ((inner_own, inner_got), (rim_own, rim_got))
    ]

    share = depth // frames

    def frame_home(t, z, p):
        frame = t % CORES * frames + (z + p) % frames
        slot = frame * share + z // frames
        return (t // CORES * CORES + slot % CORES, slot // CORES)

    def next_in_frame(t, z, step):
        slot = z * CORES + t % CORES
        slot = slot // share * share + (slot + step) % share
        return (t // CORES * CORES + slot % CORES, slot // CORES)

    own = []
    for p in range(frames):
        for chunk in sums:
            own.append(permute(chunk[p], lambda t, z: frame_home(t, z, p)))
    others = []
    for step in range(1, share):
        others += [permute(x, lambda t, z: next_in_frame(t, z, step)) for x in own]

    done = attend_call(
        own,
        others,
        (query_weight, key_weight, value_weight, out_weight),
        frames,
        rows_here,
        columns,
    )
    back = []
    for p in range(frames):
        pairs = [(b, a) for a, b in everywhere(sizes, lambda t, z: frame_home(t, z, p))]
        back.append(lax.ppermute(done[p], BOTH, pairs))
    return jnp.stack(
        [
            functools.reduce(
                lambda rest, p: jnp.where((z_index + p) % frames == f, back[p], rest),
                range(1, frames),
                back[0],
            )
            for f in range(frames)
        ]
    )


def solution(mesh):
    placed = (P("tm", "rows", None, None), P(None, "tm", None), P(), P(), P(), P())
    return jax.shard_map(
        body, mesh=mesh, in_specs=placed, out_specs=P("tm", "rows", None, None), check_vma=False
    )
```

```python
import functools

import jax
import jax.numpy as jnp
from jax import lax
from jax.experimental import pallas as pl
from jax.experimental.pallas import tpu as pltpu
from jax.sharding import PartitionSpec as P

G = 32
LANES = 128
CORES = 2

epsilon = 1e-06

BOTH = ("tm", "rows")
VMEM_LIMIT = 32 * 1024 * 1024


def everywhere(sizes, target):
    devices, depth = sizes
    pairs = []
    for t in range(devices):
        for z in range(depth):
            to = target(t, z)
            if to is not None:
                pairs.append((t * depth + z, to[0] * depth + to[1]))
    return pairs


def in_vmem(count):
    return [pl.BlockSpec(memory_space=pltpu.VMEM)] * count


def merge_kernel(group, *refs):
    meta, refs = refs[0], refs[1:]
    slices, out, sems = refs[:group], refs[group], refs[group + 1]
    chans_here = slices[0].shape[2]
    copies = []
    for lag in range(out.shape[0]):
        for step in range(group):
            owner = lax.rem(meta[1] - step + group, group)
            rows = pl.ds(pl.multiple_of(owner * chans_here, 16), chans_here)
            copies.append(
                pltpu.make_async_copy(
                    slices[step].at[:, lag], out.at[lag, :, rows], sems.at[lag, step]
                )
            )
    for copy in copies:
        copy.start()
    for copy in copies:
        copy.wait()


def merge_call(meta, slices):
    group = len(slices)
    taps, lags, chans_here, chans = slices[0].shape
    return pl.pallas_call(
        functools.partial(merge_kernel, group),
        out_shape=jax.ShapeDtypeStruct((lags, taps, group * chans_here, chans), jnp.bfloat16),
        in_specs=[pl.BlockSpec(memory_space=pltpu.SMEM)]
        + [pl.BlockSpec(memory_space=pltpu.HBM)]
        + [pl.BlockSpec(memory_space=pl.ANY)] * (group - 1),
        out_specs=pl.BlockSpec(memory_space=pltpu.VMEM),
        scratch_shapes=[pltpu.SemaphoreType.DMA((lags, group))],
        compiler_params=pltpu.CompilerParams(vmem_limit_bytes=VMEM_LIMIT),
        name="merge_kernel_slices",
    )(meta, *slices)


def partner(member, place):
    odd = member % 2 == 1
    if isinstance(member, int) and isinstance(place, int):
        return 3 - place if odd and place in (1, 2) else place
    swapped = jnp.where(jnp.logical_or(place == 1, place == 2), 3 - place, place)
    return jnp.where(odd, swapped, place)


def split_call(meta, above, below, parts):
    frames, columns, chans = above.shape
    width = chans // parts

    def kernel(meta, above, below, *outs):
        for place, out in enumerate(outs):
            to = lax.bitwise_xor(meta[0], partner(meta[1], jnp.int32(place)))
            lanes = pl.ds(pl.multiple_of(to * width, width), width)
            out[0] = above[:, :, lanes]
            out[1] = below[:, :, lanes]

    return pl.pallas_call(
        kernel,
        out_shape=[jax.ShapeDtypeStruct((2, frames, columns, width), above.dtype)] * parts,
        in_specs=[pl.BlockSpec(memory_space=pltpu.SMEM)] + in_vmem(2),
        out_specs=in_vmem(parts),
        compiler_params=pltpu.CompilerParams(vmem_limit_bytes=VMEM_LIMIT),
        name="split_halo_rows",
    )(meta, above, below)


def stack_call(pieces, after):
    def kernel(*refs):
        for i in range(len(pieces)):
            refs[-1][i] = refs[i][...]

    return pl.pallas_call(
        kernel,
        out_shape=jax.ShapeDtypeStruct((len(pieces), *pieces[0].shape), pieces[0].dtype),
        in_specs=in_vmem(len(pieces) + 1),
        out_specs=pl.BlockSpec(memory_space=pltpu.VMEM),
        compiler_params=pltpu.CompilerParams(vmem_limit_bytes=VMEM_LIMIT),
        name="stack_halo_rows",
    )(*pieces, after)


def conv_kernel(jobs, parts, group, frames, out_count, *refs):
    meta, weights, refs = refs[0], refs[1], refs[2:]
    dests = sorted({s for s, _ in jobs})
    any_rim = any(rim for _, rim in jobs)
    held, refs = refs[: len(dests)], refs[len(dests) :]
    before, refs = refs[:parts], refs[parts:]
    if any_rim:
        (rims, rims_before), refs = refs[:2], refs[2:]
    outs, raw = refs[:-1], refs[-1]
    outs = outs[len(outs) - out_count :]
    part, member, z = meta[0], meta[1], meta[2]
    lags, _, width, chans = weights.shape
    _, rows_here, columns, _ = held[0].shape

    first = member == 0
    for n, where in enumerate(dests):
        to = lax.bitwise_xor(part, partner(member, jnp.int32(where)))
        valid = jnp.logical_or(jnp.logical_not(first), to > 0)
        sender = jnp.where(first, group - 1, member - 1)
        want = jnp.where(first, jnp.maximum(to - 1, 0), to)
        place = partner(sender, lax.bitwise_xor(part, want))
        raw[n, frames:, 1 : 1 + rows_here] = held[n][...]
        if any_rim:
            raw[n, frames:, 0] = rims[where, 0]
            raw[n, frames:, 1 + rows_here] = rims[where, 1]
            raw[n, :frames, 0] = rims_before[place, 0]
            raw[n, :frames, 1 + rows_here] = rims_before[place, 1]
        for i in range(parts):

            @pl.when(place == i)
            def _():
                raw[n, :frames, 1 : 1 + rows_here] = before[i][...]

        @pl.when(jnp.logical_not(valid))
        def _():
            raw[n, :frames] = jnp.zeros_like(raw[n, :frames])

    side = 3

    def patches(a, b):
        pieces = []
        for s, rim in jobs:
            n = dests.index(s)
            for p in range(frames):
                f = lax.rem(z + p, frames) + a
                if rim:
                    pieces.append(raw[n, f, b])
                    pieces.append(raw[n, f, rows_here - 1 + b])
                else:
                    pieces.append(raw[n, f, 1 + b : b + rows_here - 1].reshape(-1, width))
        return jnp.concatenate(pieces, axis=0)

    lhs = jnp.concatenate([patches(a, b) for a in range(side) for b in range(side)], axis=1)
    count = lhs.shape[0]
    column = lax.broadcasted_iota(jnp.int32, (count, chans), 0) % columns
    total = None
    for lag in (1, 0, 2):
        product = jnp.dot(
            lhs, weights[lag].reshape(-1, chans), preferred_element_type=jnp.float32
        )
        if lag == 1:
            total = product
        elif lag == 0:
            total = total + jnp.where(column == 0, 0.0, pltpu.roll(product, 1, 0))
        else:
            moved = pltpu.roll(product, count - 1, 0)
            total = total + jnp.where(column == columns - 1, 0.0, moved)
    place = 0
    for out in outs:
        out[...] = total[place : place + out.shape[0]].astype(out.dtype)
        place += out.shape[0]


def conv_call(jobs, meta, weights, held, before, rims, group, frames, out_type, after=()):
    parts = len(held)
    dests = sorted({place for place, _ in jobs})
    _, rows_here, columns, width = held[0].shape
    lags, taps, _, chans = weights.shape
    any_rim = any(rim for _, rim in jobs)
    counts = [frames * (2 if rim else rows_here - 2) * columns for _, rim in jobs]
    total = sum(counts)
    operands = [weights, *[held[n] for n in dests], *before, *(rims if any_rim else ())]
    specs = [pl.BlockSpec(memory_space=pltpu.SMEM)] + in_vmem(len(operands))
    specs += in_vmem(len(after))
    outs = [jax.ShapeDtypeStruct((count, chans), out_type) for count in counts]
    return pl.pallas_call(
        functools.partial(conv_kernel, tuple(jobs), parts, group, frames, len(outs)),
        out_shape=outs,
        in_specs=specs,
        out_specs=in_vmem(len(outs)),
        scratch_shapes=[
            pltpu.VMEM((len(dests), 2 * frames, rows_here + 2, columns, width), jnp.bfloat16)
        ],
        compiler_params=pltpu.CompilerParams(vmem_limit_bytes=VMEM_LIMIT),
        cost_estimate=pl.CostEstimate(
            flops=2 * total * taps * lags * width * chans,
            bytes_accessed=2 * taps * lags * width * chans,
            transcendentals=0,
        ),
        name="conv_rim" if any_rim else "conv_inner",
    )(meta, *operands, *after)


def sum_call(pieces, splits, after=()):
    count, chans = pieces[0].shape
    size = count // splits

    def kernel(*refs):
        for p, out_ref in enumerate(refs[len(refs) - splits :]):
            total = None
            for ref in refs[: len(pieces)]:
                rows = ref[p * size : (p + 1) * size].astype(jnp.float32)
                total = rows if total is None else total + rows
            out_ref[...] = total.astype(out_ref.dtype)

    return pl.pallas_call(
        kernel,
        out_shape=[jax.ShapeDtypeStruct((size, chans), jnp.bfloat16)] * splits,
        in_specs=in_vmem(len(pieces) + len(after)),
        out_specs=in_vmem(splits),
        compiler_params=pltpu.CompilerParams(vmem_limit_bytes=VMEM_LIMIT),
        name="sum_parts",
    )(*pieces, *after)


def attend_kernel(frames, share, chunks, *refs):
    own_count = frames * chunks
    all_count = own_count * share
    tokens, refs = refs[:all_count], refs[all_count:]
    (wq, wk, wv, wo), refs = refs[:4], refs[4:]
    outs, (normed, keys, values) = refs[:frames], refs[frames:]
    size, chans = normed.shape
    per_group = chans // G

    tile_row = lax.broadcasted_iota(jnp.int32, (LANES, LANES), 0) // per_group
    tile_col = lax.broadcasted_iota(jnp.int32, (LANES, LANES), 1) // per_group
    same = (tile_row == tile_col).astype(jnp.float32).astype(jnp.bfloat16)

    def group_mean(sums):
        first = sums.astype(jnp.bfloat16)
        rest = sums - first.astype(jnp.float32)
        second = rest.astype(jnp.bfloat16)
        third = rest - second.astype(jnp.float32)
        tiles = []
        for tile in range(chans // LANES):
            lanes = slice(tile * LANES, (tile + 1) * LANES)
            stacked = jnp.concatenate(
                [
                    first.astype(jnp.float32)[:, lanes],
                    second.astype(jnp.float32)[:, lanes],
                    third[:, lanes],
                ],
                axis=0,
            ).astype(jnp.bfloat16)
            spread = jnp.dot(stacked, same, preferred_element_type=jnp.float32)
            tiles.append(jnp.sum(spread, axis=0, keepdims=True))
        return jnp.concatenate(tiles, axis=1) / (size * per_group)

    def folded(x):
        return jnp.sum(x.reshape(-1, 8, chans), axis=0)

    average = group_mean(sum(folded(ref[...].astype(jnp.float32)) for ref in tokens))

    def spread_of(ref):
        centered = ref[...].astype(jnp.float32) - average
        return folded(centered * centered)

    scale = lax.rsqrt(group_mean(sum(spread_of(ref) for ref in tokens)) + epsilon)
    place = 0
    for ref in tokens:
        rows = ref.shape[0]
        normed[pl.ds(place, rows)] = (
            (ref[...].astype(jnp.float32) - average) * scale
        ).astype(jnp.bfloat16)
        place += rows

    step = min(256, size)
    for start in range(0, size, step):
        x = normed[pl.ds(start, step)]
        keys[pl.ds(start, step)] = jnp.dot(
            x, wk[...], preferred_element_type=jnp.float32
        ).astype(jnp.bfloat16)
        values[pl.ds(start, step)] = jnp.dot(
            x, wv[...], preferred_element_type=jnp.float32
        ).astype(jnp.bfloat16)

    place = 0
    for p, out in enumerate(outs):
        mine = tokens[p * chunks : (p + 1) * chunks]
        rows = sum(ref.shape[0] for ref in mine)
        queries = jnp.dot(
            normed[pl.ds(place, rows)], wq[...], preferred_element_type=jnp.float32
        ).astype(jnp.bfloat16)
        place += rows
        scores = lax.dot_general(
            queries, keys[...], (((1,), (1,)), ((), ())), preferred_element_type=jnp.float32
        ) * chans ** (-0.5)
        row_max = jnp.max(scores, axis=1, keepdims=True)
        exp_weights = jnp.exp(scores - row_max).astype(jnp.bfloat16)
        denominator = jnp.sum(exp_weights.astype(jnp.float32), axis=1, keepdims=True)
        numerator = jnp.dot(exp_weights, values[...], preferred_element_type=jnp.float32)
        attended = (numerator / denominator).astype(jnp.bfloat16)
        added = jnp.dot(attended, wo[...], preferred_element_type=jnp.float32)
        rows_here, columns, _ = out.shape
        inner = mine[0].shape[0]
        first = mine[0][...].astype(jnp.float32) + added[:inner]
        out[1 : rows_here - 1] = first.astype(jnp.bfloat16).reshape(rows_here - 2, columns, chans)
        second = (mine[1][...].astype(jnp.float32) + added[inner:]).astype(jnp.bfloat16)
        out[0] = second[:columns]
        out[rows_here - 1] = second[columns:]


def attend_call(own, others, weights, frames, rows_here, columns):
    chunks = len(own) // frames
    share = 1 + len(others) // len(own)
    chans = own[0].shape[1]
    size = sum(x.shape[0] for x in own) * share
    mine = size // share
    out = jax.ShapeDtypeStruct((rows_here, columns, chans), jnp.bfloat16)
    operands = [*own, *others, *weights]
    return pl.pallas_call(
        functools.partial(attend_kernel, frames, share, chunks),
        out_shape=[out] * frames,
        in_specs=in_vmem(len(operands)),
        out_specs=in_vmem(frames),
        scratch_shapes=[pltpu.VMEM((size, chans), jnp.bfloat16)] * 3,
        compiler_params=pltpu.CompilerParams(vmem_limit_bytes=VMEM_LIMIT),
        cost_estimate=pl.CostEstimate(
            flops=2 * (2 * size * chans * chans + 2 * mine * chans * (chans + size)),
            bytes_accessed=8 * chans * chans + 2 * size * chans,
            transcendentals=mine * size,
        ),
        name="attend",
    )(*operands)


def body(latents, conv_weight, query_weight, key_weight, value_weight, out_weight):
    frames, rows_here, columns, chans = latents.shape
    taps, chans_here, _ = conv_weight.shape
    devices, depth = lax.axis_size("tm"), lax.axis_size("rows")
    sizes = (devices, depth)
    group = LANES // chans_here
    parts = devices // group
    width = group * chans_here
    t_index, z_index = lax.axis_index("tm"), lax.axis_index("rows")
    part, member = t_index // group, t_index % group
    meta = jnp.stack([part, member, z_index]).astype(jnp.int32)

    def permute(block, target):
        return lax.ppermute(block, BOTH, everywhere(sizes, target))

    def to_place(place):
        return lambda t, z: ((t // group ^ partner(t % group, place)) * group + t % group, z)

    def to_member(step):
        return lambda t, z: (t // group * group + (t + step) % group, z)

    split = conv_weight.reshape(taps // 3, 3, chans_here, chans)
    slices = [split] + [permute(split, to_member(step)) for step in range(1, group)]
    weights = merge_call(meta, slices)

    above = permute(latents[:, -1], lambda t, z: (t, z + 1) if z + 1 < depth else None)
    below = permute(latents[:, 0], lambda t, z: (t, z - 1) if z else None)

    held, before = [None] * parts, [None] * parts
    order = [0, 3, 1, 2]
    for place in order:
        start = (part ^ partner(member, jnp.int32(place))) * width
        piece = lax.dynamic_slice_in_dim(latents, start, width, axis=3)
        held[place] = permute(piece, to_place(place)) if place else piece
    held[2], weights = lax.optimization_barrier((held[2], weights))
    for place in order:
        before[place] = permute(held[place], to_member(1))

    conv = functools.partial(
        conv_call,
        meta=meta,
        weights=weights,
        held=held,
        before=before,
        group=group,
        frames=frames,
    )

    def hop(pieces):
        return [permute(x, to_place(1)) for x in pieces]

    rims = split_call(meta, above, below, parts)
    rims = [permute(x, to_place(place)) if place else x for place, x in enumerate(rims)]
    inner_sent = conv([(3, False), (1, False)], rims=None, out_type=jnp.bfloat16)
    inner_got = hop(inner_sent)
    rims = stack_call(rims, inner_sent[0])
    rims = (rims, permute(rims, to_member(1)))
    rim_sent = conv(
        [(3, True), (1, True)], rims=rims, out_type=jnp.bfloat16, after=inner_got[:2]
    )
    rim_got = hop(rim_sent)
    inner_on, inner_own = conv(
        [(2, False), (0, False)], rims=None, out_type=jnp.float32, after=rim_sent[:1]
    )
    (inner_relay,) = sum_call([inner_on, inner_got[0]], 1)
    inner_last = permute(inner_relay, to_place(2))
    rim_on, rim_own = conv(
        [(2, True), (0, True)], rims=rims, out_type=jnp.float32, after=(inner_relay,)
    )
    (rim_relay,) = sum_call([rim_on, rim_got[0]], 1)
    rim_last = permute(rim_relay, to_place(2))
    sums = [
        sum_call([inner_own, inner_got[1], inner_last], frames, after=(rim_relay,)),
        sum_call([rim_own, rim_got[1], rim_last], frames),
    ]

    share = depth // frames

    def frame_home(t, z, p):
        frame = t % CORES * frames + (z + p) % frames
        slot = frame * share + z // frames
        return (t // CORES * CORES + slot % CORES, slot // CORES)

    def next_in_frame(t, z, step):
        slot = z * CORES + t % CORES
        slot = slot // share * share + (slot + step) % share
        return (t // CORES * CORES + slot % CORES, slot // CORES)

    own = []
    for p in range(frames):
        for chunk in sums:
            own.append(permute(chunk[p], lambda t, z: frame_home(t, z, p)))
    others = []
    for step in range(1, share):
        others += [permute(x, lambda t, z: next_in_frame(t, z, step)) for x in own]

    done = attend_call(
        own,
        others,
        (query_weight, key_weight, value_weight, out_weight),
        frames,
        rows_here,
        columns,
    )
    back = []
    for p in range(frames):
        pairs = [(b, a) for a, b in everywhere(sizes, lambda t, z: frame_home(t, z, p))]
        back.append(lax.ppermute(done[p], BOTH, pairs))
    return jnp.stack(
        [
            functools.reduce(
                lambda rest, p: jnp.where((z_index + p) % frames == f, back[p], rest),
                range(1, frames),
                back[0],
            )
            for f in range(frames)
        ]
    )


def solution(mesh):
    placed = (P("tm", "rows", None, None), P(None, "tm", None), P(), P(), P(), P())
    return jax.shard_map(
        body, mesh=mesh, in_specs=placed, out_specs=P("tm", "rows", None, None), check_vma=False
    )
```

```python
import functools

import jax
import jax.numpy as jnp
from jax import lax
from jax.experimental import pallas as pl
from jax.experimental.pallas import tpu as pltpu
from jax.sharding import PartitionSpec as P

G = 32
LANES = 128
CORES = 2

epsilon = 1e-06

BOTH = ("tm", "rows")
VMEM_LIMIT = 32 * 1024 * 1024


def everywhere(sizes, target):
    devices, depth = sizes
    pairs = []
    for t in range(devices):
        for z in range(depth):
            to = target(t, z)
            if to is not None:
                pairs.append((t * depth + z, to[0] * depth + to[1]))
    return pairs


def in_vmem(count):
    return [pl.BlockSpec(memory_space=pltpu.VMEM)] * count


def merge_kernel(group, *refs):
    meta, refs = refs[0], refs[1:]
    slices, out, sems = refs[:group], refs[group], refs[group + 1]
    chans_here = slices[0].shape[2]
    copies = []
    for lag in range(out.shape[0]):
        for step in range(group):
            owner = lax.rem(meta[1] - step + group, group)
            rows = pl.ds(pl.multiple_of(owner * chans_here, 16), chans_here)
            copies.append(
                pltpu.make_async_copy(
                    slices[step].at[:, lag], out.at[lag, :, rows], sems.at[lag, step]
                )
            )
    for copy in copies:
        copy.start()
    for copy in copies:
        copy.wait()


def merge_call(meta, slices):
    group = len(slices)
    taps, lags, chans_here, chans = slices[0].shape
    return pl.pallas_call(
        functools.partial(merge_kernel, group),
        out_shape=jax.ShapeDtypeStruct((lags, taps, group * chans_here, chans), jnp.bfloat16),
        in_specs=[pl.BlockSpec(memory_space=pltpu.SMEM)]
        + [pl.BlockSpec(memory_space=pl.ANY)] * group,
        out_specs=pl.BlockSpec(memory_space=pltpu.VMEM),
        scratch_shapes=[pltpu.SemaphoreType.DMA((lags, group))],
        compiler_params=pltpu.CompilerParams(vmem_limit_bytes=VMEM_LIMIT),
        name="merge_kernel_slices",
    )(meta, *slices)


def halo_call(pieces, after):
    frames, rows_here, columns, width = pieces[0].shape
    out = jax.ShapeDtypeStruct((len(pieces), frames, columns, width), jnp.bfloat16)

    def kernel(*refs):
        first, last = refs[-2:]
        for i in range(len(pieces)):
            first[i] = refs[i][:, 0]
            last[i] = refs[i][:, rows_here - 1]

    return pl.pallas_call(
        kernel,
        out_shape=[out] * 2,
        in_specs=in_vmem(len(pieces)) + [pl.BlockSpec(memory_space=pl.ANY)],
        out_specs=in_vmem(2),
        compiler_params=pltpu.CompilerParams(vmem_limit_bytes=VMEM_LIMIT),
        name="halo_rows",
    )(*pieces, after)


def conv_kernel(jobs, parts, frames, *refs):
    meta, weights, refs = refs[0], refs[1], refs[2:]
    dests = sorted({s for s, _ in jobs})
    any_rim = any(rim for _, rim in jobs)
    held, refs = refs[: len(dests)], refs[len(dests) :]
    before, refs = refs[:parts], refs[parts:]
    if any_rim:
        (above, below), refs = refs[:2], refs[2:]
    outs, raw = refs[-1 - len(jobs) : -1], refs[-1]
    part, member, z = meta[0], meta[1], meta[2]
    lags, _, width, chans = weights.shape
    _, rows_here, columns, _ = held[0].shape

    for n, s in enumerate(dests):
        to = lax.bitwise_xor(part, s)
        wraps = member == 0
        place = jnp.where(wraps, lax.bitwise_xor(part, jnp.maximum(to - 1, 0)), s)
        valid = jnp.logical_or(jnp.logical_not(wraps), to > 0)
        raw[n, frames:, 1 : 1 + rows_here] = held[n][...]
        if any_rim:
            raw[n, frames:, 0] = above[s]
            raw[n, frames:, 1 + rows_here] = below[s]
            raw[n, :frames, 0] = above[parts + place]
            raw[n, :frames, 1 + rows_here] = below[parts + place]
        for i in range(parts):

            @pl.when(place == i)
            def _():
                raw[n, :frames, 1 : 1 + rows_here] = before[i][...]

        @pl.when(jnp.logical_not(valid))
        def _():
            raw[n, :frames] = jnp.zeros_like(raw[n, :frames])

    side = 3

    def patches(a, b):
        pieces = []
        for s, rim in jobs:
            n = dests.index(s)
            for p in range(frames):
                f = lax.rem(z + p, frames) + a
                if rim:
                    pieces.append(raw[n, f, b])
                    pieces.append(raw[n, f, rows_here - 1 + b])
                else:
                    pieces.append(raw[n, f, 1 + b : b + rows_here - 1].reshape(-1, width))
        return jnp.concatenate(pieces, axis=0)

    lhs = jnp.concatenate([patches(a, b) for a in range(side) for b in range(side)], axis=1)
    count = lhs.shape[0]
    column = lax.broadcasted_iota(jnp.int32, (count, chans), 0) % columns
    total = None
    for lag in (1, 0, 2):
        product = jnp.dot(
            lhs, weights[lag].reshape(-1, chans), preferred_element_type=jnp.float32
        )
        if lag == 1:
            total = product
        elif lag == 0:
            total = total + jnp.where(column == 0, 0.0, pltpu.roll(product, 1, 0))
        else:
            moved = pltpu.roll(product, count - 1, 0)
            total = total + jnp.where(column == columns - 1, 0.0, moved)
    place = 0
    for out in outs:
        out[...] = total[place : place + out.shape[0]].astype(out.dtype)
        place += out.shape[0]


def conv_call(jobs, meta, weights, held, before, halos, frames, out_type, after=()):
    parts = len(held)
    dests = sorted({s for s, _ in jobs})
    _, rows_here, columns, width = held[0].shape
    lags, taps, _, chans = weights.shape
    any_rim = any(rim for _, rim in jobs)
    counts = [frames * (2 if rim else rows_here - 2) * columns for _, rim in jobs]
    operands = [weights, *[held[s] for s in dests], *before, *(halos if any_rim else ())]
    specs = [pl.BlockSpec(memory_space=pltpu.SMEM)] + in_vmem(len(operands))
    specs += [pl.BlockSpec(memory_space=pl.ANY)] * len(after)
    return pl.pallas_call(
        functools.partial(conv_kernel, tuple(jobs), parts, frames),
        out_shape=[jax.ShapeDtypeStruct((count, chans), out_type) for count in counts],
        in_specs=specs,
        out_specs=in_vmem(len(jobs)),
        scratch_shapes=[
            pltpu.VMEM((len(dests), 2 * frames, rows_here + 2, columns, width), jnp.bfloat16)
        ],
        compiler_params=pltpu.CompilerParams(vmem_limit_bytes=VMEM_LIMIT),
        cost_estimate=pl.CostEstimate(
            flops=2 * sum(counts) * taps * lags * width * chans,
            bytes_accessed=2 * taps * lags * width * chans,
            transcendentals=0,
        ),
        name="conv_rim" if any_rim else "conv_inner",
    )(meta, *operands, *after)


def sum_call(pieces, frames):
    count, chans = pieces[0].shape
    out = jax.ShapeDtypeStruct((count // frames, chans), jnp.bfloat16)

    def kernel(*refs):
        ins, outs = refs[: len(pieces)], refs[len(pieces) :]
        for p, out_ref in enumerate(outs):
            size = out_ref.shape[0]
            total = ins[0][pl.ds(p * size, size)].astype(jnp.float32)
            for ref in ins[1:]:
                total = total + ref[pl.ds(p * size, size)].astype(jnp.float32)
            out_ref[...] = total.astype(out_ref.dtype)

    return pl.pallas_call(
        kernel,
        out_shape=[out] * frames,
        in_specs=in_vmem(len(pieces)),
        out_specs=in_vmem(frames),
        compiler_params=pltpu.CompilerParams(vmem_limit_bytes=VMEM_LIMIT),
        name="sum_parts",
    )(*pieces)


def attend_kernel(frames, share, chunks, *refs):
    own_count = frames * chunks
    all_count = own_count * share
    tokens, refs = refs[:all_count], refs[all_count:]
    (wq, wk, wv, wo), refs = refs[:4], refs[4:]
    outs, (normed, keys, values) = refs[:frames], refs[frames:]
    size, chans = normed.shape
    per_group = chans // G

    tile_row = lax.broadcasted_iota(jnp.int32, (LANES, LANES), 0) // per_group
    tile_col = lax.broadcasted_iota(jnp.int32, (LANES, LANES), 1) // per_group
    same = (tile_row == tile_col).astype(jnp.float32).astype(jnp.bfloat16)

    def group_mean(sums):
        first = sums.astype(jnp.bfloat16)
        rest = sums - first.astype(jnp.float32)
        second = rest.astype(jnp.bfloat16)
        third = rest - second.astype(jnp.float32)
        tiles = []
        for tile in range(chans // LANES):
            lanes = slice(tile * LANES, (tile + 1) * LANES)
            stacked = jnp.concatenate(
                [
                    first.astype(jnp.float32)[:, lanes],
                    second.astype(jnp.float32)[:, lanes],
                    third[:, lanes],
                ],
                axis=0,
            ).astype(jnp.bfloat16)
            spread = jnp.dot(stacked, same, preferred_element_type=jnp.float32)
            tiles.append(jnp.sum(spread, axis=0, keepdims=True))
        return jnp.concatenate(tiles, axis=1) / (size * per_group)

    def folded(x):
        return jnp.sum(x.reshape(-1, 8, chans), axis=0)

    average = group_mean(sum(folded(ref[...].astype(jnp.float32)) for ref in tokens))

    def spread_of(ref):
        centered = ref[...].astype(jnp.float32) - average
        return folded(centered * centered)

    scale = lax.rsqrt(group_mean(sum(spread_of(ref) for ref in tokens)) + epsilon)
    place = 0
    for ref in tokens:
        rows = ref.shape[0]
        normed[pl.ds(place, rows)] = (
            (ref[...].astype(jnp.float32) - average) * scale
        ).astype(jnp.bfloat16)
        place += rows

    step = min(256, size)
    for start in range(0, size, step):
        x = normed[pl.ds(start, step)]
        keys[pl.ds(start, step)] = jnp.dot(
            x, wk[...], preferred_element_type=jnp.float32
        ).astype(jnp.bfloat16)
        values[pl.ds(start, step)] = jnp.dot(
            x, wv[...], preferred_element_type=jnp.float32
        ).astype(jnp.bfloat16)

    place = 0
    for p, out in enumerate(outs):
        mine = tokens[p * chunks : (p + 1) * chunks]
        rows = sum(ref.shape[0] for ref in mine)
        queries = jnp.dot(
            normed[pl.ds(place, rows)], wq[...], preferred_element_type=jnp.float32
        ).astype(jnp.bfloat16)
        place += rows
        scores = lax.dot_general(
            queries, keys[...], (((1,), (1,)), ((), ())), preferred_element_type=jnp.float32
        ) * chans ** (-0.5)
        row_max = jnp.max(scores, axis=1, keepdims=True)
        exp_weights = jnp.exp(scores - row_max).astype(jnp.bfloat16)
        denominator = jnp.sum(exp_weights.astype(jnp.float32), axis=1, keepdims=True)
        numerator = jnp.dot(exp_weights, values[...], preferred_element_type=jnp.float32)
        attended = (numerator / denominator).astype(jnp.bfloat16)
        added = jnp.dot(attended, wo[...], preferred_element_type=jnp.float32)
        rows_here, columns, _ = out.shape
        inner = mine[0].shape[0]
        first = mine[0][...].astype(jnp.float32) + added[:inner]
        out[1 : rows_here - 1] = first.astype(jnp.bfloat16).reshape(rows_here - 2, columns, chans)
        second = (mine[1][...].astype(jnp.float32) + added[inner:]).astype(jnp.bfloat16)
        out[0] = second[:columns]
        out[rows_here - 1] = second[columns:]


def attend_call(own, others, weights, frames, rows_here, columns):
    chunks = len(own) // frames
    share = 1 + len(others) // len(own)
    chans = own[0].shape[1]
    size = sum(x.shape[0] for x in own) * share
    mine = size // share
    out = jax.ShapeDtypeStruct((rows_here, columns, chans), jnp.bfloat16)
    operands = [*own, *others, *weights]
    return pl.pallas_call(
        functools.partial(attend_kernel, frames, share, chunks),
        out_shape=[out] * frames,
        in_specs=in_vmem(len(operands)),
        out_specs=in_vmem(frames),
        scratch_shapes=[pltpu.VMEM((size, chans), jnp.bfloat16)] * 3,
        compiler_params=pltpu.CompilerParams(vmem_limit_bytes=VMEM_LIMIT),
        cost_estimate=pl.CostEstimate(
            flops=2 * (2 * size * chans * chans + 2 * mine * chans * (chans + size)),
            bytes_accessed=8 * chans * chans + 2 * size * chans,
            transcendentals=mine * size,
        ),
        name="attend",
    )(*operands)


def body(latents, conv_weight, query_weight, key_weight, value_weight, out_weight):
    frames, rows_here, columns, chans = latents.shape
    taps, chans_here, _ = conv_weight.shape
    devices, depth = lax.axis_size("tm"), lax.axis_size("rows")
    sizes = (devices, depth)
    group = LANES // chans_here
    parts = devices // group
    width = group * chans_here
    t_index, z_index = lax.axis_index("tm"), lax.axis_index("rows")
    part, member = t_index // group, t_index % group
    meta = jnp.stack([part, member, z_index]).astype(jnp.int32)

    def permute(block, target):
        return lax.ppermute(block, BOTH, everywhere(sizes, target))

    def to_part(s):
        return lambda t, z: ((t // group ^ s) * group + t % group, z)

    def to_member(step):
        return lambda t, z: (t // group * group + (t + step) % group, z)

    held, before = [None] * parts, [None] * parts
    for s in reversed(range(parts)):
        piece = lax.dynamic_slice_in_dim(latents, (part ^ s) * width, width, axis=3)
        held[s] = permute(piece, to_part(s)) if s else piece
    for s in range(parts):
        before[s] = permute(held[s], to_member(1))

    split = conv_weight.reshape(taps // 3, 3, chans_here, chans)
    slices = [split] + [permute(split, to_member(step)) for step in range(1, group)]
    weights = merge_call(meta, slices)

    away = list(reversed(range(1, parts)))
    conv = functools.partial(
        conv_call, meta=meta, weights=weights, held=held, before=before, frames=frames
    )
    inner = conv([(s, False) for s in away[:1]], halos=None, out_type=jnp.bfloat16)
    first, last = halo_call([*held, *before], inner[0])
    halos = (
        permute(last, lambda t, z: (t, z + 1) if z + 1 < depth else None),
        permute(first, lambda t, z: (t, z - 1) if z else None),
    )
    inner += conv([(s, False) for s in away[1:]], halos=None, out_type=jnp.bfloat16)
    rim = conv([(s, True) for s in away], halos=halos, out_type=jnp.bfloat16, after=inner[-1:])
    mine = conv([(0, False), (0, True)], halos=halos, out_type=jnp.float32, after=rim[-1:])
    sums = []
    for sent, own_part in ((inner, mine[0]), (rim, mine[1])):
        got = [permute(x, to_part(s)) for s, x in zip(away, sent)]
        sums.append(sum_call([own_part, *got], frames))

    share = depth // frames

    def frame_home(t, z, p):
        frame = t % CORES * frames + (z + p) % frames
        slot = frame * share + z // frames
        return (t // CORES * CORES + slot % CORES, slot // CORES)

    def next_in_frame(t, z, step):
        slot = z * CORES + t % CORES
        slot = slot // share * share + (slot + step) % share
        return (t // CORES * CORES + slot % CORES, slot // CORES)

    own = []
    for p in range(frames):
        for chunk in sums:
            own.append(permute(chunk[p], lambda t, z: frame_home(t, z, p)))
    others = []
    for step in range(1, share):
        others += [permute(x, lambda t, z: next_in_frame(t, z, step)) for x in own]

    done = attend_call(
        own,
        others,
        (query_weight, key_weight, value_weight, out_weight),
        frames,
        rows_here,
        columns,
    )
    back = []
    for p in range(frames):
        pairs = [(b, a) for a, b in everywhere(sizes, lambda t, z: frame_home(t, z, p))]
        back.append(lax.ppermute(done[p], BOTH, pairs))
    return jnp.stack(
        [
            functools.reduce(
                lambda rest, p: jnp.where((z_index + p) % frames == f, back[p], rest),
                range(1, frames),
                back[0],
            )
            for f in range(frames)
        ]
    )


def solution(mesh):
    placed = (P("tm", "rows", None, None), P(None, "tm", None), P(), P(), P(), P())
    return jax.shard_map(
        body, mesh=mesh, in_specs=placed, out_specs=P("tm", "rows", None, None), check_vma=False
    )
```

```python
import functools

import jax
import jax.numpy as jnp
from jax import lax
from jax.experimental import pallas as pl
from jax.experimental.pallas import tpu as pltpu
from jax.sharding import PartitionSpec as P

G = 32
LANES = 128
CORES = 2

epsilon = 1e-06

BOTH = ("tm", "rows")
VMEM_LIMIT = 32 * 1024 * 1024


def everywhere(sizes, target):
    devices, depth = sizes
    pairs = []
    for t in range(devices):
        for z in range(depth):
            to = target(t, z)
            if to is not None:
                pairs.append((t * depth + z, to[0] * depth + to[1]))
    return pairs


def in_vmem(count):
    return [pl.BlockSpec(memory_space=pltpu.VMEM)] * count


def merge_kernel(group, *refs):
    meta, refs = refs[0], refs[1:]
    slices, out, sems = refs[:group], refs[group], refs[group + 1]
    chans_here = slices[0].shape[2]
    copies = []
    for lag in range(out.shape[0]):
        for step in range(group):
            owner = lax.rem(meta[1] - step + group, group)
            rows = pl.ds(pl.multiple_of(owner * chans_here, 16), chans_here)
            copies.append(
                pltpu.make_async_copy(
                    slices[step].at[:, lag], out.at[lag, :, rows], sems.at[lag, step]
                )
            )
    for copy in copies:
        copy.start()
    for copy in copies:
        copy.wait()


def merge_call(meta, slices):
    group = len(slices)
    taps, lags, chans_here, chans = slices[0].shape
    return pl.pallas_call(
        functools.partial(merge_kernel, group),
        out_shape=jax.ShapeDtypeStruct((lags, taps, group * chans_here, chans), jnp.bfloat16),
        in_specs=[pl.BlockSpec(memory_space=pltpu.SMEM)]
        + [pl.BlockSpec(memory_space=pltpu.HBM)]
        + [pl.BlockSpec(memory_space=pl.ANY)] * (group - 1),
        out_specs=pl.BlockSpec(memory_space=pltpu.VMEM),
        scratch_shapes=[pltpu.SemaphoreType.DMA((lags, group))],
        compiler_params=pltpu.CompilerParams(vmem_limit_bytes=VMEM_LIMIT),
        name="merge_kernel_slices",
    )(meta, *slices)


def partner(member, place):
    odd = member % 2 == 1
    if isinstance(member, int) and isinstance(place, int):
        return 3 - place if odd and place in (1, 2) else place
    swapped = jnp.where(jnp.logical_or(place == 1, place == 2), 3 - place, place)
    return jnp.where(odd, swapped, place)


def split_call(meta, above, below, parts):
    frames, columns, chans = above.shape
    width = chans // parts

    def kernel(meta, above, below, *outs):
        for place, out in enumerate(outs):
            to = lax.bitwise_xor(meta[0], partner(meta[1], jnp.int32(place)))
            lanes = pl.ds(pl.multiple_of(to * width, width), width)
            out[0] = above[:, :, lanes]
            out[1] = below[:, :, lanes]

    return pl.pallas_call(
        kernel,
        out_shape=[jax.ShapeDtypeStruct((2, frames, columns, width), above.dtype)] * parts,
        in_specs=[pl.BlockSpec(memory_space=pltpu.SMEM)] + in_vmem(2),
        out_specs=in_vmem(parts),
        compiler_params=pltpu.CompilerParams(vmem_limit_bytes=VMEM_LIMIT),
        name="split_halo_rows",
    )(meta, above, below)


def stack_call(pieces, after):
    def kernel(*refs):
        for i in range(len(pieces)):
            refs[-1][i] = refs[i][...]

    return pl.pallas_call(
        kernel,
        out_shape=jax.ShapeDtypeStruct((len(pieces), *pieces[0].shape), pieces[0].dtype),
        in_specs=in_vmem(len(pieces) + 1),
        out_specs=pl.BlockSpec(memory_space=pltpu.VMEM),
        compiler_params=pltpu.CompilerParams(vmem_limit_bytes=VMEM_LIMIT),
        name="stack_halo_rows",
    )(*pieces, after)


def conv_kernel(jobs, parts, group, frames, out_count, *refs):
    meta, weights, refs = refs[0], refs[1], refs[2:]
    dests = sorted({s for s, _ in jobs})
    any_rim = any(rim for _, rim in jobs)
    held, refs = refs[: len(dests)], refs[len(dests) :]
    before, refs = refs[:parts], refs[parts:]
    if any_rim:
        (rims, rims_before), refs = refs[:2], refs[2:]
    outs, raw = refs[:-1], refs[-1]
    outs = outs[len(outs) - out_count :]
    part, member, z = meta[0], meta[1], meta[2]
    lags, _, width, chans = weights.shape
    _, rows_here, columns, _ = held[0].shape

    first = member == 0
    for n, where in enumerate(dests):
        to = lax.bitwise_xor(part, partner(member, jnp.int32(where)))
        valid = jnp.logical_or(jnp.logical_not(first), to > 0)
        sender = jnp.where(first, group - 1, member - 1)
        want = jnp.where(first, jnp.maximum(to - 1, 0), to)
        place = partner(sender, lax.bitwise_xor(part, want))
        raw[n, frames:, 1 : 1 + rows_here] = held[n][...]
        if any_rim:
            raw[n, frames:, 0] = rims[where, 0]
            raw[n, frames:, 1 + rows_here] = rims[where, 1]
            raw[n, :frames, 0] = rims_before[place, 0]
            raw[n, :frames, 1 + rows_here] = rims_before[place, 1]
        for i in range(parts):

            @pl.when(place == i)
            def _():
                raw[n, :frames, 1 : 1 + rows_here] = before[i][...]

        @pl.when(jnp.logical_not(valid))
        def _():
            raw[n, :frames] = jnp.zeros_like(raw[n, :frames])

    side = 3

    def patches(a, b):
        pieces = []
        for s, rim in jobs:
            n = dests.index(s)
            for p in range(frames):
                f = lax.rem(z + p, frames) + a
                if rim:
                    pieces.append(raw[n, f, b])
                    pieces.append(raw[n, f, rows_here - 1 + b])
                else:
                    pieces.append(raw[n, f, 1 + b : b + rows_here - 1].reshape(-1, width))
        return jnp.concatenate(pieces, axis=0)

    lhs = jnp.concatenate([patches(a, b) for a in range(side) for b in range(side)], axis=1)
    count = lhs.shape[0]
    column = lax.broadcasted_iota(jnp.int32, (count, chans), 0) % columns
    total = None
    for lag in (1, 0, 2):
        product = jnp.dot(
            lhs, weights[lag].reshape(-1, chans), preferred_element_type=jnp.float32
        )
        if lag == 1:
            total = product
        elif lag == 0:
            total = total + jnp.where(column == 0, 0.0, pltpu.roll(product, 1, 0))
        else:
            moved = pltpu.roll(product, count - 1, 0)
            total = total + jnp.where(column == columns - 1, 0.0, moved)
    place = 0
    for out in outs:
        out[...] = total[place : place + out.shape[0]].astype(out.dtype)
        place += out.shape[0]


def conv_call(jobs, meta, weights, held, before, rims, group, frames, out_type, after=()):
    parts = len(held)
    dests = sorted({place for place, _ in jobs})
    _, rows_here, columns, width = held[0].shape
    lags, taps, _, chans = weights.shape
    any_rim = any(rim for _, rim in jobs)
    counts = [frames * (2 if rim else rows_here - 2) * columns for _, rim in jobs]
    total = sum(counts)
    operands = [weights, *[held[n] for n in dests], *before, *(rims if any_rim else ())]
    specs = [pl.BlockSpec(memory_space=pltpu.SMEM)] + in_vmem(len(operands))
    specs += in_vmem(len(after))
    outs = [jax.ShapeDtypeStruct((count, chans), out_type) for count in counts]
    return pl.pallas_call(
        functools.partial(conv_kernel, tuple(jobs), parts, group, frames, len(outs)),
        out_shape=outs,
        in_specs=specs,
        out_specs=in_vmem(len(outs)),
        scratch_shapes=[
            pltpu.VMEM((len(dests), 2 * frames, rows_here + 2, columns, width), jnp.bfloat16)
        ],
        compiler_params=pltpu.CompilerParams(vmem_limit_bytes=VMEM_LIMIT),
        cost_estimate=pl.CostEstimate(
            flops=2 * total * taps * lags * width * chans,
            bytes_accessed=2 * taps * lags * width * chans,
            transcendentals=0,
        ),
        name="conv_rim" if any_rim else "conv_inner",
    )(meta, *operands, *after)


def sum_call(pieces, splits, after=()):
    count, chans = pieces[0].shape
    size = count // splits

    def kernel(*refs):
        for p, out_ref in enumerate(refs[len(refs) - splits :]):
            total = None
            for ref in refs[: len(pieces)]:
                rows = ref[p * size : (p + 1) * size].astype(jnp.float32)
                total = rows if total is None else total + rows
            out_ref[...] = total.astype(out_ref.dtype)

    return pl.pallas_call(
        kernel,
        out_shape=[jax.ShapeDtypeStruct((size, chans), jnp.bfloat16)] * splits,
        in_specs=in_vmem(len(pieces) + len(after)),
        out_specs=in_vmem(splits),
        compiler_params=pltpu.CompilerParams(vmem_limit_bytes=VMEM_LIMIT),
        name="sum_parts",
    )(*pieces, *after)


def attend_kernel(frames, share, chunks, *refs):
    own_count = frames * chunks
    all_count = own_count * share
    tokens, refs = refs[:all_count], refs[all_count:]
    (wq, wk, wv, wo), refs = refs[:4], refs[4:]
    outs, (normed, keys, values) = refs[:frames], refs[frames:]
    size, chans = normed.shape
    per_group = chans // G

    tile_row = lax.broadcasted_iota(jnp.int32, (LANES, LANES), 0) // per_group
    tile_col = lax.broadcasted_iota(jnp.int32, (LANES, LANES), 1) // per_group
    same = (tile_row == tile_col).astype(jnp.float32).astype(jnp.bfloat16)

    def group_mean(sums):
        first = sums.astype(jnp.bfloat16)
        rest = sums - first.astype(jnp.float32)
        second = rest.astype(jnp.bfloat16)
        third = rest - second.astype(jnp.float32)
        tiles = []
        for tile in range(chans // LANES):
            lanes = slice(tile * LANES, (tile + 1) * LANES)
            stacked = jnp.concatenate(
                [
                    first.astype(jnp.float32)[:, lanes],
                    second.astype(jnp.float32)[:, lanes],
                    third[:, lanes],
                ],
                axis=0,
            ).astype(jnp.bfloat16)
            spread = jnp.dot(stacked, same, preferred_element_type=jnp.float32)
            tiles.append(jnp.sum(spread, axis=0, keepdims=True))
        return jnp.concatenate(tiles, axis=1) / (size * per_group)

    def folded(x):
        return jnp.sum(x.reshape(-1, 8, chans), axis=0)

    average = group_mean(sum(folded(ref[...].astype(jnp.float32)) for ref in tokens))

    def spread_of(ref):
        centered = ref[...].astype(jnp.float32) - average
        return folded(centered * centered)

    scale = lax.rsqrt(group_mean(sum(spread_of(ref) for ref in tokens)) + epsilon)
    place = 0
    for ref in tokens:
        rows = ref.shape[0]
        normed[pl.ds(place, rows)] = (
            (ref[...].astype(jnp.float32) - average) * scale
        ).astype(jnp.bfloat16)
        place += rows

    step = min(256, size)
    for start in range(0, size, step):
        x = normed[pl.ds(start, step)]
        keys[pl.ds(start, step)] = jnp.dot(
            x, wk[...], preferred_element_type=jnp.float32
        ).astype(jnp.bfloat16)
        values[pl.ds(start, step)] = jnp.dot(
            x, wv[...], preferred_element_type=jnp.float32
        ).astype(jnp.bfloat16)

    place = 0
    for p, out in enumerate(outs):
        mine = tokens[p * chunks : (p + 1) * chunks]
        rows = sum(ref.shape[0] for ref in mine)
        queries = jnp.dot(
            normed[pl.ds(place, rows)], wq[...], preferred_element_type=jnp.float32
        ).astype(jnp.bfloat16)
        place += rows
        scores = lax.dot_general(
            queries, keys[...], (((1,), (1,)), ((), ())), preferred_element_type=jnp.float32
        ) * chans ** (-0.5)
        row_max = jnp.max(scores, axis=1, keepdims=True)
        exp_weights = jnp.exp(scores - row_max).astype(jnp.bfloat16)
        denominator = jnp.sum(exp_weights.astype(jnp.float32), axis=1, keepdims=True)
        numerator = jnp.dot(exp_weights, values[...], preferred_element_type=jnp.float32)
        attended = (numerator / denominator).astype(jnp.bfloat16)
        added = jnp.dot(attended, wo[...], preferred_element_type=jnp.float32)
        rows_here, columns, _ = out.shape
        inner = mine[0].shape[0]
        first = mine[0][...].astype(jnp.float32) + added[:inner]
        out[1 : rows_here - 1] = first.astype(jnp.bfloat16).reshape(rows_here - 2, columns, chans)
        second = (mine[1][...].astype(jnp.float32) + added[inner:]).astype(jnp.bfloat16)
        out[0] = second[:columns]
        out[rows_here - 1] = second[columns:]


def attend_call(own, others, weights, frames, rows_here, columns):
    chunks = len(own) // frames
    share = 1 + len(others) // len(own)
    chans = own[0].shape[1]
    size = sum(x.shape[0] for x in own) * share
    mine = size // share
    out = jax.ShapeDtypeStruct((rows_here, columns, chans), jnp.bfloat16)
    operands = [*own, *others, *weights]
    return pl.pallas_call(
        functools.partial(attend_kernel, frames, share, chunks),
        out_shape=[out] * frames,
        in_specs=in_vmem(len(operands)),
        out_specs=in_vmem(frames),
        scratch_shapes=[pltpu.VMEM((size, chans), jnp.bfloat16)] * 3,
        compiler_params=pltpu.CompilerParams(vmem_limit_bytes=VMEM_LIMIT),
        cost_estimate=pl.CostEstimate(
            flops=2 * (2 * size * chans * chans + 2 * mine * chans * (chans + size)),
            bytes_accessed=8 * chans * chans + 2 * size * chans,
            transcendentals=mine * size,
        ),
        name="attend",
    )(*operands)


def body(latents, conv_weight, query_weight, key_weight, value_weight, out_weight):
    frames, rows_here, columns, chans = latents.shape
    taps, chans_here, _ = conv_weight.shape
    devices, depth = lax.axis_size("tm"), lax.axis_size("rows")
    sizes = (devices, depth)
    group = LANES // chans_here
    parts = devices // group
    width = group * chans_here
    t_index, z_index = lax.axis_index("tm"), lax.axis_index("rows")
    part, member = t_index // group, t_index % group
    meta = jnp.stack([part, member, z_index]).astype(jnp.int32)

    def permute(block, target):
        return lax.ppermute(block, BOTH, everywhere(sizes, target))

    def to_place(place):
        return lambda t, z: ((t // group ^ partner(t % group, place)) * group + t % group, z)

    def to_member(step):
        return lambda t, z: (t // group * group + (t + step) % group, z)

    split = conv_weight.reshape(taps // 3, 3, chans_here, chans)
    slices = [split] + [permute(split, to_member(step)) for step in range(1, group)]
    weights = merge_call(meta, slices)

    above = permute(latents[:, -1], lambda t, z: (t, z + 1) if z + 1 < depth else None)
    below = permute(latents[:, 0], lambda t, z: (t, z - 1) if z else None)

    held, before = [None] * parts, [None] * parts
    order = [0, 3, 1, 2]
    for place in order:
        start = (part ^ partner(member, jnp.int32(place))) * width
        piece = lax.dynamic_slice_in_dim(latents, start, width, axis=3)
        held[place] = permute(piece, to_place(place)) if place else piece
    held[2], weights = lax.optimization_barrier((held[2], weights))
    for place in order:
        before[place] = permute(held[place], to_member(1))

    conv = functools.partial(
        conv_call,
        meta=meta,
        weights=weights,
        held=held,
        before=before,
        group=group,
        frames=frames,
    )

    def hop(pieces):
        return [permute(x, to_place(1)) for x in pieces]

    rims = split_call(meta, above, below, parts)
    rims = [permute(x, to_place(place)) if place else x for place, x in enumerate(rims)]
    inner_sent = conv([(3, False), (1, False)], rims=None, out_type=jnp.bfloat16)
    inner_got = hop(inner_sent)
    rims = stack_call(rims, inner_sent[0])
    rims = (rims, permute(rims, to_member(1)))
    rim_sent = conv(
        [(3, True), (1, True)], rims=rims, out_type=jnp.bfloat16, after=inner_got[:0]
    )
    rim_got = hop(rim_sent)
    inner_on, inner_own = conv(
        [(2, False), (0, False)], rims=None, out_type=jnp.float32, after=rim_sent[:1]
    )
    (inner_relay,) = sum_call([inner_on, inner_got[0]], 1)
    inner_last = permute(inner_relay, to_place(2))
    rim_on, rim_own = conv(
        [(2, True), (0, True)], rims=rims, out_type=jnp.float32, after=(inner_relay,)
    )
    (rim_relay,) = sum_call([rim_on, rim_got[0]], 1)
    rim_last = permute(rim_relay, to_place(2))
    sums = [
        sum_call([inner_own, inner_got[1], inner_last], frames, after=(rim_relay,)),
        sum_call([rim_own, rim_got[1], rim_last], frames),
    ]

    share = depth // frames

    def frame_home(t, z, p):
        frame = t % CORES * frames + (z + p) % frames
        slot = frame * share + z // frames
        return (t // CORES * CORES + slot % CORES, slot // CORES)

    def next_in_frame(t, z, step):
        slot = z * CORES + t % CORES
        slot = slot // share * share + (slot + step) % share
        return (t // CORES * CORES + slot % CORES, slot // CORES)

    own = []
    for p in range(frames):
        for chunk in sums:
            own.append(permute(chunk[p], lambda t, z: frame_home(t, z, p)))
    others = []
    for step in range(1, share):
        others += [permute(x, lambda t, z: next_in_frame(t, z, step)) for x in own]

    done = attend_call(
        own,
        others,
        (query_weight, key_weight, value_weight, out_weight),
        frames,
        rows_here,
        columns,
    )
    back = []
    for p in range(frames):
        pairs = [(b, a) for a, b in everywhere(sizes, lambda t, z: frame_home(t, z, p))]
        back.append(lax.ppermute(done[p], BOTH, pairs))
    return jnp.stack(
        [
            functools.reduce(
                lambda rest, p: jnp.where((z_index + p) % frames == f, back[p], rest),
                range(1, frames),
                back[0],
            )
            for f in range(frames)
        ]
    )


def solution(mesh):
    placed = (P("tm", "rows", None, None), P(None, "tm", None), P(), P(), P(), P())
    return jax.shard_map(
        body, mesh=mesh, in_specs=placed, out_specs=P("tm", "rows", None, None), check_vma=False
    )
```

```python
import functools

import jax
import jax.numpy as jnp
from jax import lax
from jax.experimental import pallas as pl
from jax.experimental.pallas import tpu as pltpu
from jax.sharding import PartitionSpec as P

G = 32
LANES = 128
CORES = 2

epsilon = 1e-06

BOTH = ("tm", "rows")
VMEM_LIMIT = 32 * 1024 * 1024


def everywhere(sizes, target):
    devices, depth = sizes
    pairs = []
    for t in range(devices):
        for z in range(depth):
            to = target(t, z)
            if to is not None:
                pairs.append((t * depth + z, to[0] * depth + to[1]))
    return pairs


def in_vmem(count):
    return [pl.BlockSpec(memory_space=pltpu.VMEM)] * count


def merge_kernel(group, *refs):
    meta, refs = refs[0], refs[1:]
    slices, out, sems = refs[:group], refs[group], refs[group + 1]
    chans_here = slices[0].shape[2]
    copies = []
    for lag in range(out.shape[0]):
        for step in range(group):
            owner = lax.rem(meta[1] - step + group, group)
            rows = pl.ds(pl.multiple_of(owner * chans_here, 16), chans_here)
            copies.append(
                pltpu.make_async_copy(
                    slices[step].at[:, lag], out.at[lag, :, rows], sems.at[lag, step]
                )
            )
    for copy in copies:
        copy.start()
    for copy in copies:
        copy.wait()


def merge_call(meta, slices):
    group = len(slices)
    taps, lags, chans_here, chans = slices[0].shape
    return pl.pallas_call(
        functools.partial(merge_kernel, group),
        out_shape=jax.ShapeDtypeStruct((lags, taps, group * chans_here, chans), jnp.bfloat16),
        in_specs=[pl.BlockSpec(memory_space=pltpu.SMEM)]
        + [pl.BlockSpec(memory_space=pltpu.HBM)]
        + [pl.BlockSpec(memory_space=pl.ANY)] * (group - 1),
        out_specs=pl.BlockSpec(memory_space=pltpu.VMEM),
        scratch_shapes=[pltpu.SemaphoreType.DMA((lags, group))],
        compiler_params=pltpu.CompilerParams(vmem_limit_bytes=VMEM_LIMIT),
        name="merge_kernel_slices",
    )(meta, *slices)


def partner(member, place):
    odd = member % 2 == 1
    if isinstance(member, int) and isinstance(place, int):
        return 3 - place if odd and place in (1, 2) else place
    swapped = jnp.where(jnp.logical_or(place == 1, place == 2), 3 - place, place)
    return jnp.where(odd, swapped, place)


def split_call(meta, above, below, parts):
    frames, columns, chans = above.shape
    width = chans // parts

    def kernel(meta, above, below, *outs):
        for place, out in enumerate(outs):
            to = lax.bitwise_xor(meta[0], partner(meta[1], jnp.int32(place)))
            lanes = pl.ds(pl.multiple_of(to * width, width), width)
            out[0] = above[:, :, lanes]
            out[1] = below[:, :, lanes]

    return pl.pallas_call(
        kernel,
        out_shape=[jax.ShapeDtypeStruct((2, frames, columns, width), above.dtype)] * parts,
        in_specs=[pl.BlockSpec(memory_space=pltpu.SMEM)] + in_vmem(2),
        out_specs=in_vmem(parts),
        compiler_params=pltpu.CompilerParams(vmem_limit_bytes=VMEM_LIMIT),
        name="split_halo_rows",
    )(meta, above, below)


def stack_call(pieces, after):
    def kernel(*refs):
        for i in range(len(pieces)):
            refs[-1][i] = refs[i][...]

    return pl.pallas_call(
        kernel,
        out_shape=jax.ShapeDtypeStruct((len(pieces), *pieces[0].shape), pieces[0].dtype),
        in_specs=in_vmem(len(pieces) + 1),
        out_specs=pl.BlockSpec(memory_space=pltpu.VMEM),
        compiler_params=pltpu.CompilerParams(vmem_limit_bytes=VMEM_LIMIT),
        name="stack_halo_rows",
    )(*pieces, after)


def conv_kernel(jobs, parts, group, frames, out_count, *refs):
    meta, weights, refs = refs[0], refs[1], refs[2:]
    dests = sorted({s for s, _ in jobs})
    any_rim = any(rim for _, rim in jobs)
    held, refs = refs[: len(dests)], refs[len(dests) :]
    before, refs = refs[:parts], refs[parts:]
    if any_rim:
        (rims, rims_before), refs = refs[:2], refs[2:]
    outs, raw = refs[:-1], refs[-1]
    outs = outs[len(outs) - out_count :]
    part, member, z = meta[0], meta[1], meta[2]
    lags, _, width, chans = weights.shape
    _, rows_here, columns, _ = held[0].shape

    first = member == 0
    for n, where in enumerate(dests):
        to = lax.bitwise_xor(part, partner(member, jnp.int32(where)))
        valid = jnp.logical_or(jnp.logical_not(first), to > 0)
        sender = jnp.where(first, group - 1, member - 1)
        want = jnp.where(first, jnp.maximum(to - 1, 0), to)
        place = partner(sender, lax.bitwise_xor(part, want))
        raw[n, frames:, 1 : 1 + rows_here] = held[n][...]
        if any_rim:
            raw[n, frames:, 0] = rims[where, 0]
            raw[n, frames:, 1 + rows_here] = rims[where, 1]
            raw[n, :frames, 0] = rims_before[place, 0]
            raw[n, :frames, 1 + rows_here] = rims_before[place, 1]
        for i in range(parts):

            @pl.when(place == i)
            def _():
                raw[n, :frames, 1 : 1 + rows_here] = before[i][...]

        @pl.when(jnp.logical_not(valid))
        def _():
            raw[n, :frames] = jnp.zeros_like(raw[n, :frames])

    side = 3

    def patches(a, b):
        pieces = []
        for s, rim in jobs:
            n = dests.index(s)
            for p in range(frames):
                f = lax.rem(z + p, frames) + a
                if rim:
                    pieces.append(raw[n, f, b])
                    pieces.append(raw[n, f, rows_here - 1 + b])
                else:
                    pieces.append(raw[n, f, 1 + b : b + rows_here - 1].reshape(-1, width))
        return jnp.concatenate(pieces, axis=0)

    lhs = jnp.concatenate([patches(a, b) for a in range(side) for b in range(side)], axis=1)
    count = lhs.shape[0]
    column = lax.broadcasted_iota(jnp.int32, (count, chans), 0) % columns
    total = None
    for lag in (1, 0, 2):
        product = jnp.dot(
            lhs, weights[lag].reshape(-1, chans), preferred_element_type=jnp.float32
        )
        if lag == 1:
            total = product
        elif lag == 0:
            total = total + jnp.where(column == 0, 0.0, pltpu.roll(product, 1, 0))
        else:
            moved = pltpu.roll(product, count - 1, 0)
            total = total + jnp.where(column == columns - 1, 0.0, moved)
    place = 0
    for out in outs:
        out[...] = total[place : place + out.shape[0]].astype(out.dtype)
        place += out.shape[0]


def conv_call(jobs, meta, weights, held, before, rims, group, frames, out_type, after=()):
    parts = len(held)
    dests = sorted({place for place, _ in jobs})
    _, rows_here, columns, width = held[0].shape
    lags, taps, _, chans = weights.shape
    any_rim = any(rim for _, rim in jobs)
    counts = [frames * (2 if rim else rows_here - 2) * columns for _, rim in jobs]
    total = sum(counts)
    operands = [weights, *[held[n] for n in dests], *before, *(rims if any_rim else ())]
    specs = [pl.BlockSpec(memory_space=pltpu.SMEM)] + in_vmem(len(operands))
    specs += in_vmem(len(after))
    outs = [jax.ShapeDtypeStruct((count, chans), out_type) for count in counts]
    return pl.pallas_call(
        functools.partial(conv_kernel, tuple(jobs), parts, group, frames, len(outs)),
        out_shape=outs,
        in_specs=specs,
        out_specs=in_vmem(len(outs)),
        scratch_shapes=[
            pltpu.VMEM((len(dests), 2 * frames, rows_here + 2, columns, width), jnp.bfloat16)
        ],
        compiler_params=pltpu.CompilerParams(vmem_limit_bytes=VMEM_LIMIT),
        cost_estimate=pl.CostEstimate(
            flops=20 * total * taps * lags * width * chans,
            bytes_accessed=2 * taps * lags * width * chans,
            transcendentals=0,
        ),
        name="conv_rim" if any_rim else "conv_inner",
    )(meta, *operands, *after)


def sum_call(pieces, splits, after=()):
    count, chans = pieces[0].shape
    size = count // splits

    def kernel(*refs):
        for p, out_ref in enumerate(refs[len(refs) - splits :]):
            total = None
            for ref in refs[: len(pieces)]:
                rows = ref[p * size : (p + 1) * size].astype(jnp.float32)
                total = rows if total is None else total + rows
            out_ref[...] = total.astype(out_ref.dtype)

    return pl.pallas_call(
        kernel,
        out_shape=[jax.ShapeDtypeStruct((size, chans), jnp.bfloat16)] * splits,
        in_specs=in_vmem(len(pieces) + len(after)),
        out_specs=in_vmem(splits),
        compiler_params=pltpu.CompilerParams(vmem_limit_bytes=VMEM_LIMIT),
        name="sum_parts",
    )(*pieces, *after)


def attend_kernel(frames, share, chunks, *refs):
    own_count = frames * chunks
    all_count = own_count * share
    tokens, refs = refs[:all_count], refs[all_count:]
    (wq, wk, wv, wo), refs = refs[:4], refs[4:]
    outs, (normed, keys, values) = refs[:frames], refs[frames:]
    size, chans = normed.shape
    per_group = chans // G

    tile_row = lax.broadcasted_iota(jnp.int32, (LANES, LANES), 0) // per_group
    tile_col = lax.broadcasted_iota(jnp.int32, (LANES, LANES), 1) // per_group
    same = (tile_row == tile_col).astype(jnp.float32).astype(jnp.bfloat16)

    def group_mean(sums):
        first = sums.astype(jnp.bfloat16)
        rest = sums - first.astype(jnp.float32)
        second = rest.astype(jnp.bfloat16)
        third = rest - second.astype(jnp.float32)
        tiles = []
        for tile in range(chans // LANES):
            lanes = slice(tile * LANES, (tile + 1) * LANES)
            stacked = jnp.concatenate(
                [
                    first.astype(jnp.float32)[:, lanes],
                    second.astype(jnp.float32)[:, lanes],
                    third[:, lanes],
                ],
                axis=0,
            ).astype(jnp.bfloat16)
            spread = jnp.dot(stacked, same, preferred_element_type=jnp.float32)
            tiles.append(jnp.sum(spread, axis=0, keepdims=True))
        return jnp.concatenate(tiles, axis=1) / (size * per_group)

    def folded(x):
        return jnp.sum(x.reshape(-1, 8, chans), axis=0)

    average = group_mean(sum(folded(ref[...].astype(jnp.float32)) for ref in tokens))

    def spread_of(ref):
        centered = ref[...].astype(jnp.float32) - average
        return folded(centered * centered)

    scale = lax.rsqrt(group_mean(sum(spread_of(ref) for ref in tokens)) + epsilon)
    place = 0
    for ref in tokens:
        rows = ref.shape[0]
        normed[pl.ds(place, rows)] = (
            (ref[...].astype(jnp.float32) - average) * scale
        ).astype(jnp.bfloat16)
        place += rows

    step = min(256, size)
    for start in range(0, size, step):
        x = normed[pl.ds(start, step)]
        keys[pl.ds(start, step)] = jnp.dot(
            x, wk[...], preferred_element_type=jnp.float32
        ).astype(jnp.bfloat16)
        values[pl.ds(start, step)] = jnp.dot(
            x, wv[...], preferred_element_type=jnp.float32
        ).astype(jnp.bfloat16)

    place = 0
    for p, out in enumerate(outs):
        mine = tokens[p * chunks : (p + 1) * chunks]
        rows = sum(ref.shape[0] for ref in mine)
        queries = jnp.dot(
            normed[pl.ds(place, rows)], wq[...], preferred_element_type=jnp.float32
        ).astype(jnp.bfloat16)
        place += rows
        scores = lax.dot_general(
            queries, keys[...], (((1,), (1,)), ((), ())), preferred_element_type=jnp.float32
        ) * chans ** (-0.5)
        row_max = jnp.max(scores, axis=1, keepdims=True)
        exp_weights = jnp.exp(scores - row_max).astype(jnp.bfloat16)
        denominator = jnp.sum(exp_weights.astype(jnp.float32), axis=1, keepdims=True)
        numerator = jnp.dot(exp_weights, values[...], preferred_element_type=jnp.float32)
        attended = (numerator / denominator).astype(jnp.bfloat16)
        added = jnp.dot(attended, wo[...], preferred_element_type=jnp.float32)
        rows_here, columns, _ = out.shape
        inner = mine[0].shape[0]
        first = mine[0][...].astype(jnp.float32) + added[:inner]
        out[1 : rows_here - 1] = first.astype(jnp.bfloat16).reshape(rows_here - 2, columns, chans)
        second = (mine[1][...].astype(jnp.float32) + added[inner:]).astype(jnp.bfloat16)
        out[0] = second[:columns]
        out[rows_here - 1] = second[columns:]


def attend_call(own, others, weights, frames, rows_here, columns):
    chunks = len(own) // frames
    share = 1 + len(others) // len(own)
    chans = own[0].shape[1]
    size = sum(x.shape[0] for x in own) * share
    mine = size // share
    out = jax.ShapeDtypeStruct((rows_here, columns, chans), jnp.bfloat16)
    operands = [*own, *others, *weights]
    return pl.pallas_call(
        functools.partial(attend_kernel, frames, share, chunks),
        out_shape=[out] * frames,
        in_specs=in_vmem(len(operands)),
        out_specs=in_vmem(frames),
        scratch_shapes=[pltpu.VMEM((size, chans), jnp.bfloat16)] * 3,
        compiler_params=pltpu.CompilerParams(vmem_limit_bytes=VMEM_LIMIT),
        cost_estimate=pl.CostEstimate(
            flops=2 * (2 * size * chans * chans + 2 * mine * chans * (chans + size)),
            bytes_accessed=8 * chans * chans + 2 * size * chans,
            transcendentals=mine * size,
        ),
        name="attend",
    )(*operands)


def body(latents, conv_weight, query_weight, key_weight, value_weight, out_weight):
    frames, rows_here, columns, chans = latents.shape
    taps, chans_here, _ = conv_weight.shape
    devices, depth = lax.axis_size("tm"), lax.axis_size("rows")
    sizes = (devices, depth)
    group = LANES // chans_here
    parts = devices // group
    width = group * chans_here
    t_index, z_index = lax.axis_index("tm"), lax.axis_index("rows")
    part, member = t_index // group, t_index % group
    meta = jnp.stack([part, member, z_index]).astype(jnp.int32)

    def permute(block, target):
        return lax.ppermute(block, BOTH, everywhere(sizes, target))

    def to_place(place):
        return lambda t, z: ((t // group ^ partner(t % group, place)) * group + t % group, z)

    def to_member(step):
        return lambda t, z: (t // group * group + (t + step) % group, z)

    split = conv_weight.reshape(taps // 3, 3, chans_here, chans)
    slices = [split] + [permute(split, to_member(step)) for step in range(1, group)]
    weights = merge_call(meta, slices)

    above = permute(latents[:, -1], lambda t, z: (t, z + 1) if z + 1 < depth else None)
    below = permute(latents[:, 0], lambda t, z: (t, z - 1) if z else None)

    held, before = [None] * parts, [None] * parts
    order = [0, 3, 1, 2]
    for place in order:
        start = (part ^ partner(member, jnp.int32(place))) * width
        piece = lax.dynamic_slice_in_dim(latents, start, width, axis=3)
        held[place] = permute(piece, to_place(place)) if place else piece
    held[2], weights = lax.optimization_barrier((held[2], weights))
    for place in order:
        before[place] = permute(held[place], to_member(1))

    conv = functools.partial(
        conv_call,
        meta=meta,
        weights=weights,
        held=held,
        before=before,
        group=group,
        frames=frames,
    )

    def hop(pieces):
        return [permute(x, to_place(1)) for x in pieces]

    rims = split_call(meta, above, below, parts)
    rims = [permute(x, to_place(place)) if place else x for place, x in enumerate(rims)]
    inner_sent = conv([(3, False), (1, False)], rims=None, out_type=jnp.bfloat16)
    inner_got = hop(inner_sent)
    inner_on, inner_own = conv(
        [(2, False), (0, False)], rims=None, out_type=jnp.float32, after=inner_sent[:1]
    )
    rims = stack_call(rims, inner_sent[0])
    rims = (rims, permute(rims, to_member(1)))
    rim_sent = conv([(3, True), (1, True)], rims=rims, out_type=jnp.bfloat16, after=(inner_on,))
    rim_got = hop(rim_sent)
    (inner_relay,) = sum_call([inner_on, inner_got[0]], 1)
    inner_last = permute(inner_relay, to_place(2))
    rim_on, rim_own = conv(
        [(2, True), (0, True)], rims=rims, out_type=jnp.float32, after=(inner_relay,)
    )
    (rim_relay,) = sum_call([rim_on, rim_got[0]], 1)
    rim_last = permute(rim_relay, to_place(2))
    sums = [
        sum_call([inner_own, inner_got[1], inner_last], frames, after=(rim_relay,)),
        sum_call([rim_own, rim_got[1], rim_last], frames),
    ]

    share = depth // frames

    def frame_home(t, z, p):
        frame = t % CORES * frames + (z + p) % frames
        slot = frame * share + z // frames
        return (t // CORES * CORES + slot % CORES, slot // CORES)

    def next_in_frame(t, z, step):
        slot = z * CORES + t % CORES
        slot = slot // share * share + (slot + step) % share
        return (t // CORES * CORES + slot % CORES, slot // CORES)

    own = []
    for p in range(frames):
        for chunk in sums:
            own.append(permute(chunk[p], lambda t, z: frame_home(t, z, p)))
    others = []
    for step in range(1, share):
        others += [permute(x, lambda t, z: next_in_frame(t, z, step)) for x in own]

    done = attend_call(
        own,
        others,
        (query_weight, key_weight, value_weight, out_weight),
        frames,
        rows_here,
        columns,
    )
    back = []
    for p in range(frames):
        pairs = [(b, a) for a, b in everywhere(sizes, lambda t, z: frame_home(t, z, p))]
        back.append(lax.ppermute(done[p], BOTH, pairs))
    return jnp.stack(
        [
            functools.reduce(
                lambda rest, p: jnp.where((z_index + p) % frames == f, back[p], rest),
                range(1, frames),
                back[0],
            )
            for f in range(frames)
        ]
    )


def solution(mesh):
    placed = (P("tm", "rows", None, None), P(None, "tm", None), P(), P(), P(), P())
    return jax.shard_map(
        body, mesh=mesh, in_specs=placed, out_specs=P("tm", "rows", None, None), check_vma=False
    )
```

```python
import functools

import jax
import jax.numpy as jnp
from jax import lax
from jax.experimental import pallas as pl
from jax.experimental.pallas import tpu as pltpu
from jax.sharding import PartitionSpec as P

G = 32
LANES = 128
CORES = 2

epsilon = 1e-06

BOTH = ("tm", "rows")
VMEM_LIMIT = 32 * 1024 * 1024


def everywhere(sizes, target):
    devices, depth = sizes
    pairs = []
    for t in range(devices):
        for z in range(depth):
            to = target(t, z)
            if to is not None:
                pairs.append((t * depth + z, to[0] * depth + to[1]))
    return pairs


def in_vmem(count):
    return [pl.BlockSpec(memory_space=pltpu.VMEM)] * count


def merge_kernel(group, *refs):
    meta, refs = refs[0], refs[1:]
    slices, out, sems = refs[:group], refs[group], refs[group + 1]
    chans_here = slices[0].shape[2]
    copies = []
    for lag in range(out.shape[0]):
        for step in range(group):
            owner = lax.rem(meta[1] - step + group, group)
            rows = pl.ds(pl.multiple_of(owner * chans_here, 16), chans_here)
            copies.append(
                pltpu.make_async_copy(
                    slices[step].at[:, lag], out.at[lag, :, rows], sems.at[lag, step]
                )
            )
    for copy in copies:
        copy.start()
    for copy in copies:
        copy.wait()


def merge_call(meta, slices):
    group = len(slices)
    taps, lags, chans_here, chans = slices[0].shape
    return pl.pallas_call(
        functools.partial(merge_kernel, group),
        out_shape=jax.ShapeDtypeStruct((lags, taps, group * chans_here, chans), jnp.bfloat16),
        in_specs=[pl.BlockSpec(memory_space=pltpu.SMEM)]
        + [pl.BlockSpec(memory_space=pltpu.HBM)]
        + [pl.BlockSpec(memory_space=pl.ANY)] * (group - 1),
        out_specs=pl.BlockSpec(memory_space=pltpu.VMEM),
        scratch_shapes=[pltpu.SemaphoreType.DMA((lags, group))],
        compiler_params=pltpu.CompilerParams(vmem_limit_bytes=VMEM_LIMIT),
        name="merge_kernel_slices",
    )(meta, *slices)


def partner(member, place):
    odd = member % 2 == 1
    if isinstance(member, int) and isinstance(place, int):
        return 3 - place if odd and place in (1, 2) else place
    swapped = jnp.where(jnp.logical_or(place == 1, place == 2), 3 - place, place)
    return jnp.where(odd, swapped, place)


def split_call(meta, above, below, parts):
    frames, columns, chans = above.shape
    width = chans // parts

    def kernel(meta, above, below, *outs):
        for place, out in enumerate(outs):
            to = lax.bitwise_xor(meta[0], partner(meta[1], jnp.int32(place)))
            lanes = pl.ds(pl.multiple_of(to * width, width), width)
            out[0] = above[:, :, lanes]
            out[1] = below[:, :, lanes]

    return pl.pallas_call(
        kernel,
        out_shape=[jax.ShapeDtypeStruct((2, frames, columns, width), above.dtype)] * parts,
        in_specs=[pl.BlockSpec(memory_space=pltpu.SMEM)] + in_vmem(2),
        out_specs=in_vmem(parts),
        compiler_params=pltpu.CompilerParams(vmem_limit_bytes=VMEM_LIMIT),
        name="split_halo_rows",
    )(meta, above, below)


def stack_call(pieces, after):
    def kernel(*refs):
        for i in range(len(pieces)):
            refs[-1][i] = refs[i][...]

    return pl.pallas_call(
        kernel,
        out_shape=jax.ShapeDtypeStruct((len(pieces), *pieces[0].shape), pieces[0].dtype),
        in_specs=in_vmem(len(pieces) + 1),
        out_specs=pl.BlockSpec(memory_space=pltpu.VMEM),
        compiler_params=pltpu.CompilerParams(vmem_limit_bytes=VMEM_LIMIT),
        name="stack_halo_rows",
    )(*pieces, after)


def conv_kernel(jobs, parts, group, frames, out_count, *refs):
    meta, weights, refs = refs[0], refs[1], refs[2:]
    dests = sorted({s for s, _ in jobs})
    any_rim = any(rim for _, rim in jobs)
    held, refs = refs[: len(dests)], refs[len(dests) :]
    before, refs = refs[:parts], refs[parts:]
    if any_rim:
        (rims, rims_before), refs = refs[:2], refs[2:]
    outs, raw = refs[:-1], refs[-1]
    outs = outs[len(outs) - out_count :]
    part, member, z = meta[0], meta[1], meta[2]
    lags, _, width, chans = weights.shape
    _, rows_here, columns, _ = held[0].shape

    first = member == 0
    for n, where in enumerate(dests):
        to = lax.bitwise_xor(part, partner(member, jnp.int32(where)))
        valid = jnp.logical_or(jnp.logical_not(first), to > 0)
        sender = jnp.where(first, group - 1, member - 1)
        want = jnp.where(first, jnp.maximum(to - 1, 0), to)
        place = partner(sender, lax.bitwise_xor(part, want))
        raw[n, frames:, 1 : 1 + rows_here] = held[n][...]
        if any_rim:
            raw[n, frames:, 0] = rims[where, 0]
            raw[n, frames:, 1 + rows_here] = rims[where, 1]
            raw[n, :frames, 0] = rims_before[place, 0]
            raw[n, :frames, 1 + rows_here] = rims_before[place, 1]
        for i in range(parts):

            @pl.when(place == i)
            def _():
                raw[n, :frames, 1 : 1 + rows_here] = before[i][...]

        @pl.when(jnp.logical_not(valid))
        def _():
            raw[n, :frames] = jnp.zeros_like(raw[n, :frames])

    side = 3

    def patches(a, b):
        pieces = []
        for s, rim in jobs:
            n = dests.index(s)
            for p in range(frames):
                f = lax.rem(z + p, frames) + a
                if rim:
                    pieces.append(raw[n, f, b])
                    pieces.append(raw[n, f, rows_here - 1 + b])
                else:
                    pieces.append(raw[n, f, 1 + b : b + rows_here - 1].reshape(-1, width))
        return jnp.concatenate(pieces, axis=0)

    lhs = jnp.concatenate([patches(a, b) for a in range(side) for b in range(side)], axis=1)
    count = lhs.shape[0]
    column = lax.broadcasted_iota(jnp.int32, (count, chans), 0) % columns
    total = None
    for lag in (1, 0, 2):
        product = jnp.dot(
            lhs, weights[lag].reshape(-1, chans), preferred_element_type=jnp.float32
        )
        if lag == 1:
            total = product
        elif lag == 0:
            total = total + jnp.where(column == 0, 0.0, pltpu.roll(product, 1, 0))
        else:
            moved = pltpu.roll(product, count - 1, 0)
            total = total + jnp.where(column == columns - 1, 0.0, moved)
    place = 0
    for out in outs:
        out[...] = total[place : place + out.shape[0]].astype(out.dtype)
        place += out.shape[0]


def conv_call(jobs, meta, weights, held, before, rims, group, frames, out_type, after=()):
    parts = len(held)
    dests = sorted({place for place, _ in jobs})
    _, rows_here, columns, width = held[0].shape
    lags, taps, _, chans = weights.shape
    any_rim = any(rim for _, rim in jobs)
    counts = [frames * (2 if rim else rows_here - 2) * columns for _, rim in jobs]
    total = sum(counts)
    operands = [weights, *[held[n] for n in dests], *before, *(rims if any_rim else ())]
    specs = [pl.BlockSpec(memory_space=pltpu.SMEM)] + in_vmem(len(operands))
    specs += in_vmem(len(after))
    outs = [jax.ShapeDtypeStruct((count, chans), out_type) for count in counts]
    return pl.pallas_call(
        functools.partial(conv_kernel, tuple(jobs), parts, group, frames, len(outs)),
        out_shape=outs,
        in_specs=specs,
        out_specs=in_vmem(len(outs)),
        scratch_shapes=[
            pltpu.VMEM((len(dests), 2 * frames, rows_here + 2, columns, width), jnp.bfloat16)
        ],
        compiler_params=pltpu.CompilerParams(vmem_limit_bytes=VMEM_LIMIT),
        cost_estimate=pl.CostEstimate(
            flops=20 * total * taps * lags * width * chans,
            bytes_accessed=2 * taps * lags * width * chans,
            transcendentals=0,
        ),
        name="conv_rim" if any_rim else "conv_inner",
    )(meta, *operands, *after)


def sum_call(pieces, splits, after=()):
    count, chans = pieces[0].shape
    size = count // splits

    def kernel(*refs):
        for p, out_ref in enumerate(refs[len(refs) - splits :]):
            total = None
            for ref in refs[: len(pieces)]:
                rows = ref[p * size : (p + 1) * size].astype(jnp.float32)
                total = rows if total is None else total + rows
            out_ref[...] = total.astype(out_ref.dtype)

    return pl.pallas_call(
        kernel,
        out_shape=[jax.ShapeDtypeStruct((size, chans), jnp.bfloat16)] * splits,
        in_specs=in_vmem(len(pieces) + len(after)),
        out_specs=in_vmem(splits),
        compiler_params=pltpu.CompilerParams(vmem_limit_bytes=VMEM_LIMIT),
        name="sum_parts",
    )(*pieces, *after)


def attend_kernel(frames, share, chunks, *refs):
    own_count = frames * chunks
    all_count = own_count * share
    tokens, refs = refs[:all_count], refs[all_count:]
    (wq, wk, wv, wo), refs = refs[:4], refs[4:]
    outs, (normed, keys, values) = refs[:frames], refs[frames:]
    size, chans = normed.shape
    per_group = chans // G

    tile_row = lax.broadcasted_iota(jnp.int32, (LANES, LANES), 0) // per_group
    tile_col = lax.broadcasted_iota(jnp.int32, (LANES, LANES), 1) // per_group
    same = (tile_row == tile_col).astype(jnp.float32).astype(jnp.bfloat16)

    def group_mean(sums):
        first = sums.astype(jnp.bfloat16)
        rest = sums - first.astype(jnp.float32)
        second = rest.astype(jnp.bfloat16)
        third = rest - second.astype(jnp.float32)
        tiles = []
        for tile in range(chans // LANES):
            lanes = slice(tile * LANES, (tile + 1) * LANES)
            stacked = jnp.concatenate(
                [
                    first.astype(jnp.float32)[:, lanes],
                    second.astype(jnp.float32)[:, lanes],
                    third[:, lanes],
                ],
                axis=0,
            ).astype(jnp.bfloat16)
            spread = jnp.dot(stacked, same, preferred_element_type=jnp.float32)
            tiles.append(jnp.sum(spread, axis=0, keepdims=True))
        return jnp.concatenate(tiles, axis=1) / (size * per_group)

    def folded(x):
        return jnp.sum(x.reshape(-1, 8, chans), axis=0)

    average = group_mean(sum(folded(ref[...].astype(jnp.float32)) for ref in tokens))

    def spread_of(ref):
        centered = ref[...].astype(jnp.float32) - average
        return folded(centered * centered)

    scale = lax.rsqrt(group_mean(sum(spread_of(ref) for ref in tokens)) + epsilon)
    place = 0
    for ref in tokens:
        rows = ref.shape[0]
        normed[pl.ds(place, rows)] = (
            (ref[...].astype(jnp.float32) - average) * scale
        ).astype(jnp.bfloat16)
        place += rows

    step = min(256, size)
    for start in range(0, size, step):
        x = normed[pl.ds(start, step)]
        keys[pl.ds(start, step)] = jnp.dot(
            x, wk[...], preferred_element_type=jnp.float32
        ).astype(jnp.bfloat16)
        values[pl.ds(start, step)] = jnp.dot(
            x, wv[...], preferred_element_type=jnp.float32
        ).astype(jnp.bfloat16)

    place = 0
    for p, out in enumerate(outs):
        mine = tokens[p * chunks : (p + 1) * chunks]
        rows = sum(ref.shape[0] for ref in mine)
        queries = jnp.dot(
            normed[pl.ds(place, rows)], wq[...], preferred_element_type=jnp.float32
        ).astype(jnp.bfloat16)
        place += rows
        scores = lax.dot_general(
            queries, keys[...], (((1,), (1,)), ((), ())), preferred_element_type=jnp.float32
        ) * chans ** (-0.5)
        row_max = jnp.max(scores, axis=1, keepdims=True)
        exp_weights = jnp.exp(scores - row_max).astype(jnp.bfloat16)
        denominator = jnp.sum(exp_weights.astype(jnp.float32), axis=1, keepdims=True)
        numerator = jnp.dot(exp_weights, values[...], preferred_element_type=jnp.float32)
        attended = (numerator / denominator).astype(jnp.bfloat16)
        added = jnp.dot(attended, wo[...], preferred_element_type=jnp.float32)
        rows_here, columns, _ = out.shape
        inner = mine[0].shape[0]
        first = mine[0][...].astype(jnp.float32) + added[:inner]
        out[1 : rows_here - 1] = first.astype(jnp.bfloat16).reshape(rows_here - 2, columns, chans)
        second = (mine[1][...].astype(jnp.float32) + added[inner:]).astype(jnp.bfloat16)
        out[0] = second[:columns]
        out[rows_here - 1] = second[columns:]


def attend_call(own, others, weights, frames, rows_here, columns):
    chunks = len(own) // frames
    share = 1 + len(others) // len(own)
    chans = own[0].shape[1]
    size = sum(x.shape[0] for x in own) * share
    mine = size // share
    out = jax.ShapeDtypeStruct((rows_here, columns, chans), jnp.bfloat16)
    operands = [*own, *others, *weights]
    return pl.pallas_call(
        functools.partial(attend_kernel, frames, share, chunks),
        out_shape=[out] * frames,
        in_specs=in_vmem(len(operands)),
        out_specs=in_vmem(frames),
        scratch_shapes=[pltpu.VMEM((size, chans), jnp.bfloat16)] * 3,
        compiler_params=pltpu.CompilerParams(vmem_limit_bytes=VMEM_LIMIT),
        cost_estimate=pl.CostEstimate(
            flops=2 * (2 * size * chans * chans + 2 * mine * chans * (chans + size)),
            bytes_accessed=8 * chans * chans + 2 * size * chans,
            transcendentals=mine * size,
        ),
        name="attend",
    )(*operands)


def body(latents, conv_weight, query_weight, key_weight, value_weight, out_weight):
    frames, rows_here, columns, chans = latents.shape
    taps, chans_here, _ = conv_weight.shape
    devices, depth = lax.axis_size("tm"), lax.axis_size("rows")
    sizes = (devices, depth)
    group = LANES // chans_here
    parts = devices // group
    width = group * chans_here
    t_index, z_index = lax.axis_index("tm"), lax.axis_index("rows")
    part, member = t_index // group, t_index % group
    meta = jnp.stack([part, member, z_index]).astype(jnp.int32)

    def permute(block, target):
        return lax.ppermute(block, BOTH, everywhere(sizes, target))

    def to_place(place):
        return lambda t, z: ((t // group ^ partner(t % group, place)) * group + t % group, z)

    def to_member(step):
        return lambda t, z: (t // group * group + (t + step) % group, z)

    split = conv_weight.reshape(taps // 3, 3, chans_here, chans)
    slices = [split] + [permute(split, to_member(step)) for step in range(1, group)]
    weights = merge_call(meta, slices)

    above = permute(latents[:, -1], lambda t, z: (t, z + 1) if z + 1 < depth else None)
    below = permute(latents[:, 0], lambda t, z: (t, z - 1) if z else None)

    held, before = [None] * parts, [None] * parts
    order = [0, 3, 1, 2]
    for place in order:
        start = (part ^ partner(member, jnp.int32(place))) * width
        piece = lax.dynamic_slice_in_dim(latents, start, width, axis=3)
        held[place] = permute(piece, to_place(place)) if place else piece
    held[2], weights = lax.optimization_barrier((held[2], weights))
    for place in order:
        before[place] = permute(held[place], to_member(1))

    conv = functools.partial(
        conv_call,
        meta=meta,
        weights=weights,
        held=held,
        before=before,
        group=group,
        frames=frames,
    )

    def hop(pieces):
        return [permute(x, to_place(1)) for x in pieces]

    rims = split_call(meta, above, below, parts)
    rims = [permute(x, to_place(place)) if place else x for place, x in enumerate(rims)]
    inner_sent = conv([(3, False), (1, False)], rims=None, out_type=jnp.bfloat16)
    inner_got = hop(inner_sent)
    inner_on, inner_own = conv(
        [(2, False), (0, False)], rims=None, out_type=jnp.float32, after=inner_sent[:1]
    )
    rims = stack_call(rims, inner_on)
    rims = (rims, permute(rims, to_member(1)))
    rim_sent = conv([(3, True), (1, True)], rims=rims, out_type=jnp.bfloat16, after=(inner_on,))
    rim_got = hop(rim_sent)
    (inner_relay,) = sum_call([inner_on, inner_got[0]], 1)
    inner_last = permute(inner_relay, to_place(2))
    rim_on, rim_own = conv(
        [(2, True), (0, True)], rims=rims, out_type=jnp.float32, after=rim_sent[:1]
    )
    inner_sums = sum_call([inner_own, inner_got[1], inner_last], frames, after=(rim_on,))
    (rim_relay,) = sum_call([rim_on, rim_got[0]], 1, after=inner_sums[:1])
    rim_last = permute(rim_relay, to_place(2))
    sums = [inner_sums, sum_call([rim_own, rim_got[1], rim_last], frames)]

    share = depth // frames

    def frame_home(t, z, p):
        frame = t % CORES * frames + (z + p) % frames
        slot = frame * share + z // frames
        return (t // CORES * CORES + slot % CORES, slot // CORES)

    def next_in_frame(t, z, step):
        slot = z * CORES + t % CORES
        slot = slot // share * share + (slot + step) % share
        return (t // CORES * CORES + slot % CORES, slot // CORES)

    own = []
    for p in range(frames):
        for chunk in sums:
            own.append(permute(chunk[p], lambda t, z: frame_home(t, z, p)))
    others = []
    for step in range(1, share):
        others += [permute(x, lambda t, z: next_in_frame(t, z, step)) for x in own]

    done = attend_call(
        own,
        others,
        (query_weight, key_weight, value_weight, out_weight),
        frames,
        rows_here,
        columns,
    )
    back = []
    for p in range(frames):
        pairs = [(b, a) for a, b in everywhere(sizes, lambda t, z: frame_home(t, z, p))]
        back.append(lax.ppermute(done[p], BOTH, pairs))
    return jnp.stack(
        [
            functools.reduce(
                lambda rest, p: jnp.where((z_index + p) % frames == f, back[p], rest),
                range(1, frames),
                back[0],
            )
            for f in range(frames)
        ]
    )


def solution(mesh):
    placed = (P("tm", "rows", None, None), P(None, "tm", None), P(), P(), P(), P())
    return jax.shard_map(
        body, mesh=mesh, in_specs=placed, out_specs=P("tm", "rows", None, None), check_vma=False
    )
```

```python
import functools

import jax
import jax.numpy as jnp
from jax import lax
from jax.experimental import pallas as pl
from jax.experimental.pallas import tpu as pltpu
from jax.sharding import PartitionSpec as P

G = 32
LANES = 128
CORES = 2

epsilon = 1e-06

BOTH = ("tm", "rows")
VMEM_LIMIT = 32 * 1024 * 1024


def everywhere(sizes, target):
    devices, depth = sizes
    pairs = []
    for t in range(devices):
        for z in range(depth):
            to = target(t, z)
            if to is not None:
                pairs.append((t * depth + z, to[0] * depth + to[1]))
    return pairs


def in_vmem(count):
    return [pl.BlockSpec(memory_space=pltpu.VMEM)] * count


def merge_kernel(group, *refs):
    meta, refs = refs[0], refs[1:]
    slices, out, sems = refs[:group], refs[group], refs[group + 1]
    chans_here = slices[0].shape[2]
    copies = []
    for lag in range(out.shape[0]):
        for step in range(group):
            owner = lax.rem(meta[1] - step + group, group)
            rows = pl.ds(pl.multiple_of(owner * chans_here, 16), chans_here)
            copies.append(
                pltpu.make_async_copy(
                    slices[step].at[:, lag], out.at[lag, :, rows], sems.at[lag, step]
                )
            )
    for copy in copies:
        copy.start()
    for copy in copies:
        copy.wait()


def merge_call(meta, slices):
    group = len(slices)
    taps, lags, chans_here, chans = slices[0].shape
    return pl.pallas_call(
        functools.partial(merge_kernel, group),
        out_shape=jax.ShapeDtypeStruct((lags, taps, group * chans_here, chans), jnp.bfloat16),
        in_specs=[pl.BlockSpec(memory_space=pltpu.SMEM)]
        + [pl.BlockSpec(memory_space=pltpu.HBM)]
        + [pl.BlockSpec(memory_space=pl.ANY)] * (group - 1),
        out_specs=pl.BlockSpec(memory_space=pltpu.VMEM),
        scratch_shapes=[pltpu.SemaphoreType.DMA((lags, group))],
        compiler_params=pltpu.CompilerParams(vmem_limit_bytes=VMEM_LIMIT),
        name="merge_kernel_slices",
    )(meta, *slices)


def partner(member, place):
    odd = member % 2 == 1
    if isinstance(member, int) and isinstance(place, int):
        return 3 - place if odd and place in (1, 2) else place
    swapped = jnp.where(jnp.logical_or(place == 1, place == 2), 3 - place, place)
    return jnp.where(odd, swapped, place)


def split_call(meta, above, below, parts):
    frames, columns, chans = above.shape
    width = chans // parts

    def kernel(meta, above, below, *outs):
        for place, out in enumerate(outs):
            to = lax.bitwise_xor(meta[0], partner(meta[1], jnp.int32(place)))
            lanes = pl.ds(pl.multiple_of(to * width, width), width)
            out[0] = above[:, :, lanes]
            out[1] = below[:, :, lanes]

    return pl.pallas_call(
        kernel,
        out_shape=[jax.ShapeDtypeStruct((2, frames, columns, width), above.dtype)] * parts,
        in_specs=[pl.BlockSpec(memory_space=pltpu.SMEM)] + in_vmem(2),
        out_specs=in_vmem(parts),
        compiler_params=pltpu.CompilerParams(vmem_limit_bytes=VMEM_LIMIT),
        name="split_halo_rows",
    )(meta, above, below)


def stack_call(pieces, after):
    def kernel(*refs):
        for i in range(len(pieces)):
            refs[-1][i] = refs[i][...]

    return pl.pallas_call(
        kernel,
        out_shape=jax.ShapeDtypeStruct((len(pieces), *pieces[0].shape), pieces[0].dtype),
        in_specs=in_vmem(len(pieces) + 1),
        out_specs=pl.BlockSpec(memory_space=pltpu.VMEM),
        compiler_params=pltpu.CompilerParams(vmem_limit_bytes=VMEM_LIMIT),
        name="stack_halo_rows",
    )(*pieces, after)


def conv_kernel(jobs, parts, group, frames, out_count, *refs):
    meta, weights, refs = refs[0], refs[1], refs[2:]
    dests = sorted({s for s, _ in jobs})
    any_rim = any(rim for _, rim in jobs)
    held, refs = refs[: len(dests)], refs[len(dests) :]
    before, refs = refs[:parts], refs[parts:]
    if any_rim:
        (rims, rims_before), refs = refs[:2], refs[2:]
    outs, raw = refs[:-1], refs[-1]
    outs = outs[len(outs) - out_count :]
    part, member, z = meta[0], meta[1], meta[2]
    lags, _, width, chans = weights.shape
    _, rows_here, columns, _ = held[0].shape

    first = member == 0
    for n, where in enumerate(dests):
        to = lax.bitwise_xor(part, partner(member, jnp.int32(where)))
        valid = jnp.logical_or(jnp.logical_not(first), to > 0)
        sender = jnp.where(first, group - 1, member - 1)
        want = jnp.where(first, jnp.maximum(to - 1, 0), to)
        place = partner(sender, lax.bitwise_xor(part, want))
        raw[n, frames:, 1 : 1 + rows_here] = held[n][...]
        if any_rim:
            raw[n, frames:, 0] = rims[where, 0]
            raw[n, frames:, 1 + rows_here] = rims[where, 1]
            raw[n, :frames, 0] = rims_before[place, 0]
            raw[n, :frames, 1 + rows_here] = rims_before[place, 1]
        for i in range(parts):

            @pl.when(place == i)
            def _():
                raw[n, :frames, 1 : 1 + rows_here] = before[i][...]

        @pl.when(jnp.logical_not(valid))
        def _():
            raw[n, :frames] = jnp.zeros_like(raw[n, :frames])

    side = 3

    def patches(a, b):
        pieces = []
        for s, rim in jobs:
            n = dests.index(s)
            for p in range(frames):
                f = lax.rem(z + p, frames) + a
                if rim:
                    pieces.append(raw[n, f, b])
                    pieces.append(raw[n, f, rows_here - 1 + b])
                else:
                    pieces.append(raw[n, f, 1 + b : b + rows_here - 1].reshape(-1, width))
        return jnp.concatenate(pieces, axis=0)

    lhs = jnp.concatenate([patches(a, b) for a in range(side) for b in range(side)], axis=1)
    count = lhs.shape[0]
    column = lax.broadcasted_iota(jnp.int32, (count, chans), 0) % columns
    total = None
    for lag in (1, 0, 2):
        product = jnp.dot(
            lhs, weights[lag].reshape(-1, chans), preferred_element_type=jnp.float32
        )
        if lag == 1:
            total = product
        elif lag == 0:
            total = total + jnp.where(column == 0, 0.0, pltpu.roll(product, 1, 0))
        else:
            moved = pltpu.roll(product, count - 1, 0)
            total = total + jnp.where(column == columns - 1, 0.0, moved)
    place = 0
    for out in outs:
        out[...] = total[place : place + out.shape[0]].astype(out.dtype)
        place += out.shape[0]


def conv_call(jobs, meta, weights, held, before, rims, group, frames, out_type, after=()):
    parts = len(held)
    dests = sorted({place for place, _ in jobs})
    _, rows_here, columns, width = held[0].shape
    lags, taps, _, chans = weights.shape
    any_rim = any(rim for _, rim in jobs)
    counts = [frames * (2 if rim else rows_here - 2) * columns for _, rim in jobs]
    total = sum(counts)
    operands = [weights, *[held[n] for n in dests], *before, *(rims if any_rim else ())]
    specs = [pl.BlockSpec(memory_space=pltpu.SMEM)] + in_vmem(len(operands))
    specs += in_vmem(len(after))
    outs = [jax.ShapeDtypeStruct((count, chans), out_type) for count in counts]
    return pl.pallas_call(
        functools.partial(conv_kernel, tuple(jobs), parts, group, frames, len(outs)),
        out_shape=outs,
        in_specs=specs,
        out_specs=in_vmem(len(outs)),
        scratch_shapes=[
            pltpu.VMEM((len(dests), 2 * frames, rows_here + 2, columns, width), jnp.bfloat16)
        ],
        compiler_params=pltpu.CompilerParams(vmem_limit_bytes=VMEM_LIMIT),
        cost_estimate=pl.CostEstimate(
            flops=2 * total * taps * lags * width * chans,
            bytes_accessed=2 * taps * lags * width * chans,
            transcendentals=0,
        ),
        name="conv_rim" if any_rim else "conv_inner",
    )(meta, *operands, *after)


def sum_call(pieces, splits, after=()):
    count, chans = pieces[0].shape
    size = count // splits

    def kernel(*refs):
        for p, out_ref in enumerate(refs[len(refs) - splits :]):
            total = None
            for ref in refs[: len(pieces)]:
                rows = ref[p * size : (p + 1) * size].astype(jnp.float32)
                total = rows if total is None else total + rows
            out_ref[...] = total.astype(out_ref.dtype)

    return pl.pallas_call(
        kernel,
        out_shape=[jax.ShapeDtypeStruct((size, chans), jnp.bfloat16)] * splits,
        in_specs=in_vmem(len(pieces) + len(after)),
        out_specs=in_vmem(splits),
        compiler_params=pltpu.CompilerParams(vmem_limit_bytes=VMEM_LIMIT),
        name="sum_parts",
    )(*pieces, *after)


def attend_kernel(frames, share, chunks, *refs):
    own_count = frames * chunks
    all_count = own_count * share
    tokens, refs = refs[:all_count], refs[all_count:]
    (wq, wk, wv, wo), refs = refs[:4], refs[4:]
    outs, (normed, keys, values) = refs[:frames], refs[frames:]
    size, chans = normed.shape
    per_group = chans // G

    tile_row = lax.broadcasted_iota(jnp.int32, (LANES, LANES), 0) // per_group
    tile_col = lax.broadcasted_iota(jnp.int32, (LANES, LANES), 1) // per_group
    same = (tile_row == tile_col).astype(jnp.float32).astype(jnp.bfloat16)

    def group_mean(sums):
        first = sums.astype(jnp.bfloat16)
        rest = sums - first.astype(jnp.float32)
        second = rest.astype(jnp.bfloat16)
        third = rest - second.astype(jnp.float32)
        tiles = []
        for tile in range(chans // LANES):
            lanes = slice(tile * LANES, (tile + 1) * LANES)
            stacked = jnp.concatenate(
                [
                    first.astype(jnp.float32)[:, lanes],
                    second.astype(jnp.float32)[:, lanes],
                    third[:, lanes],
                ],
                axis=0,
            ).astype(jnp.bfloat16)
            spread = jnp.dot(stacked, same, preferred_element_type=jnp.float32)
            tiles.append(jnp.sum(spread, axis=0, keepdims=True))
        return jnp.concatenate(tiles, axis=1) / (size * per_group)

    def folded(x):
        return jnp.sum(x.reshape(-1, 8, chans), axis=0)

    average = group_mean(sum(folded(ref[...].astype(jnp.float32)) for ref in tokens))

    def spread_of(ref):
        centered = ref[...].astype(jnp.float32) - average
        return folded(centered * centered)

    scale = lax.rsqrt(group_mean(sum(spread_of(ref) for ref in tokens)) + epsilon)
    place = 0
    for ref in tokens:
        rows = ref.shape[0]
        normed[pl.ds(place, rows)] = (
            (ref[...].astype(jnp.float32) - average) * scale
        ).astype(jnp.bfloat16)
        place += rows

    step = min(256, size)
    for start in range(0, size, step):
        x = normed[pl.ds(start, step)]
        keys[pl.ds(start, step)] = jnp.dot(
            x, wk[...], preferred_element_type=jnp.float32
        ).astype(jnp.bfloat16)
        values[pl.ds(start, step)] = jnp.dot(
            x, wv[...], preferred_element_type=jnp.float32
        ).astype(jnp.bfloat16)

    place = 0
    for p, out in enumerate(outs):
        mine = tokens[p * chunks : (p + 1) * chunks]
        rows = sum(ref.shape[0] for ref in mine)
        queries = jnp.dot(
            normed[pl.ds(place, rows)], wq[...], preferred_element_type=jnp.float32
        ).astype(jnp.bfloat16)
        place += rows
        scores = lax.dot_general(
            queries, keys[...], (((1,), (1,)), ((), ())), preferred_element_type=jnp.float32
        )
        row_max = jnp.max(scores, axis=1, keepdims=True)
        exp_weights = jnp.exp((scores - row_max) * chans ** (-0.5)).astype(jnp.bfloat16)
        denominator = jnp.sum(exp_weights.astype(jnp.float32), axis=1, keepdims=True)
        numerator = jnp.dot(exp_weights, values[...], preferred_element_type=jnp.float32)
        attended = (numerator * (1.0 / denominator)).astype(jnp.bfloat16)
        added = jnp.dot(attended, wo[...], preferred_element_type=jnp.float32)
        rows_here, columns, _ = out.shape
        inner = mine[0].shape[0]
        first = mine[0][...].astype(jnp.float32) + added[:inner]
        out[1 : rows_here - 1] = first.astype(jnp.bfloat16).reshape(rows_here - 2, columns, chans)
        second = (mine[1][...].astype(jnp.float32) + added[inner:]).astype(jnp.bfloat16)
        out[0] = second[:columns]
        out[rows_here - 1] = second[columns:]


def attend_call(own, others, weights, frames, rows_here, columns):
    chunks = len(own) // frames
    share = 1 + len(others) // len(own)
    chans = own[0].shape[1]
    size = sum(x.shape[0] for x in own) * share
    mine = size // share
    out = jax.ShapeDtypeStruct((rows_here, columns, chans), jnp.bfloat16)
    operands = [*own, *others, *weights]
    return pl.pallas_call(
        functools.partial(attend_kernel, frames, share, chunks),
        out_shape=[out] * frames,
        in_specs=in_vmem(len(operands)),
        out_specs=in_vmem(frames),
        scratch_shapes=[pltpu.VMEM((size, chans), jnp.bfloat16)] * 3,
        compiler_params=pltpu.CompilerParams(vmem_limit_bytes=VMEM_LIMIT),
        cost_estimate=pl.CostEstimate(
            flops=2 * (2 * size * chans * chans + 2 * mine * chans * (chans + size)),
            bytes_accessed=8 * chans * chans + 2 * size * chans,
            transcendentals=mine * size,
        ),
        name="attend",
    )(*operands)


def body(latents, conv_weight, query_weight, key_weight, value_weight, out_weight):
    frames, rows_here, columns, chans = latents.shape
    taps, chans_here, _ = conv_weight.shape
    devices, depth = lax.axis_size("tm"), lax.axis_size("rows")
    sizes = (devices, depth)
    group = LANES // chans_here
    parts = devices // group
    width = group * chans_here
    t_index, z_index = lax.axis_index("tm"), lax.axis_index("rows")
    part, member = t_index // group, t_index % group
    meta = jnp.stack([part, member, z_index]).astype(jnp.int32)

    def permute(block, target):
        return lax.ppermute(block, BOTH, everywhere(sizes, target))

    def to_place(place):
        return lambda t, z: ((t // group ^ partner(t % group, place)) * group + t % group, z)

    def to_member(step):
        return lambda t, z: (t // group * group + (t + step) % group, z)

    split = conv_weight.reshape(taps // 3, 3, chans_here, chans)
    slices = [split] + [permute(split, to_member(step)) for step in range(1, group)]
    weights = merge_call(meta, slices)

    above = permute(latents[:, -1], lambda t, z: (t, z + 1) if z + 1 < depth else None)
    below = permute(latents[:, 0], lambda t, z: (t, z - 1) if z else None)

    held, before = [None] * parts, [None] * parts
    order = [0, 3, 1, 2]
    for place in order:
        start = (part ^ partner(member, jnp.int32(place))) * width
        piece = lax.dynamic_slice_in_dim(latents, start, width, axis=3)
        held[place] = permute(piece, to_place(place)) if place else piece
    held[2], weights = lax.optimization_barrier((held[2], weights))
    for place in order:
        before[place] = permute(held[place], to_member(1))

    conv = functools.partial(
        conv_call,
        meta=meta,
        weights=weights,
        held=held,
        before=before,
        group=group,
        frames=frames,
    )

    def hop(pieces):
        return [permute(x, to_place(1)) for x in pieces]

    rims = split_call(meta, above, below, parts)
    rims = [permute(x, to_place(place)) if place else x for place, x in enumerate(rims)]
    inner_sent = conv([(3, False), (1, False)], rims=None, out_type=jnp.bfloat16)
    inner_got = hop(inner_sent)
    rims = stack_call(rims, inner_sent[0])
    rims = (rims, permute(rims, to_member(1)))
    rim_sent = conv(
        [(3, True), (1, True)], rims=rims, out_type=jnp.bfloat16, after=inner_got[:0]
    )
    rim_got = hop(rim_sent)
    inner_on, inner_own = conv(
        [(2, False), (0, False)], rims=None, out_type=jnp.float32, after=rim_sent[:1]
    )
    (inner_relay,) = sum_call([inner_on, inner_got[0]], 1)
    inner_last = permute(inner_relay, to_place(2))
    rim_on, rim_own = conv(
        [(2, True), (0, True)], rims=rims, out_type=jnp.float32, after=(inner_relay,)
    )
    (rim_relay,) = sum_call([rim_on, rim_got[0]], 1)
    rim_last = permute(rim_relay, to_place(2))
    sums = [
        sum_call([inner_own, inner_got[1], inner_last], frames, after=(rim_relay,)),
        sum_call([rim_own, rim_got[1], rim_last], frames),
    ]

    share = depth // frames

    def frame_home(t, z, p):
        frame = t % CORES * frames + (z + p) % frames
        slot = frame * share + z // frames
        return (t // CORES * CORES + slot % CORES, slot // CORES)

    def next_in_frame(t, z, step):
        slot = z * CORES + t % CORES
        slot = slot // share * share + (slot + step) % share
        return (t // CORES * CORES + slot % CORES, slot // CORES)

    own = []
    for p in range(frames):
        for chunk in sums:
            own.append(permute(chunk[p], lambda t, z: frame_home(t, z, p)))
    others = []
    for step in range(1, share):
        others += [permute(x, lambda t, z: next_in_frame(t, z, step)) for x in own]

    done = attend_call(
        own,
        others,
        (query_weight, key_weight, value_weight, out_weight),
        frames,
        rows_here,
        columns,
    )
    back = []
    for p in range(frames):
        pairs = [(b, a) for a, b in everywhere(sizes, lambda t, z: frame_home(t, z, p))]
        back.append(lax.ppermute(done[p], BOTH, pairs))
    return jnp.stack(
        [
            functools.reduce(
                lambda rest, p: jnp.where((z_index + p) % frames == f, back[p], rest),
                range(1, frames),
                back[0],
            )
            for f in range(frames)
        ]
    )


def solution(mesh):
    placed = (P("tm", "rows", None, None), P(None, "tm", None), P(), P(), P(), P())
    return jax.shard_map(
        body, mesh=mesh, in_specs=placed, out_specs=P("tm", "rows", None, None), check_vma=False
    )
```
